32 devices in a mesh: group: 2 (over x), adapter: 16 (over z, y, core).
Axes of the slice: x: 2, y: 2, z: 4, core: 2. Of those that a mesh axis runs over, the one named last changes fastest.
Arguments:
- hidden: bfloat16 [768, 8192], P(('group', 'adapter')), parts along dimension 0, may hold values from -6 to 6
- norm_weight: float32 [8192], replicated, may hold values from 0.5 to 1.5
- query_weight: bfloat16 [8192, 8192], P(None, 'adapter'), may hold values from -0.0625 to 0.0625
- down_weights: bfloat16 [16, 8192, 64], P('adapter'), may hold values from -0.0625 to 0.0625
- up_weights: bfloat16 [16, 64, 8192], P(None, None, 'adapter'), may hold values from -0.75 to 0.75
- adapter_index: int32 [768, 1], P(('group', 'adapter')), parts along dimension 0, may hold values from 0 to 15; in each aligned block of 384 rows (0 to 383, 384 to 767, ...) at most 96 rows name the same one
- adapter_slot: int32 [16], replicated, may hold values from 0 to 15, each once
Outputs:
- query: bfloat16 [768, 8192], P(('group', 'adapter')), parts along dimension 0
The draws below stay inside these ranges and needn't reach their ends.
There are 2 independent parts, one for each index of `group`. The reference program is written for one: setup_inputs(seed, part) draws one part's arguments, and reference() takes and returns one part's arrays. A program takes and returns all parts, laid end to end along the dimension named above; an argument that names none is the same for every part. Nothing has to cross between parts.
Inputs may be any that keep to these rules, and one draw needn't show every extreme that they name: `adapter_index`: no adapter is named by more than 96 token rows of a part, a bound that some block reaches. `adapter_slot`: each slot holds exactly one adapter.
All inputs are finite; a program needn't handle non-finite values.
Results may differ from the reference program's by a relative error of at most 0.0052.
Values may be sent and summed in bfloat16 or wider, within the bound.
No kernel may reach another device: no remote copies, remote signals or barrier semaphores. Data moves between devices by JAX's collectives and lax.ppermute only.
A program may use at most 128 MiB of HBM per device.

```python
import math
import jax
import jax.numpy as jnp
import numpy as np
from jax import lax

MODEL_WIDTH = 8192
ADAPTER_RANK = 64
TOKEN_ROWS = 384
ADAPTER_COUNT = 16
MOST = 96


def steps_of(stream_key, extent, pieces, low, high):
    level, own = 1.0, jax.random.fold_in(stream_key, 6)
    for position, blocks in pieces:
        draws = jnp.exp(jax.random.uniform(jax.random.fold_in(own, position), (blocks,), jnp.float32, low / len(pieces), high / len(pieces)))
        level = level * jnp.repeat(draws, extent[position] // blocks).reshape([-1 if axis == position else 1 for axis in range(len(extent))])
    return level


def deal_out(key, own, number, rows, amount, top, bound, skew):
    ranking = jax.random.permutation(key, amount)
    heavy_load, common = shares(amount, rows * top, bound, skew, True), shares(amount, rows * top, bound, skew, False)
    places = jnp.arange(amount)

    def named(lengths, rotation):
        used = int((lengths > 0).sum())
        fixed = max(1, used // 4)
        shifted = fixed + (places - fixed + rotation * (used - fixed)) % max(1, amount - fixed)
        return jnp.zeros((amount,), jnp.int32).at[ranking[jnp.where(places < fixed, places, shifted)]].set(jnp.asarray(lengths, jnp.int32))

    lengths = jnp.where(number % 4 == 0, named(heavy_load, number // 4), named(common, number - number // 4 - 1))
    mixed = jax.random.permutation(jax.random.fold_in(own, 3), amount)
    donor, receiver = mixed[0:amount // 2 * 2:2], mixed[1:amount // 2 * 2:2]
    slack = jnp.minimum(lengths[donor] - 1, bound - lengths[receiver]) // 2
    slack = jnp.where((donor == ranking[0]) | (receiver == ranking[0]) | (lengths[receiver] == 0), 0, jnp.maximum(slack, 0))
    shifted = jax.random.randint(jax.random.fold_in(own, 4), (amount // 2,), 0, 1 << 20) % (slack + 1)
    lengths = lengths.at[donor].add(-shifted).at[receiver].add(shifted)
    members = jnp.searchsorted(jnp.cumsum(lengths), jnp.arange(rows * top), side="right").astype(jnp.int32)
    listing = members.reshape(top, rows).T
    listing = listing[jax.random.permutation(jax.random.fold_in(own, 1), rows)]
    rotation = jax.random.randint(jax.random.fold_in(own, 2), (rows, 1), 0, top)
    return jnp.take_along_axis(listing, (jnp.arange(top)[None, :] + rotation) % top, axis=1)


def shares(amount, total, bound, skew, full):
    weights = [(1 << 20) // math.isqrt(standing ** skew) + 1 for standing in range(1, amount + 1)]
    largest = bound if full else min(bound, max(-(-total // amount), total * weights[0] // sum(weights)))
    least = 1 if total - largest >= amount - 1 else 0
    holding, surplus = [largest] + [least] * (amount - 1), total - largest - least * (amount - 1)
    while surplus > 0:
        candidates = [i for i in range(1, amount) if holding[i] < largest] or [i for i in range(1, amount) if holding[i] < bound]
        pool, budget = sum([weights[i] for i in candidates]), surplus
        for i in candidates:
            more = min(bound - holding[i], max(1, budget * weights[i] // pool), surplus)
            holding[i] = holding[i] + more
            surplus = surplus - more
    return np.array(holding)


def normal_values(rng, extent, deviation, bound, split=(), held_as=jnp.bfloat16):
    level = steps_of(rng, extent, split, -0.22, 0.18) if split else 1.0
    result = jax.random.normal(rng, extent, jnp.float32) * deviation * level
    return jnp.minimum(jnp.maximum(result, -bound), bound).astype(held_as)


def setup_inputs(seed: int = 0, part: int = 0) -> dict:
    streams_of = jax.random.split(jax.random.key(seed), 8)
    part_splits = jax.random.split(jax.random.fold_in(streams_of[7], part), 8)
    hidden = normal_values(part_splits[0], (TOKEN_ROWS, MODEL_WIDTH), 1.0, 6.0, ((0, 16),))
    norm_weight = jnp.clip(1.0 + 0.1 * jax.random.normal(streams_of[1], (MODEL_WIDTH,), jnp.float32), 0.5, 1.5)
    query_weight = normal_values(streams_of[2], (MODEL_WIDTH, MODEL_WIDTH), MODEL_WIDTH ** -0.5, 0.0625, ((1, 16),))
    down_weights = normal_values(streams_of[3], (ADAPTER_COUNT, MODEL_WIDTH, ADAPTER_RANK), MODEL_WIDTH ** -0.5, 0.0625, ((0, 16),))
    up_weights = normal_values(streams_of[4], (ADAPTER_COUNT, ADAPTER_RANK, MODEL_WIDTH), ADAPTER_RANK ** -0.5, 0.75, ((2, 16),))
    adapter_index_keys = jax.random.split(jax.random.fold_in(part_splits[5], 1), TOKEN_ROWS // TOKEN_ROWS)
    adapter_index_turns = jax.random.permutation(jax.random.fold_in(part_splits[5], 3), TOKEN_ROWS // TOKEN_ROWS)
    adapter_index = jax.vmap(lambda own, number: deal_out(jax.random.fold_in(part_splits[5], 2), own, number, TOKEN_ROWS, ADAPTER_COUNT, 1, MOST, 2))(adapter_index_keys, adapter_index_turns).reshape((TOKEN_ROWS, 1))
    adapter_slot = jax.random.permutation(streams_of[6], ADAPTER_COUNT).astype(jnp.int32)
    return {"hidden": hidden, "norm_weight": norm_weight, "query_weight": query_weight, "down_weights": down_weights, "up_weights": up_weights, "adapter_index": adapter_index, "adapter_slot": adapter_slot}


ADAPTER_SCALE = 0.5
EPS = 1e-05

def reference(hidden, norm_weight, query_weight, down_weights, up_weights, adapter_index, adapter_slot):
    wide32 = hidden.astype(jnp.float32)
    inv_rms = lax.rsqrt(lax.optimization_barrier(jnp.mean(wide32 * wide32, axis=1, keepdims=True)) + EPS)
    normalized_input = (wide32 * inv_rms * norm_weight).astype(jnp.bfloat16)
    slot_tok = adapter_slot[adapter_index[:, 0]].astype(jnp.int32)

    def shrink_one(selected_index, total):
        partial_output = jnp.dot(normalized_input, down_weights[selected_index], preferred_element_type=jnp.float32)
        return total + jnp.where((slot_tok == selected_index)[:, None], partial_output, jnp.float32(0.0))
    down_project = lax.fori_loop(0, ADAPTER_COUNT, shrink_one, jnp.zeros((TOKEN_ROWS, ADAPTER_RANK), jnp.float32)).astype(jnp.bfloat16)

    def expand_single(selected_index, total):
        partial_output = jnp.dot(down_project, up_weights[selected_index], preferred_element_type=jnp.float32)
        return total + jnp.where((slot_tok == selected_index)[:, None], partial_output, jnp.float32(0.0))
    adapter_update = lax.fori_loop(0, ADAPTER_COUNT, expand_single, jnp.zeros((TOKEN_ROWS, MODEL_WIDTH), jnp.float32))
    base_columns = jnp.dot(normalized_input, query_weight, preferred_element_type=jnp.float32)
    return (base_columns + ADAPTER_SCALE * adapter_update).astype(jnp.bfloat16)
```

```python
import jax
import jax.numpy as jnp
from jax import lax
from jax.sharding import PartitionSpec as P

ADAPTER_SCALE = 0.5
EPS = 1e-05

SIDE = 2
CORES = 2


def line_ring(places):
    odd = list(range(1, places, 2))
    even = list(range(0, places, 2))
    return [0] + odd + even[:0:-1]


def pairs(places, move):
    steps, flip_y, flip_core = move
    ring = line_ring(places)
    out = []
    for at, place in enumerate(ring):
        target = ring[(at + steps) % places]
        for y in range(SIDE):
            for core in range(CORES):
                source = (place * SIDE + y) * CORES + core
                out.append((source, (target * SIDE + (y ^ flip_y)) * CORES + (core ^ flip_core)))
    return out


def shards(
    hidden, norm_weight, query_weight, down_weights, up_weights, adapter_index, adapter_slot
):
    devices = lax.axis_size("adapter")
    me = lax.axis_index("adapter")
    places = devices // (SIDE * CORES)
    own_rows, width = hidden.shape
    columns = query_weight.shape[1]
    rank = down_weights.shape[2]
    ring = line_ring(places)

    wide32 = hidden.astype(jnp.float32)
    inv_rms = lax.rsqrt(jnp.mean(wide32 * wide32, axis=1, keepdims=True) + EPS)
    normed = (wide32 * inv_rms * norm_weight).astype(jnp.bfloat16)

    slots = jnp.arange(devices, dtype=jnp.int32)
    hits = (adapter_index[:, 0][:, None] == slots[None, :]).astype(jnp.int32)
    slot_own = jnp.sum(hits * adapter_slot[None, :], axis=1)
    slot_all = lax.all_gather(slot_own, "adapter", axis=0, tiled=True)

    def move(x, *how):
        return lax.ppermute(x, "adapter", pairs(places, how))

    place_of = jnp.asarray(ring, jnp.int32)
    turn_of = jnp.asarray([ring.index(p) for p in range(places)], jnp.int32)
    turn = turn_of[me // (SIDE * CORES)]
    corner = me % (SIDE * CORES)

    chain = normed
    slot_blocks = slot_all.reshape(devices, own_rows)
    bases, shrinks, origins = [], [], []
    for step in range(places):
        if step:
            chain = move(chain, 1, 0, 0)
        other_y = move(chain, 0, 1, 0)
        other_core = move(chain, 0, 0, 1)
        both = move(other_y, 0, 0, 1)
        rows = jnp.concatenate([chain, other_core, other_y, both], axis=0)
        place = place_of[(turn - step + places) % places]
        origin = place * (SIDE * CORES) + (corner ^ jnp.arange(SIDE * CORES, dtype=jnp.int32))
        slot_here = slot_blocks[origin].reshape(-1)
        part = jnp.dot(rows, down_weights[0], preferred_element_type=jnp.float32)
        shrinks.append(jnp.where((slot_here == me)[:, None], part, 0.0).astype(jnp.bfloat16))
        bases.append(jnp.dot(rows, query_weight, preferred_element_type=jnp.float32))
        origins.append(origin)
    origin_all = jnp.concatenate(origins)
    base = jnp.concatenate(bases, axis=0)
    base = jnp.zeros((devices, own_rows, columns), jnp.float32).at[origin_all].set(
        base.reshape(devices, own_rows, columns)
    )
    shrink = jnp.concatenate(shrinks, axis=0).reshape(devices, own_rows, rank)
    shrink = jnp.zeros((devices, own_rows, rank), jnp.bfloat16).at[origin_all].set(shrink)
    shrink_all = lax.all_gather(shrink.reshape(devices * own_rows, rank), "adapter", axis=0)
    shrink_all = jnp.sum(shrink_all, axis=0, dtype=jnp.float32).astype(jnp.bfloat16)
    slot_hits = slot_all[:, None] == slots[None, :]
    spread = jnp.where(
        slot_hits[:, :, None], shrink_all[:, None, :], jnp.zeros((), jnp.bfloat16)
    ).reshape(devices * own_rows, devices * rank)
    update = jnp.dot(
        spread,
        up_weights.reshape(devices * rank, columns),
        preferred_element_type=jnp.float32,
    )
    query = (base.reshape(devices * own_rows, columns) + ADAPTER_SCALE * update).astype(jnp.bfloat16)
    return lax.all_to_all(query, "adapter", split_axis=0, concat_axis=1, tiled=True)


def solution(mesh):
    in_specs = (
        P(("group", "adapter"), None),
        P(),
        P(None, "adapter"),
        P("adapter", None, None),
        P(None, None, "adapter"),
        P(("group", "adapter"), None),
        P(),
    )
    out_specs = P(("group", "adapter"), None)
    return jax.shard_map(shards, mesh=mesh, in_specs=in_specs, out_specs=out_specs, check_vma=False)
```

```python
import jax
import jax.numpy as jnp
from jax import lax
from jax.experimental import pallas as pl
from jax.experimental.pallas import tpu as pltpu
from jax.sharding import PartitionSpec as P

ADAPTER_SCALE = 0.5
EPS = 1e-05

SIDE = 2
CORES = 2
CORNERS = SIDE * CORES
LANES = 128
CHUNK = 1024


def line_ring(places):
    odd = list(range(1, places, 2))
    even = list(range(0, places, 2))
    return [0] + odd + even[:0:-1]


def pairs(places, steps, flip):
    ring = line_ring(places)
    out = []
    for at, place in enumerate(ring):
        target = ring[(at + steps) % places]
        for corner in range(CORNERS):
            out.append((place * CORNERS + corner, target * CORNERS + (corner ^ flip)))
    return out


def ring_device(places, steps, flip):
    me = lax.axis_index("adapter")
    ring = line_ring(places)
    place, corner = me // CORNERS, me % CORNERS
    target = jnp.int32(0)
    for at, name in enumerate(ring):
        target = jnp.where(place == name, jnp.int32(ring[(at + steps) % places]), target)
    return target * CORNERS + (corner ^ flip)


def norm_kernel(hidden_ref, gain_ref, index_ref, slot_ref, keep_ref, give_ref, slots_ref):
    rows, width = hidden_ref.shape
    half = width // CORES
    core = lax.axis_index("adapter") % CORES
    squares = jnp.zeros((rows, LANES), jnp.float32)
    for start in range(0, width, CHUNK):
        wide = hidden_ref[:, start : start + CHUNK].astype(jnp.float32)
        wide = wide * wide
        for lane in range(0, CHUNK, LANES):
            squares = squares + wide[:, lane : lane + LANES]
    inv_rms = lax.rsqrt(jnp.sum(squares, axis=1, keepdims=True) / width + EPS)
    for which, out_ref in ((core, keep_ref), (1 - core, give_ref)):
        for start in range(0, half, CHUNK):
            at = pl.multiple_of(which * half + start, CHUNK)
            wide = hidden_ref[:, pl.ds(at, CHUNK)].astype(jnp.float32)
            gain = gain_ref[:, pl.ds(at, CHUNK)]
            out_ref[:, start : start + CHUNK] = (wide * inv_rms * gain).astype(jnp.bfloat16)
    index = index_ref[...]
    slot = jnp.zeros(index.shape, jnp.float32)
    for name in range(slot_ref.shape[0]):
        slot = jnp.where(index == name, slot_ref[name].astype(jnp.float32), slot)
    slots_ref[...] = jnp.zeros(slots_ref.shape, jnp.float32)
    slots_ref[0:1, 0:rows] = slot


def normalize(hidden, norm_weight, adapter_index, adapter_slot):
    rows, width = hidden.shape
    vmem = pl.BlockSpec(memory_space=pltpu.VMEM)
    return pl.pallas_call(
        norm_kernel,
        out_shape=(
            jax.ShapeDtypeStruct((rows, width // CORES), jnp.bfloat16),
            jax.ShapeDtypeStruct((rows, width // CORES), jnp.bfloat16),
            jax.ShapeDtypeStruct((8, LANES), jnp.float32),
        ),
        in_specs=[vmem, vmem, vmem, pl.BlockSpec(memory_space=pltpu.SMEM)],
        out_specs=(vmem, vmem, vmem),
    )(hidden, norm_weight.reshape(1, width), adapter_index.reshape(1, rows), adapter_slot)


def order_kernel(places, rows, slots_ref, out_ref):
    across = lax.broadcasted_iota(jnp.int32, (rows, LANES), 1)
    down = lax.broadcasted_iota(jnp.int32, (rows, LANES), 0)
    for step in range(places):
        for corner in range(CORNERS):
            origin = ring_device(places, -step, corner)
            row = slots_ref[origin, 0:1, :]
            column = jnp.sum(jnp.where(across == down, row, 0.0), axis=1, keepdims=True)
            out_ref[step, corner] = jnp.broadcast_to(column, (rows, LANES))


def order_slots(slots, places, rows):
    vmem = pl.BlockSpec(memory_space=pltpu.VMEM)
    return pl.pallas_call(
        lambda slots_ref, out_ref: order_kernel(places, rows, slots_ref, out_ref),
        out_shape=jax.ShapeDtypeStruct((places, CORNERS, rows, LANES), jnp.float32),
        in_specs=[vmem],
        out_specs=vmem,
    )(slots)


def assemble_kernel(places, columns, *refs):
    parts, out_ref, sems = refs[:-2], refs[-2], refs[-1]
    copies = []
    for step in range(places):
        for corner in range(CORNERS):
            which = step * CORNERS + corner
            at = pl.multiple_of(ring_device(places, step, corner) * columns, columns)
            copies.append(
                pltpu.make_async_copy(parts[which], out_ref.at[:, pl.ds(at, columns)], sems.at[which])
            )
    for copy in copies:
        copy.start()
    for copy in copies:
        copy.wait()


def assemble(parts, places):
    rows, columns = parts[0].shape
    anywhere = pl.BlockSpec(memory_space=pl.ANY)
    return pl.pallas_call(
        lambda *refs: assemble_kernel(places, columns, *refs),
        out_shape=jax.ShapeDtypeStruct((rows, columns * len(parts)), jnp.bfloat16),
        in_specs=[anywhere] * len(parts),
        out_specs=anywhere,
        scratch_shapes=[pltpu.SemaphoreType.DMA((len(parts),))],
    )(*parts)


def shards(
    hidden, norm_weight, query_weight, down_weights, up_weights, adapter_index, adapter_slot
):
    devices = lax.axis_size("adapter")
    me = lax.axis_index("adapter")
    core = me % CORES
    places = devices // CORNERS
    own_rows, width = hidden.shape
    half = width // CORES
    columns = query_weight.shape[1]
    rank = down_weights.shape[2]
    step_rows = CORNERS * own_rows

    def move(x, steps, flip):
        return lax.ppermute(x, "adapter", pairs(places, steps, flip))

    def matmul(x, y):
        return jnp.dot(x, y, preferred_element_type=jnp.float32)

    keep, give, slots_own = normalize(hidden, norm_weight, adapter_index, adapter_slot)
    slots_all = lax.all_gather(slots_own, "adapter", axis=0)

    first = [keep]
    second = [move(give, 0, 1)]
    first_y = [move(keep, 0, 2)]
    second_y = [move(second[0], 0, 2)]
    for step in range(1, places):
        first.append(move(first[-1], 1, 0))
        second.append(move(second[-1], 1, 0))
        first_y.append(move(first[-1], 0, 2))
        if step < places - 1:
            second_y.append(move(second[-1], 0, 2))
        else:
            second_y.append(move(second_y[-1], 1, 0))

    w_keep = lax.dynamic_slice_in_dim(query_weight, core * half, half, 0)
    w_got = move(lax.dynamic_slice_in_dim(query_weight, (1 - core) * half, half, 0), 0, 1)
    down = down_weights[0]
    d_keep = lax.dynamic_slice_in_dim(down, core * half, half, 0)
    d_got = move(lax.dynamic_slice_in_dim(down, (1 - core) * half, half, 0), 0, 1)
    d_both = jnp.concatenate([d_keep, d_got], axis=1)

    slots = order_slots(slots_all, places, own_rows).reshape(places, step_rows, LANES)
    holder = jnp.where(jnp.arange(2 * rank) < rank, me, me ^ 1).astype(jnp.float32)

    bases, travelling = [], None
    for step in range(places):
        a, b, c, d = first[step], second[step], first_y[step], second_y[step]
        mine = jnp.concatenate([a, b, c, d], axis=0)
        theirs = jnp.concatenate([b, a, d, c], axis=0)
        part = matmul(mine, d_both)
        part = jnp.where(slots[step][:, :1] == holder[None, :], part, 0.0)
        part = part[:, :rank] + part[:, rank:]
        travelling = part if travelling is None else part + move(travelling, 1, 0)
        bases.append(matmul(mine, w_keep) + move(matmul(theirs, w_got), 0, 1))

    def flipped(x, flip):
        blocks = x.reshape(CORNERS, own_rows, rank)
        return jnp.stack([blocks[k ^ flip] for k in range(CORNERS)]).reshape(step_rows, rank)

    shrink = (travelling + flipped(move(travelling, 0, 1), 1)).astype(jnp.bfloat16)
    shrink = shrink + flipped(move(shrink, 0, 2), 2)

    up = up_weights.reshape(devices * rank, columns)
    names = jnp.arange(devices, dtype=jnp.float32)
    parts = []
    for step in range(places):
        mine = shrink if step == places - 1 else move(shrink, step + 1, 0)
        hits = slots[step][:, :1] == names[None, :]
        spread = jnp.where(hits[:, :, None], mine[:, None, :], jnp.zeros((), jnp.bfloat16))
        update = matmul(spread.reshape(step_rows, devices * rank), up)
        query = (bases[step] + ADAPTER_SCALE * update).astype(jnp.bfloat16)
        for corner in range(CORNERS):
            piece = query[corner * own_rows : (corner + 1) * own_rows]
            parts.append(move(piece, -step, corner) if step or corner else piece)
    return assemble(parts, places)


def solution(mesh):
    in_specs = (
        P(("group", "adapter"), None),
        P(),
        P(None, "adapter"),
        P("adapter", None, None),
        P(None, None, "adapter"),
        P(("group", "adapter"), None),
        P(),
    )
    out_specs = P(("group", "adapter"), None)
    return jax.shard_map(shards, mesh=mesh, in_specs=in_specs, out_specs=out_specs, check_vma=False)
```

```python
import jax
import jax.numpy as jnp
from jax import lax
from jax.experimental import pallas as pl
from jax.experimental.pallas import tpu as pltpu
from jax.sharding import PartitionSpec as P

ADAPTER_SCALE = 0.5
EPS = 1e-05

SIDE = 2
CORES = 2
CORNERS = SIDE * CORES
LANES = 128
CHUNK = 1024


def round_trip(devices):
    places = devices // CORNERS
    up = [place * CORNERS + core for place in range(places) for core in range(CORES)]
    back = [
        place * CORNERS + CORES + core for place in reversed(range(places)) for core in range(CORES)
    ]
    return up + back


def norm_kernel(hidden_ref, gain_ref, low_ref, high_ref):
    rows, width = hidden_ref.shape
    half = width // 2
    squares = jnp.zeros((rows, LANES), jnp.float32)
    for start in range(0, width, CHUNK):
        wide = hidden_ref[:, start : start + CHUNK].astype(jnp.float32)
        wide = wide * wide
        for lane in range(0, CHUNK, LANES):
            squares = squares + wide[:, lane : lane + LANES]
    inv_rms = lax.rsqrt(jnp.sum(squares, axis=1, keepdims=True) / width + EPS)
    for first, out_ref in ((0, low_ref), (half, high_ref)):
        for start in range(0, half, CHUNK):
            at = first + start
            wide = hidden_ref[:, at : at + CHUNK].astype(jnp.float32)
            gain = gain_ref[:, at : at + CHUNK]
            out_ref[:, start : start + CHUNK] = (wide * inv_rms * gain).astype(jnp.bfloat16)


def normalize(hidden, norm_weight):
    rows, width = hidden.shape
    vmem = pl.BlockSpec(memory_space=pltpu.VMEM)
    half = jax.ShapeDtypeStruct((rows, width // 2), jnp.bfloat16)
    return pl.pallas_call(
        norm_kernel, out_shape=(half, half), in_specs=[vmem, vmem], out_specs=(vmem, vmem)
    )(hidden, norm_weight.reshape(1, width))


def shards(
    hidden, norm_weight, query_weight, down_weights, up_weights, adapter_index, adapter_slot
):
    devices = lax.axis_size("adapter")
    me = lax.axis_index("adapter")
    places = devices // CORNERS
    own_rows, width = hidden.shape
    half = width // 2
    columns = query_weight.shape[1]
    rank = down_weights.shape[2]
    rows = devices * own_rows
    order = round_trip(devices)

    def matmul(x, y):
        return jnp.dot(x, y, preferred_element_type=jnp.float32)

    def flip(x, how):
        return lax.ppermute(x, "adapter", [(i, i ^ how) for i in range(devices)])

    def along(x, steps):
        step = steps * CORNERS
        return lax.ppermute(x, "adapter", [(i, (i + step) % devices) for i in range(devices)])

    low, high = normalize(hidden, norm_weight)
    low = lax.all_gather(low, "adapter", axis_index_groups=[order])
    high = lax.all_gather(high, "adapter", axis_index_groups=[order[::-1]])
    ids = lax.all_gather(adapter_index, "adapter")
    ids = ids[:, :, 0][jnp.asarray(order)].reshape(rows)

    names = jnp.arange(devices, dtype=jnp.int32)
    hits = (ids[:, None] == names[None, :]).astype(jnp.int32)
    slot_tok = jnp.sum(hits * adapter_slot[None, :], axis=1)
    slot_hits = slot_tok[:, None] == names[None, :]

    def project(weight):
        one = matmul(low.reshape(rows, half), weight[:half])
        other = matmul(high.reshape(rows, half), weight[half:])
        return one + other.reshape(devices, own_rows, -1)[::-1].reshape(rows, -1)

    shrink = project(down_weights[0])
    shrink = jnp.where((slot_tok == me)[:, None], shrink, 0.0).astype(jnp.bfloat16)
    shrink = shrink + flip(shrink, 1)
    shrink = shrink + flip(shrink, 2)
    parts = [along(shrink, steps) for steps in range(1, places)]
    for part in parts:
        shrink = shrink + part
    base = project(query_weight)
    spread = jnp.where(slot_hits[:, :, None], shrink[:, None, :], jnp.zeros((), jnp.bfloat16))
    update = matmul(spread.reshape(rows, devices * rank), up_weights.reshape(devices * rank, columns))
    query = (base + ADAPTER_SCALE * update).astype(jnp.bfloat16)
    query = query.reshape(devices, own_rows, columns)
    back = [order.index(i) for i in range(devices)]
    query = jnp.concatenate([query[i] for i in back], axis=0)
    return lax.all_to_all(query, "adapter", split_axis=0, concat_axis=1, tiled=True)


def solution(mesh):
    in_specs = (
        P(("group", "adapter"), None),
        P(),
        P(None, "adapter"),
        P("adapter", None, None),
        P(None, None, "adapter"),
        P(("group", "adapter"), None),
        P(),
    )
    out_specs = P(("group", "adapter"), None)
    return jax.shard_map(shards, mesh=mesh, in_specs=in_specs, out_specs=out_specs, check_vma=False)
```

```python
import jax
import jax.numpy as jnp
from jax import lax
from jax.experimental import pallas as pl
from jax.experimental.pallas import tpu as pltpu
from jax.sharding import PartitionSpec as P

ADAPTER_SCALE = 0.5
EPS = 1e-05

SIDE = 2
CORES = 2
CORNERS = SIDE * CORES
LANES = 128
CHUNK = 1024
SMALL = 16 << 20


def line_ring(places):
    odd = list(range(1, places, 2))
    even = list(range(0, places, 2))
    return [0] + odd + even[:0:-1]


def pairs(places, steps, flip):
    ring = line_ring(places)
    out = []
    for at, place in enumerate(ring):
        target = ring[(at + steps) % places]
        for corner in range(CORNERS):
            out.append((place * CORNERS + corner, target * CORNERS + (corner ^ flip)))
    return out


def ring_device(places, steps, flip):
    me = lax.axis_index("adapter")
    ring = line_ring(places)
    place, corner = me // CORNERS, me % CORNERS
    target = jnp.int32(0)
    for at, name in enumerate(ring):
        target = jnp.where(place == name, jnp.int32(ring[(at + steps) % places]), target)
    return target * CORNERS + (corner ^ flip)


def slots_kernel(index_ref, slot_ref, out_ref):
    index = index_ref[...]
    slot = jnp.zeros(index.shape, jnp.float32)
    for name in range(slot_ref.shape[0]):
        slot = jnp.where(index == name, slot_ref[name].astype(jnp.float32), slot)
    out_ref[...] = jnp.zeros(out_ref.shape, jnp.float32)
    out_ref[0:1, 0 : index.shape[1]] = slot


def own_slots(adapter_index, adapter_slot):
    rows = adapter_index.shape[0]
    vmem = pl.BlockSpec(memory_space=pltpu.VMEM)
    return pl.pallas_call(
        slots_kernel,
        out_shape=jax.ShapeDtypeStruct((8, LANES), jnp.float32),
        in_specs=[vmem, pl.BlockSpec(memory_space=pltpu.SMEM)],
        out_specs=vmem,
        compiler_params=pltpu.CompilerParams(vmem_limit_bytes=SMALL),
    )(adapter_index.reshape(1, rows), adapter_slot)


def slot_column(slots_ref, own_rows):
    across = lax.broadcasted_iota(jnp.int32, (own_rows, LANES), 1)
    down = lax.broadcasted_iota(jnp.int32, (own_rows, LANES), 0)
    columns = []
    for corner in range(CORNERS):
        row = slots_ref[corner : corner + 1, :]
        columns.append(jnp.sum(jnp.where(across == down, row, 0.0), axis=1, keepdims=True))
    return jnp.concatenate(columns, axis=0).astype(jnp.int32)


def prepare_kernel(*refs):
    blocks, refs = refs[:CORNERS], refs[CORNERS:]
    gain_ref, own_ref, other_ref, slots_ref, *before, rows_ref, part_ref = refs
    own_rows, width = blocks[0].shape
    rank = own_ref.shape[0]
    inverse = []
    for block in blocks:
        squares = jnp.zeros((own_rows, LANES), jnp.float32)
        for start in range(0, width, CHUNK):
            wide = block[:, start : start + CHUNK].astype(jnp.float32)
            wide = wide * wide
            for lane in range(0, CHUNK, LANES):
                squares = squares + wide[:, lane : lane + LANES]
        inverse.append(lax.rsqrt(jnp.sum(squares, axis=1, keepdims=True) / width + EPS))
    part = jnp.zeros((own_rows * CORNERS, 2 * rank), jnp.float32)
    for start in range(0, width, CHUNK):
        lanes = slice(start, start + CHUNK)
        gain = gain_ref[:, lanes]
        wide = [block[:, lanes].astype(jnp.float32) * inv * gain for block, inv in zip(blocks, inverse)]
        rows = jnp.concatenate(wide, axis=0).astype(jnp.bfloat16)
        rows_ref[:, lanes] = rows
        down = jnp.concatenate([own_ref[:, lanes], other_ref[:, lanes]], axis=0)
        part += lax.dot_general(
            rows, down, (((1,), (1,)), ((), ())), preferred_element_type=jnp.float32
        )
    slot = slot_column(slots_ref, own_rows)
    me = lax.axis_index("adapter")
    lanes = lax.broadcasted_iota(jnp.int32, part.shape, 1)
    holder = jnp.where(lanes < rank, me, me ^ 1)
    part = jnp.where(slot == holder, part, 0.0)
    part = part[:, :rank] + part[:, rank:]
    for ref in before:
        part = part + ref[...].astype(jnp.float32)
    part_ref[...] = part.astype(jnp.bfloat16)


def prepare(blocks, gain, own, other, slots, before):
    own_rows, width = blocks[0].shape
    rank = own.shape[0]
    rows = own_rows * CORNERS
    before = [] if before is None else [before]
    vmem = pl.BlockSpec(memory_space=pltpu.VMEM)
    return pl.pallas_call(
        prepare_kernel,
        out_shape=(
            jax.ShapeDtypeStruct((rows, width), jnp.bfloat16),
            jax.ShapeDtypeStruct((rows, rank), jnp.bfloat16),
        ),
        in_specs=[vmem] * (CORNERS + 4 + len(before)),
        out_specs=(vmem, vmem),
        compiler_params=pltpu.CompilerParams(vmem_limit_bytes=SMALL),
        cost_estimate=pl.CostEstimate(
            flops=2 * rows * width * 256, bytes_accessed=rows * width * 4, transcendentals=rows
        ),
    )(*blocks, gain, own, other, slots, *before)


def finish_kernel(places, devices, *refs):
    bases, shrinks, slots = refs[:places], refs[places : 2 * places], refs[2 * places : 3 * places]
    up_ref, out_ref = refs[3 * places :]
    rows, rank = shrinks[0].shape
    own_rows = rows // CORNERS
    lanes = lax.broadcasted_iota(jnp.int32, (rows, devices * rank), 1)
    for step in range(places):
        shrink = shrinks[step][...].astype(jnp.float32)
        wide = jnp.concatenate([shrink] * devices, axis=1)
        slot = slot_column(slots[step], own_rows)
        spread = jnp.where(lanes // rank == slot, wide, 0.0).astype(jnp.bfloat16)
        update = jnp.dot(spread, up_ref[...], preferred_element_type=jnp.float32)
        query = (bases[step][...] + ADAPTER_SCALE * update).astype(jnp.bfloat16)
        for corner in range(CORNERS):
            owner = ring_device(places, -step, corner)
            out_ref[owner] = query[corner * own_rows : (corner + 1) * own_rows]


def finish(bases, shrinks, slots, up):
    places, devices = len(bases), up.shape[0]
    rows, columns = bases[0].shape
    rank = up.shape[1]
    vmem = pl.BlockSpec(memory_space=pltpu.VMEM)
    return pl.pallas_call(
        lambda *refs: finish_kernel(places, devices, *refs),
        out_shape=jax.ShapeDtypeStruct((devices, rows // CORNERS, columns), jnp.bfloat16),
        in_specs=[vmem] * (3 * places + 1),
        out_specs=vmem,
        compiler_params=pltpu.CompilerParams(vmem_limit_bytes=SMALL),
    )(*bases, *shrinks, *slots, up.reshape(devices * rank, columns))


def shards(
    hidden, norm_weight, query_weight, down_weights, up_weights, adapter_index, adapter_slot
):
    devices = lax.axis_size("adapter")
    me = lax.axis_index("adapter")
    places = devices // CORNERS
    own_rows, width = hidden.shape
    rank = down_weights.shape[2]

    def move(x, steps, flip):
        return lax.ppermute(x, "adapter", pairs(places, steps, flip))

    def matmul(x, y):
        return jnp.dot(x, y, preferred_element_type=jnp.float32)

    slots = own_slots(adapter_index, adapter_slot)
    empty = jnp.zeros((8 - CORNERS, LANES), jnp.float32)
    pair = jnp.concatenate([slots[:1], move(slots, 0, 1)[:1], slots[2:]], axis=0)
    four = jnp.concatenate([pair[:2], move(pair, 0, 2)[:2], empty], axis=0)
    slots = [four] + [move(four, step, 0) for step in range(1, places)]

    chain = hidden
    gain = norm_weight.reshape(1, width)
    down = down_weights[0].T
    down_other = move(down, 0, 1)

    bases, travelling = [], None
    for step in range(places):
        if step:
            chain = move(chain, 1, 0)
        other_y = move(chain, 0, 2)
        blocks = [chain, move(chain, 0, 1), other_y, move(other_y, 0, 1)]
        before = None if travelling is None else move(travelling, 1, 0)
        rows, travelling = prepare(blocks, gain, down, down_other, slots[step], before)
        bases.append(matmul(rows, query_weight))

    blocks = move(travelling, 0, 2).reshape(CORNERS, own_rows, rank)
    blocks = jnp.concatenate([blocks[corner ^ 2] for corner in range(CORNERS)], axis=0)
    shrink = travelling + blocks
    shrinks = [move(shrink, step + 1, 0) for step in range(places - 1)] + [shrink]
    query = finish(bases, shrinks, slots, up_weights)
    query = query.reshape(devices * own_rows, query.shape[2])
    return lax.all_to_all(query, "adapter", split_axis=0, concat_axis=1, tiled=True)


def solution(mesh):
    in_specs = (
        P(("group", "adapter"), None),
        P(),
        P(None, "adapter"),
        P("adapter", None, None),
        P(None, None, "adapter"),
        P(("group", "adapter"), None),
        P(),
    )
    out_specs = P(("group", "adapter"), None)
    return jax.shard_map(shards, mesh=mesh, in_specs=in_specs, out_specs=out_specs, check_vma=False)
```

```python
import jax
import jax.numpy as jnp
from jax import lax
from jax.experimental import pallas as pl
from jax.experimental.pallas import tpu as pltpu
from jax.sharding import PartitionSpec as P

ADAPTER_SCALE = 0.5
EPS = 1e-05

SIDE = 2
CORES = 2
CORNERS = SIDE * CORES
LANES = 128
CHUNK = 1024
SMALL = 16 << 20


def line_ring(places):
    odd = list(range(1, places, 2))
    even = list(range(0, places, 2))
    return [0] + odd + even[:0:-1]


def pairs(places, steps, flip):
    ring = line_ring(places)
    out = []
    for at, place in enumerate(ring):
        target = ring[(at + steps) % places]
        for corner in range(CORNERS):
            out.append((place * CORNERS + corner, target * CORNERS + (corner ^ flip)))
    return out


def split_pairs(places):
    flips, steps = pairs(places, 0, 2), pairs(places, 1, 0)
    return [pair for pair in flips if pair[0] % CORES == 0] + [
        pair for pair in steps if pair[0] % CORES
    ]


def ring_device(places, steps, flip):
    me = lax.axis_index("adapter")
    ring = line_ring(places)
    place, corner = me // CORNERS, me % CORNERS
    target = jnp.int32(0)
    for at, name in enumerate(ring):
        target = jnp.where(place == name, jnp.int32(ring[(at + steps) % places]), target)
    return target * CORNERS + (corner ^ flip)


def slot_column(blocks, width):
    return jnp.concatenate(
        [block[:, width : width + 1].astype(jnp.float32) for block in blocks], axis=0
    ).astype(jnp.int32)


def norm_kernel(hidden_ref, gain_ref, index_ref, slot_ref, out_ref):
    rows, width = hidden_ref.shape
    squares = jnp.zeros((rows, LANES), jnp.float32)
    for start in range(0, width, CHUNK):
        wide = hidden_ref[:, start : start + CHUNK].astype(jnp.float32)
        wide = wide * wide
        for lane in range(0, CHUNK, LANES):
            squares = squares + wide[:, lane : lane + LANES]
    inv_rms = lax.rsqrt(jnp.sum(squares, axis=1, keepdims=True) / width + EPS)
    for start in range(0, width, CHUNK):
        lanes = slice(start, start + CHUNK)
        wide = hidden_ref[:, lanes].astype(jnp.float32)
        out_ref[:, lanes] = (wide * inv_rms * gain_ref[:, lanes]).astype(jnp.bfloat16)
    index = index_ref[...]
    slot = jnp.zeros(index.shape, jnp.float32)
    for name in range(slot_ref.shape[0]):
        slot = jnp.where(index == name, slot_ref[name].astype(jnp.float32), slot)
    across = lax.broadcasted_iota(jnp.int32, (rows, rows), 1)
    down = lax.broadcasted_iota(jnp.int32, (rows, rows), 0)
    column = jnp.sum(jnp.where(across == down, slot, 0.0), axis=1, keepdims=True)
    out_ref[:, width:] = jnp.broadcast_to(column, (rows, LANES)).astype(jnp.bfloat16)


def normalize(hidden, norm_weight, adapter_index, adapter_slot):
    rows, width = hidden.shape
    vmem = pl.BlockSpec(memory_space=pltpu.VMEM)
    return pl.pallas_call(
        norm_kernel,
        out_shape=jax.ShapeDtypeStruct((rows, width + LANES), jnp.bfloat16),
        in_specs=[vmem, vmem, vmem, pl.BlockSpec(memory_space=pltpu.SMEM)],
        out_specs=vmem,
        compiler_params=pltpu.CompilerParams(vmem_limit_bytes=SMALL),
    )(hidden, norm_weight.reshape(1, width), adapter_index.reshape(1, rows), adapter_slot)


def prepare_kernel(*refs):
    blocks, refs = refs[:CORNERS], refs[CORNERS:]
    own_ref, other_ref, *before, rows_ref, part_ref, slot_ref = refs
    rank, width = own_ref.shape
    rows = rows_ref.shape[0]
    part = jnp.zeros((rows, 2 * rank), jnp.float32)
    for start in range(0, width, CHUNK):
        lanes = slice(start, start + CHUNK)
        wide = [block[:, lanes].astype(jnp.float32) for block in blocks]
        chunk = jnp.concatenate(wide, axis=0).astype(jnp.bfloat16)
        rows_ref[:, lanes] = chunk
        down = jnp.concatenate([own_ref[:, lanes], other_ref[:, lanes]], axis=0)
        part += lax.dot_general(
            chunk, down, (((1,), (1,)), ((), ())), preferred_element_type=jnp.float32
        )
    slot = slot_column(blocks, width)
    slot_ref[...] = jnp.broadcast_to(slot, slot_ref.shape)
    me = lax.axis_index("adapter")
    lanes = lax.broadcasted_iota(jnp.int32, part.shape, 1)
    holder = jnp.where(lanes < rank, me, me ^ 1)
    part = jnp.where(slot == holder, part, 0.0)
    part = part[:, :rank] + part[:, rank:]
    for ref in before:
        part = part + ref[...].astype(jnp.float32)
    part_ref[...] = part.astype(jnp.bfloat16)


def prepare(blocks, own, other, before):
    rows = blocks[0].shape[0] * CORNERS
    rank, width = own.shape
    before = [] if before is None else [before]
    vmem = pl.BlockSpec(memory_space=pltpu.VMEM)
    return pl.pallas_call(
        prepare_kernel,
        out_shape=(
            jax.ShapeDtypeStruct((rows, width), jnp.bfloat16),
            jax.ShapeDtypeStruct((rows, rank), jnp.bfloat16),
            jax.ShapeDtypeStruct((rows, LANES), jnp.int32),
        ),
        in_specs=[vmem] * (CORNERS + 2 + len(before)),
        out_specs=(vmem, vmem, vmem),
        compiler_params=pltpu.CompilerParams(vmem_limit_bytes=SMALL),
        cost_estimate=pl.CostEstimate(
            flops=2 * rows * width * 256, bytes_accessed=rows * width * 4, transcendentals=0
        ),
    )(*blocks, own, other, *before)


def finish_kernel(places, devices, *refs):
    bases, shrinks, slots = refs[:places], refs[places : 2 * places], refs[2 * places : 3 * places]
    up_ref, out_ref = refs[3 * places :]
    rows, rank = shrinks[0].shape
    own_rows = rows // CORNERS
    lanes = lax.broadcasted_iota(jnp.int32, (rows, devices * rank), 1)
    for step in range(places):
        shrink = shrinks[step][...].astype(jnp.float32)
        wide = jnp.concatenate([shrink] * devices, axis=1)
        slot = slots[step][:, 0:1]
        spread = jnp.where(lanes // rank == slot, wide, 0.0).astype(jnp.bfloat16)
        update = jnp.dot(spread, up_ref[...], preferred_element_type=jnp.float32)
        query = (bases[step][...] + ADAPTER_SCALE * update).astype(jnp.bfloat16)
        for corner in range(CORNERS):
            owner = ring_device(places, -step, corner)
            out_ref[owner] = query[corner * own_rows : (corner + 1) * own_rows]


def finish(bases, shrinks, slots, up):
    places, devices = len(bases), up.shape[0]
    rows, columns = bases[0].shape
    rank = up.shape[1]
    vmem = pl.BlockSpec(memory_space=pltpu.VMEM)
    return pl.pallas_call(
        lambda *refs: finish_kernel(places, devices, *refs),
        out_shape=jax.ShapeDtypeStruct((devices, rows // CORNERS, columns), jnp.bfloat16),
        in_specs=[vmem] * (3 * places + 1),
        out_specs=vmem,
        compiler_params=pltpu.CompilerParams(vmem_limit_bytes=SMALL),
    )(*bases, *shrinks, *slots, up.reshape(devices * rank, columns))


def shards(
    hidden, norm_weight, query_weight, down_weights, up_weights, adapter_index, adapter_slot
):
    devices = lax.axis_size("adapter")
    me = lax.axis_index("adapter")
    places = devices // CORNERS
    own_rows, width = hidden.shape
    rank = down_weights.shape[2]

    def move(x, steps, flip):
        return lax.ppermute(x, "adapter", pairs(places, steps, flip))

    def matmul(x, y):
        return jnp.dot(x, y, preferred_element_type=jnp.float32)

    chain = normalize(hidden, norm_weight, adapter_index, adapter_slot)
    down = down_weights[0].T
    down_other = move(down, 0, 1)

    bases, slots, travelling, other_y = [], [], None, None
    for step in range(places):
        if step:
            chain = move(chain, 1, 0)
        if step < places - 1:
            other_y = move(chain, 0, 2)
        else:
            source = jnp.where(me % CORES == 0, chain, other_y)
            other_y = lax.ppermute(source, "adapter", split_pairs(places))
        blocks = [chain, move(chain, 0, 1), other_y, move(other_y, 0, 1)]
        before = None if travelling is None else move(travelling, 1, 0)
        rows, travelling, slot = prepare(blocks, down, down_other, before)
        slots.append(slot)
        bases.append(matmul(rows, query_weight))

    blocks = move(travelling, 0, 2).reshape(CORNERS, own_rows, rank)
    blocks = jnp.concatenate([blocks[corner ^ 2] for corner in range(CORNERS)], axis=0)
    shrink = travelling + blocks
    shrinks = [move(shrink, step + 1, 0) for step in range(places - 1)] + [shrink]
    query = finish(bases, shrinks, slots, up_weights)
    query = query.reshape(devices * own_rows, query.shape[2])
    return lax.all_to_all(query, "adapter", split_axis=0, concat_axis=1, tiled=True)


def solution(mesh):
    in_specs = (
        P(("group", "adapter"), None),
        P(),
        P(None, "adapter"),
        P("adapter", None, None),
        P(None, None, "adapter"),
        P(("group", "adapter"), None),
        P(),
    )
    out_specs = P(("group", "adapter"), None)
    return jax.shard_map(shards, mesh=mesh, in_specs=in_specs, out_specs=out_specs, check_vma=False)
```

```python
import jax
import jax.numpy as jnp
from jax import lax
from jax.experimental import pallas as pl
from jax.experimental.pallas import tpu as pltpu
from jax.sharding import PartitionSpec as P

ADAPTER_SCALE = 0.5
EPS = 1e-05

SIDE = 2
CORES = 2
CORNERS = SIDE * CORES
LANES = 128
CHUNK = 1024
SMALL = 16 << 20


def line_ring(places):
    odd = list(range(1, places, 2))
    even = list(range(0, places, 2))
    return [0] + odd + even[:0:-1]


def pairs(places, steps, flip):
    ring = line_ring(places)
    out = []
    for at, place in enumerate(ring):
        target = ring[(at + steps) % places]
        for corner in range(CORNERS):
            out.append((place * CORNERS + corner, target * CORNERS + (corner ^ flip)))
    return out


def split_pairs(places):
    flips, steps = pairs(places, 0, 2), pairs(places, 1, 0)
    return [pair for pair in flips if pair[0] % CORES == 0] + [
        pair for pair in steps if pair[0] % CORES
    ]


def ring_device(places, steps, flip):
    me = lax.axis_index("adapter")
    ring = line_ring(places)
    place, corner = me // CORNERS, me % CORNERS
    target = jnp.int32(0)
    for at, name in enumerate(ring):
        target = jnp.where(place == name, jnp.int32(ring[(at + steps) % places]), target)
    return target * CORNERS + (corner ^ flip)


def slot_column(blocks, width):
    return jnp.concatenate(
        [block[:, width : width + 1].astype(jnp.float32) for block in blocks], axis=0
    ).astype(jnp.int32)


def norm_kernel(*refs):
    sources, (out_ref, *buffers, sems) = refs[:4], refs[4:]
    copies = [
        pltpu.make_async_copy(source, buffer, sems.at[number])
        for number, (source, buffer) in enumerate(zip(sources, buffers))
    ]
    for copy in copies:
        copy.start()
    for copy in copies:
        copy.wait()
    hidden_ref, gain_ref, index_ref, slot_ref = buffers
    rows, width = hidden_ref.shape
    squares = jnp.zeros((rows, LANES), jnp.float32)
    for start in range(0, width, CHUNK):
        wide = hidden_ref[:, start : start + CHUNK].astype(jnp.float32)
        wide = wide * wide
        for lane in range(0, CHUNK, LANES):
            squares = squares + wide[:, lane : lane + LANES]
    inv_rms = lax.rsqrt(jnp.sum(squares, axis=1, keepdims=True) / width + EPS)
    for start in range(0, width, CHUNK):
        lanes = slice(start, start + CHUNK)
        wide = hidden_ref[:, lanes].astype(jnp.float32)
        out_ref[:, lanes] = (wide * inv_rms * gain_ref[:, lanes]).astype(jnp.bfloat16)
    index = index_ref[...]
    slot = jnp.zeros(index.shape, jnp.float32)
    for name in range(slot_ref.shape[1]):
        slot = jnp.where(index == name, slot_ref[0, name].astype(jnp.float32), slot)
    across = lax.broadcasted_iota(jnp.int32, (rows, rows), 1)
    down = lax.broadcasted_iota(jnp.int32, (rows, rows), 0)
    column = jnp.sum(jnp.where(across == down, slot, 0.0), axis=1, keepdims=True)
    out_ref[:, width:] = jnp.broadcast_to(column, (rows, LANES)).astype(jnp.bfloat16)


def normalize(hidden, norm_weight, adapter_index, adapter_slot):
    rows, width = hidden.shape
    sources = (
        hidden,
        norm_weight.reshape(1, width),
        adapter_index.reshape(1, rows),
        adapter_slot.reshape(1, -1),
    )
    spaces = (pltpu.VMEM, pltpu.VMEM, pltpu.VMEM, pltpu.SMEM)
    return pl.pallas_call(
        norm_kernel,
        out_shape=jax.ShapeDtypeStruct((rows, width + LANES), jnp.bfloat16),
        in_specs=[pl.BlockSpec(memory_space=pltpu.HBM)] * len(sources),
        out_specs=pl.BlockSpec(memory_space=pltpu.VMEM),
        scratch_shapes=[space(x.shape, x.dtype) for space, x in zip(spaces, sources)]
        + [pltpu.SemaphoreType.DMA((len(sources),))],
    )(*sources)


def step_kernel(with_base, *refs):
    blocks, refs = refs[:CORNERS], refs[CORNERS:]
    own_ref, other_ref, *refs = refs
    if with_base:
        weight_ref, *before, part_ref, slot_ref, base_ref = refs
    else:
        *before, part_ref, slot_ref, rows_ref = refs
    rank, width = own_ref.shape
    rows = part_ref.shape[0]
    part = jnp.zeros((rows, 2 * rank), jnp.float32)
    if with_base:
        base_ref[...] = jnp.zeros(base_ref.shape, jnp.float32)
    for start in range(0, width, CHUNK):
        lanes = slice(start, start + CHUNK)
        wide = [block[:, lanes].astype(jnp.float32) for block in blocks]
        chunk = jnp.concatenate(wide, axis=0).astype(jnp.bfloat16)
        down = jnp.concatenate([own_ref[:, lanes], other_ref[:, lanes]], axis=0)
        part += lax.dot_general(
            chunk, down, (((1,), (1,)), ((), ())), preferred_element_type=jnp.float32
        )
        if with_base:
            base_ref[...] += jnp.dot(
                chunk, weight_ref[lanes, :], preferred_element_type=jnp.float32
            )
        else:
            rows_ref[:, lanes] = chunk
    slot = slot_column(blocks, width)
    slot_ref[...] = jnp.broadcast_to(slot, slot_ref.shape)
    me = lax.axis_index("adapter")
    lanes = lax.broadcasted_iota(jnp.int32, part.shape, 1)
    holder = jnp.where(lanes < rank, me, me ^ 1)
    part = jnp.where(slot == holder, part, 0.0)
    part = part[:, :rank] + part[:, rank:]
    for ref in before:
        part = part + ref[...].astype(jnp.float32)
    part_ref[...] = part.astype(jnp.bfloat16)


def step_rows(blocks, own, other, weight, before):
    rows = blocks[0].shape[0] * CORNERS
    rank, width = own.shape
    with_base = weight is not None
    third = (
        jax.ShapeDtypeStruct((rows, weight.shape[1]), jnp.float32)
        if with_base
        else jax.ShapeDtypeStruct((rows, width), jnp.bfloat16)
    )
    operands = [*blocks, own, other, *([weight] if with_base else []), *before]
    vmem = pl.BlockSpec(memory_space=pltpu.VMEM)
    return pl.pallas_call(
        lambda *refs: step_kernel(with_base, *refs),
        out_shape=(
            jax.ShapeDtypeStruct((rows, rank), jnp.bfloat16),
            jax.ShapeDtypeStruct((rows, LANES), jnp.int32),
            third,
        ),
        in_specs=[vmem] * len(operands),
        out_specs=(vmem, vmem, vmem),
        compiler_params=pltpu.CompilerParams(vmem_limit_bytes=SMALL),
        cost_estimate=pl.CostEstimate(flops=1, bytes_accessed=1, transcendentals=0),
    )(*operands)


def after(x, *others):
    return lax.optimization_barrier((x, *others))[0]


def finish_kernel(offsets, devices, *refs):
    places = len(offsets)
    bases, shrinks, slots = refs[:places], refs[places : 2 * places], refs[2 * places : 3 * places]
    up_ref, out_ref = refs[3 * places :]
    rows, rank = shrinks[0].shape
    own_rows = rows // CORNERS
    lanes = lax.broadcasted_iota(jnp.int32, (rows, devices * rank), 1)
    for step, offset in enumerate(offsets):
        shrink = shrinks[step][...].astype(jnp.float32)
        wide = jnp.concatenate([shrink] * devices, axis=1)
        slot = slots[step][:, 0:1]
        spread = jnp.where(lanes // rank == slot, wide, 0.0).astype(jnp.bfloat16)
        update = jnp.dot(spread, up_ref[...], preferred_element_type=jnp.float32)
        query = (bases[step][...] + ADAPTER_SCALE * update).astype(jnp.bfloat16)
        for corner in range(CORNERS):
            owner = ring_device(places, -offset, corner)
            out_ref[owner] = query[corner * own_rows : (corner + 1) * own_rows]


def finish(offsets, bases, shrinks, slots, up):
    places, devices = len(bases), up.shape[0]
    rows, columns = bases[0].shape
    rank = up.shape[1]
    vmem = pl.BlockSpec(memory_space=pltpu.VMEM)
    return pl.pallas_call(
        lambda *refs: finish_kernel(offsets, devices, *refs),
        out_shape=jax.ShapeDtypeStruct((devices, rows // CORNERS, columns), jnp.bfloat16),
        in_specs=[vmem] * (3 * places + 1),
        out_specs=vmem,
        compiler_params=pltpu.CompilerParams(vmem_limit_bytes=SMALL),
    )(*bases, *shrinks, *slots, up.reshape(devices * rank, columns))


def shards(
    hidden, norm_weight, query_weight, down_weights, up_weights, adapter_index, adapter_slot
):
    devices = lax.axis_size("adapter")
    me = lax.axis_index("adapter")
    places = devices // CORNERS
    own_rows, width = hidden.shape
    rank = down_weights.shape[2]

    def move(x, steps, flip):
        return lax.ppermute(x, "adapter", pairs(places, steps, flip))

    chain = normalize(hidden, norm_weight, adapter_index, adapter_slot)
    down = down_weights[0].T
    down_other = move(down, 0, 1)

    far = places // 2
    offsets = [0] + [sign * near for near in range(1, far) for sign in (1, -1)] + [far]
    block = {0: chain}
    for near in range(1, far):
        block[near] = move(block[near - 1], 1, 0)
        block[-near] = move(block[1 - near], -1, 0)
    block[far] = move(block[far - 1], 1, 0)
    other, crossed = {}, None
    parts, slots, bases, done, before = {}, {}, {}, [], []
    for offset in offsets:
        here = after(block[offset], *done[:-1])
        if offset != far:
            other[offset] = move(here, 0, 2)
        else:
            source = jnp.where((me & 1) == 0, after(here, *before[:-1]), other[far - 1])
            other[far] = lax.ppermute(source, "adapter", split_pairs(places))
        there = after(other[offset], *done)
        rows = [here, move(here, 0, 1), there, move(there, 0, 1)]
        if offset != far:
            parts[offset], slots[offset], bases[offset] = step_rows(
                rows, down, down_other, query_weight, []
            )
            done.append(parts[offset])
            before.append(move(parts[offset], far - offset, 0))
    part, slots[far], rows = step_rows(rows, down, down_other, None, before)
    bases[far] = jnp.dot(rows, query_weight, preferred_element_type=jnp.float32)

    blocks = move(part, 0, 2).reshape(CORNERS, own_rows, rank)
    blocks = jnp.concatenate([blocks[corner ^ 2] for corner in range(CORNERS)], axis=0)
    part = part + blocks
    shrinks = [part if offset == far else move(part, offset - far, 0) for offset in offsets]
    bases = [bases[offset] for offset in offsets]
    slots = [slots[offset] for offset in offsets]
    query = finish(offsets, bases, shrinks, slots, up_weights)
    query = query.reshape(devices * own_rows, query.shape[2])
    return lax.all_to_all(query, "adapter", split_axis=0, concat_axis=1, tiled=True)


def solution(mesh):
    in_specs = (
        P(("group", "adapter"), None),
        P(),
        P(None, "adapter"),
        P("adapter", None, None),
        P(None, None, "adapter"),
        P(("group", "adapter"), None),
        P(),
    )
    out_specs = P(("group", "adapter"), None)
    return jax.shard_map(shards, mesh=mesh, in_specs=in_specs, out_specs=out_specs, check_vma=False)
```

```python
import jax
import jax.numpy as jnp
from jax import lax
from jax.experimental import pallas as pl
from jax.experimental.pallas import tpu as pltpu
from jax.sharding import PartitionSpec as P

ADAPTER_SCALE = 0.5
EPS = 1e-05

SIDE = 2
CORES = 2
CORNERS = SIDE * CORES
LANES = 128
CHUNK = 1024
VMEM_LIMIT = 24 << 20
VMEM = pl.BlockSpec(memory_space=pltpu.VMEM)


def line_ring(places):
    odd = list(range(1, places, 2))
    even = list(range(0, places, 2))
    return [0] + odd + even[:0:-1]


def pairs(places, steps, flip):
    ring = line_ring(places)
    out = []
    for at, place in enumerate(ring):
        target = ring[(at + steps) % places]
        for corner in range(CORNERS):
            out.append((place * CORNERS + corner, target * CORNERS + (corner ^ flip)))
    return out


def split_pairs(places):
    flips, steps = pairs(places, 0, 2), pairs(places, 1, 0)
    return [pair for pair in flips if pair[0] % CORES == 0] + [
        pair for pair in steps if pair[0] % CORES
    ]


def ring_chip(places, steps, side):
    chip = lax.axis_index("adapter") // CORES
    ring = line_ring(places)
    target = jnp.int32(0)
    for at, name in enumerate(ring):
        target = jnp.where(chip // SIDE == name, jnp.int32(ring[(at + steps) % places]), target)
    return target * SIDE + ((chip % SIDE) ^ side)


def after(x, *others):
    return lax.optimization_barrier((x, *others))[0]


def call(kernel, out_shape, operands, specs=None, scratch=(), limit=VMEM_LIMIT):
    return pl.pallas_call(
        kernel,
        out_shape=out_shape,
        in_specs=[VMEM] * len(operands) if specs is None else specs,
        out_specs=jax.tree.map(lambda _: VMEM, out_shape),
        scratch_shapes=list(scratch),
        compiler_params=pltpu.CompilerParams(vmem_limit_bytes=limit),
        cost_estimate=pl.CostEstimate(flops=1, bytes_accessed=1, transcendentals=0),
    )(*operands)


def norm_kernel(*refs):
    sources, (out_ref, *buffers, sems) = refs[:4], refs[4:]
    copies = [
        pltpu.make_async_copy(source, buffer, sems.at[number])
        for number, (source, buffer) in enumerate(zip(sources, buffers))
    ]
    for copy in copies:
        copy.start()
    for copy in copies:
        copy.wait()
    hidden_ref, gain_ref, index_ref, slot_ref = buffers
    rows, width = hidden_ref.shape
    squares = jnp.zeros((rows, LANES), jnp.float32)
    for start in range(0, width, CHUNK):
        wide = hidden_ref[:, start : start + CHUNK].astype(jnp.float32)
        wide = wide * wide
        for lane in range(0, CHUNK, LANES):
            squares = squares + wide[:, lane : lane + LANES]
    inv_rms = lax.rsqrt(jnp.sum(squares, axis=1, keepdims=True) / width + EPS)
    for start in range(0, width, CHUNK):
        lanes = slice(start, start + CHUNK)
        wide = hidden_ref[:, lanes].astype(jnp.float32)
        out_ref[:, lanes] = (wide * inv_rms * gain_ref[:, lanes]).astype(jnp.bfloat16)
    index = index_ref[...]
    slot = jnp.zeros(index.shape, jnp.float32)
    for name in range(slot_ref.shape[1]):
        slot = jnp.where(index == name, slot_ref[0, name].astype(jnp.float32), slot)
    across = lax.broadcasted_iota(jnp.int32, (rows, rows), 1)
    down = lax.broadcasted_iota(jnp.int32, (rows, rows), 0)
    column = jnp.sum(jnp.where(across == down, slot, 0.0), axis=1, keepdims=True)
    out_ref[:, width:] = jnp.broadcast_to(column, (rows, LANES)).astype(jnp.bfloat16)


def normalize(hidden, norm_weight, adapter_index, adapter_slot):
    rows, width = hidden.shape
    sources = (
        hidden,
        norm_weight.reshape(1, width),
        adapter_index.reshape(1, rows),
        adapter_slot.reshape(1, -1),
    )
    spaces = (pltpu.VMEM, pltpu.VMEM, pltpu.VMEM, pltpu.SMEM)
    return pl.pallas_call(
        norm_kernel,
        out_shape=jax.ShapeDtypeStruct((rows, width + LANES), jnp.bfloat16),
        in_specs=[pl.BlockSpec(memory_space=pltpu.HBM)] * len(sources),
        out_specs=VMEM,
        scratch_shapes=[space(x.shape, x.dtype) for space, x in zip(spaces, sources)]
        + [pltpu.SemaphoreType.DMA((len(sources),))],
    )(*sources)


def stacked(blocks, lanes):
    wide = [block[:, lanes].astype(jnp.float32) for block in blocks]
    return jnp.concatenate(wide, axis=0).astype(jnp.bfloat16)


def shrink_kernel(*refs):
    blocks, (own_ref, other_ref, *before, part_ref, slot_ref) = refs[:SIDE], refs[SIDE:]
    rank, width = own_ref.shape
    rows = part_ref.shape[0]
    part = jnp.zeros((rows, 2 * rank), jnp.float32)
    for start in range(0, width, CHUNK):
        lanes = slice(start, start + CHUNK)
        down = jnp.concatenate([own_ref[:, lanes], other_ref[:, lanes]], axis=0)
        part += lax.dot_general(
            stacked(blocks, lanes), down, (((1,), (1,)), ((), ())), preferred_element_type=jnp.float32
        )
    slot = jnp.concatenate(
        [block[:, width : width + 1].astype(jnp.float32) for block in blocks], axis=0
    ).astype(jnp.int32)
    slot_ref[...] = jnp.broadcast_to(slot, slot_ref.shape)
    me = lax.axis_index("adapter")
    lanes = lax.broadcasted_iota(jnp.int32, part.shape, 1)
    part = jnp.where(slot == jnp.where(lanes < rank, me, me ^ 1), part, 0.0)
    part = part[:, :rank] + part[:, rank:]
    for ref in before:
        part = part + ref[...].astype(jnp.float32)
    part_ref[...] = part.astype(jnp.bfloat16)


def shrink_rows(blocks, own, other, before):
    rows = blocks[0].shape[0] * SIDE
    out_shape = (
        jax.ShapeDtypeStruct((rows, own.shape[0]), jnp.bfloat16),
        jax.ShapeDtypeStruct((rows, LANES), jnp.int32),
    )
    return call(shrink_kernel, out_shape, (*blocks, own, other, *before))


def base_kernel(*refs):
    *blocks, weight_ref, out_ref, buffer, sems = refs
    width = weight_ref.shape[0]
    copies = []
    for number, start in enumerate(range(0, width, CHUNK)):
        rows = pl.ds(start, CHUNK)
        copies.append(
            pltpu.make_async_copy(weight_ref.at[rows], buffer.at[rows], sems.at[number])
        )
        copies[-1].start()
    out_ref[...] = jnp.zeros(out_ref.shape, jnp.float32)
    for number, start in enumerate(range(0, width, CHUNK)):
        lanes = slice(start, start + CHUNK)
        rows = stacked(blocks, lanes)
        copies[number].wait()
        out_ref[...] += jnp.dot(rows, buffer[lanes, :], preferred_element_type=jnp.float32)


def base_rows(blocks, weight):
    rows = blocks[0].shape[0] * len(blocks)
    specs = [VMEM] * len(blocks) + [pl.BlockSpec(memory_space=pltpu.HBM)]
    return call(
        base_kernel,
        jax.ShapeDtypeStruct((rows, weight.shape[1]), jnp.float32),
        (*blocks, weight),
        specs,
        (
            pltpu.VMEM(weight.shape, weight.dtype),
            pltpu.SemaphoreType.DMA((weight.shape[0] // CHUNK,)),
        ),
        48 << 20,
    )


def finish_kernel(steps, per_base, *refs):
    bases, refs = refs[: 2 * (steps // per_base)], refs[2 * (steps // per_base) :]
    shrinks, slots, (own_ref, other_ref, *outs) = refs[:steps], refs[steps : 2 * steps], refs[2 * steps :]
    rows, rank = shrinks[0].shape
    own_rows = rows // SIDE
    columns = own_ref.shape[1]
    depth = own_ref.shape[0]
    core = lax.axis_index("adapter") % CORES
    lanes = lax.broadcasted_iota(jnp.int32, (rows, depth), 1)
    for step in range(steps):
        wide = jnp.concatenate([shrinks[step][...].astype(jnp.float32)] * (depth // rank), axis=1)
        spread = jnp.where(lanes // rank == slots[step][:, 0:1], wide, 0.0).astype(jnp.bfloat16)
        first = step % per_base * rows
        for which, up_ref in enumerate((own_ref, other_ref)):
            update = jnp.dot(spread, up_ref[...], preferred_element_type=jnp.float32)
            base = bases[2 * (step // per_base) + which][first : first + rows, :]
            query = (base + ADAPTER_SCALE * update).astype(jnp.bfloat16)
            at = pl.multiple_of((core ^ which) * columns, columns)
            for side in range(SIDE):
                outs[step * SIDE + side][:, pl.ds(at, columns)] = query[
                    side * own_rows : (side + 1) * own_rows
                ]


def finish(bases, shrinks, slots, own, other):
    steps, per_base = len(shrinks), 2 * len(shrinks) // len(bases)
    rows = shrinks[0].shape[0] // SIDE
    block = jax.ShapeDtypeStruct((rows, CORES * own.shape[1]), jnp.bfloat16)
    return call(
        lambda *refs: finish_kernel(steps, per_base, *refs),
        [block] * (steps * SIDE),
        (*bases, *shrinks, *slots, own, other),
    )


def assemble_kernel(places, offsets, *refs):
    *blocks, out_ref = refs
    columns = blocks[0].shape[1]
    for step, offset in enumerate(offsets):
        for side in range(SIDE):
            at = pl.multiple_of(ring_chip(places, offset, side) * columns, columns)
            out_ref[:, pl.ds(at, columns)] = blocks[step * SIDE + side][...]


def assemble(places, offsets, blocks):
    rows, columns = blocks[0].shape
    return call(
        lambda *refs: assemble_kernel(places, offsets, *refs),
        jax.ShapeDtypeStruct((rows, columns * len(blocks)), jnp.bfloat16),
        blocks,
    )


def shards(
    hidden, norm_weight, query_weight, down_weights, up_weights, adapter_index, adapter_slot
):
    devices = lax.axis_size("adapter")
    me = lax.axis_index("adapter")
    places = devices // CORNERS
    own_rows, width = hidden.shape
    columns = query_weight.shape[1]
    rank = down_weights.shape[2]

    def move(x, steps, flip):
        return lax.ppermute(x, "adapter", pairs(places, steps, flip))

    chain = normalize(hidden, norm_weight, adapter_index, adapter_slot)
    down = down_weights[0].T
    up = up_weights.reshape(devices * rank, columns)
    down_other = move(down, 0, 1)
    weight_other = move(query_weight, 0, 1)

    far = places // 2
    offsets = [0] + [sign * near for near in range(1, far) for sign in (1, -1)] + [far]
    block = {0: chain}
    for near in range(1, far):
        block[near] = move(block[near - 1], 1, 0)
        block[-near] = move(block[1 - near], -1, 0)
    block[far] = move(block[far - 1], 1, 0)
    other, parts, slots, before, bases, queue = {}, [], [], [], [], []
    for number, offset in enumerate(offsets):
        here = after(block[offset], *parts[:-1])
        if offset != far:
            other[offset] = move(here, 0, 2)
        else:
            here = after(here, other[offsets[-2]], *before[:-1], *bases)
            source = jnp.where((me & 1) == 0, here, other[far - 1])
            other[far] = lax.ppermute(source, "adapter", split_pairs(places))
            bases.append(base_rows(after(queue, source), weight_other))
            up_other = move(after(up, source), 0, 1)
            other[far] = after(other[far], bases[-1])
        rows = [here, after(other[offset], *parts)]
        if 0 < offset < far:
            rows = after(rows, block[-offset])
        part, slot = shrink_rows(rows, down, down_other, before if offset == far else [])
        parts.append(part)
        slots.append(slot)
        if offset != far:
            before.append(move(part, far - offset, 0))
        if number % 2 == 0:
            waiting = rows
        else:
            if queue and offset != far:
                bases.append(base_rows(queue, weight_other))
            queue = waiting + rows
            if offset != far:
                bases.append(base_rows(queue, query_weight))

    across = move(part, 0, 2)
    base_own = base_rows(queue, query_weight)
    across = after(across, base_own)
    part = part + jnp.concatenate([across[own_rows:], across[:own_rows]], axis=0)
    shrinks = [part if offset == far else move(part, offset - far, 0) for offset in offsets]
    bases += [base_own, base_rows(queue, weight_other)]
    blocks = finish(bases, shrinks, slots, up, up_other)
    parts = []
    for number, offset in enumerate(offsets):
        for side in range(SIDE):
            piece = blocks[number * SIDE + side]
            parts.append(move(piece, -offset, 2 * side) if offset or side else piece)
    return assemble(places, offsets, parts)


def solution(mesh):
    in_specs = (
        P(("group", "adapter"), None),
        P(),
        P(None, "adapter"),
        P("adapter", None, None),
        P(None, None, "adapter"),
        P(("group", "adapter"), None),
        P(),
    )
    out_specs = P(("group", "adapter"), None)
    return jax.shard_map(shards, mesh=mesh, in_specs=in_specs, out_specs=out_specs, check_vma=False)
```

```python
import jax
import jax.numpy as jnp
from jax import lax
from jax.experimental import pallas as pl
from jax.experimental.pallas import tpu as pltpu
from jax.sharding import PartitionSpec as P

ADAPTER_SCALE = 0.5
EPS = 1e-05

SIDE = 2
CORES = 2
CORNERS = SIDE * CORES
LANES = 128
CHUNK = 1024
VMEM_LIMIT = 24 << 20
AHEAD = 2
VMEM = pl.BlockSpec(memory_space=pltpu.VMEM)


def line_ring(places):
    odd = list(range(1, places, 2))
    even = list(range(0, places, 2))
    return [0] + odd + even[:0:-1]


def pairs(places, steps, flip):
    ring = line_ring(places)
    out = []
    for at, place in enumerate(ring):
        target = ring[(at + steps) % places]
        for corner in range(CORNERS):
            out.append((place * CORNERS + corner, target * CORNERS + (corner ^ flip)))
    return out


def split_pairs(places):
    flips, steps = pairs(places, 0, 2), pairs(places, 1, 0)
    return [pair for pair in flips if pair[0] % CORES == 0] + [
        pair for pair in steps if pair[0] % CORES
    ]


def ring_chip(places, steps, side):
    chip = lax.axis_index("adapter") // CORES
    ring = line_ring(places)
    target = jnp.int32(0)
    for at, name in enumerate(ring):
        target = jnp.where(chip // SIDE == name, jnp.int32(ring[(at + steps) % places]), target)
    return target * SIDE + ((chip % SIDE) ^ side)


def after(x, *others):
    return lax.optimization_barrier((x, *others))[0]


def call(kernel, out_shape, operands, specs=None, scratch=(), limit=VMEM_LIMIT):
    return pl.pallas_call(
        kernel,
        out_shape=out_shape,
        in_specs=[VMEM] * len(operands) if specs is None else specs,
        out_specs=jax.tree.map(lambda _: VMEM, out_shape),
        scratch_shapes=list(scratch),
        compiler_params=pltpu.CompilerParams(vmem_limit_bytes=limit),
        cost_estimate=pl.CostEstimate(flops=1, bytes_accessed=1, transcendentals=0),
    )(*operands)


def norm_kernel(*refs):
    sources, (out_ref, *buffers, sems) = refs[:4], refs[4:]
    copies = [
        pltpu.make_async_copy(source, buffer, sems.at[number])
        for number, (source, buffer) in enumerate(zip(sources, buffers))
    ]
    for copy in copies:
        copy.start()
    for copy in copies:
        copy.wait()
    hidden_ref, gain_ref, index_ref, slot_ref = buffers
    rows, width = hidden_ref.shape
    squares = jnp.zeros((rows, LANES), jnp.float32)
    for start in range(0, width, CHUNK):
        wide = hidden_ref[:, start : start + CHUNK].astype(jnp.float32)
        wide = wide * wide
        for lane in range(0, CHUNK, LANES):
            squares = squares + wide[:, lane : lane + LANES]
    inv_rms = lax.rsqrt(jnp.sum(squares, axis=1, keepdims=True) / width + EPS)
    for start in range(0, width, CHUNK):
        lanes = slice(start, start + CHUNK)
        wide = hidden_ref[:, lanes].astype(jnp.float32)
        out_ref[:, lanes] = (wide * inv_rms * gain_ref[:, lanes]).astype(jnp.bfloat16)
    index = index_ref[...]
    slot = jnp.zeros(index.shape, jnp.float32)
    for name in range(slot_ref.shape[1]):
        slot = jnp.where(index == name, slot_ref[0, name].astype(jnp.float32), slot)
    across = lax.broadcasted_iota(jnp.int32, (rows, rows), 1)
    down = lax.broadcasted_iota(jnp.int32, (rows, rows), 0)
    column = jnp.sum(jnp.where(across == down, slot, 0.0), axis=1, keepdims=True)
    out_ref[:, width:] = jnp.broadcast_to(column, (rows, LANES)).astype(jnp.bfloat16)


def normalize(hidden, norm_weight, adapter_index, adapter_slot):
    rows, width = hidden.shape
    sources = (
        hidden,
        norm_weight.reshape(1, width),
        adapter_index.reshape(1, rows),
        adapter_slot.reshape(1, -1),
    )
    spaces = (pltpu.VMEM, pltpu.VMEM, pltpu.VMEM, pltpu.SMEM)
    return pl.pallas_call(
        norm_kernel,
        out_shape=jax.ShapeDtypeStruct((rows, width + LANES), jnp.bfloat16),
        in_specs=[pl.BlockSpec(memory_space=pltpu.HBM)] * len(sources),
        out_specs=VMEM,
        scratch_shapes=[space(x.shape, x.dtype) for space, x in zip(spaces, sources)]
        + [pltpu.SemaphoreType.DMA((len(sources),))],
    )(*sources)


def stacked(blocks, lanes):
    wide = [block[:, lanes].astype(jnp.float32) for block in blocks]
    return jnp.concatenate(wide, axis=0).astype(jnp.bfloat16)


def shrink_kernel(count, *refs):
    blocks, (own_ref, other_ref, *before, part_ref, slot_ref) = refs[:count], refs[count:]
    rank, width = own_ref.shape
    rows = slot_ref.shape[0]
    part = jnp.zeros((rows, 2 * rank), jnp.float32)
    for start in range(0, width, CHUNK):
        lanes = slice(start, start + CHUNK)
        down = jnp.concatenate([own_ref[:, lanes], other_ref[:, lanes]], axis=0)
        part += lax.dot_general(
            stacked(blocks, lanes), down, (((1,), (1,)), ((), ())), preferred_element_type=jnp.float32
        )
    slot = jnp.concatenate(
        [block[:, width : width + 1].astype(jnp.float32) for block in blocks], axis=0
    ).astype(jnp.int32)
    slot_ref[...] = jnp.broadcast_to(slot, slot_ref.shape)
    me = lax.axis_index("adapter")
    lanes = lax.broadcasted_iota(jnp.int32, part.shape, 1)
    part = jnp.where(slot == jnp.where(lanes < rank, me, me ^ 1), part, 0.0)
    part = part[:, :rank] + part[:, rank:]
    first = 0
    for ref in before:
        part_ref[first : first + ref.shape[0], :] = ref[...]
        first += ref.shape[0]
    part_ref[first:, :] = part.astype(jnp.bfloat16)


def shrink_rows(blocks, own, other, before=()):
    rows = blocks[0].shape[0] * len(blocks)
    total = rows + sum(part.shape[0] for part in before)
    out_shape = (
        jax.ShapeDtypeStruct((total, own.shape[0]), jnp.bfloat16),
        jax.ShapeDtypeStruct((rows, LANES), jnp.int32),
    )
    return call(
        lambda *refs: shrink_kernel(len(blocks), *refs), out_shape, (*blocks, own, other, *before)
    )


def pack_kernel(own_rows, part_ref, across_ref, out_ref):
    rows, rank = part_ref.shape
    part = part_ref[...].astype(jnp.float32)
    across = across_ref[...].astype(jnp.float32)
    swapped = []
    for first in range(0, rows, SIDE * own_rows):
        middle, last = first + own_rows, first + SIDE * own_rows
        swapped += [across[middle:last], across[first:middle]]
    total = part + jnp.concatenate(swapped, axis=0)
    out_ref[...] = jnp.concatenate([total[: rows // 2], total[rows // 2 :]], axis=1).astype(jnp.bfloat16)


def pack(part, across, own_rows):
    rows, rank = part.shape
    out_shape = jax.ShapeDtypeStruct((rows // 2, 2 * rank), part.dtype)
    return call(lambda *refs: pack_kernel(own_rows, *refs), out_shape, (part, across))


def base_kernel(*refs):
    *blocks, weight_ref, out_ref, buffer, sems = refs
    width = weight_ref.shape[0]
    copies = []
    for number, start in enumerate(range(0, width, CHUNK)):
        rows = pl.ds(start, CHUNK)
        copies.append(
            pltpu.make_async_copy(weight_ref.at[rows], buffer.at[rows], sems.at[number])
        )
    for copy in copies[:AHEAD]:
        copy.start()
    out_ref[...] = jnp.zeros(out_ref.shape, jnp.float32)
    for number, start in enumerate(range(0, width, CHUNK)):
        lanes = slice(start, start + CHUNK)
        rows = stacked(blocks, lanes)
        copies[number].wait()
        if number + AHEAD < len(copies):
            copies[number + AHEAD].start()
        out_ref[...] += jnp.dot(rows, buffer[lanes, :], preferred_element_type=jnp.float32)


def base_rows(blocks, weight):
    rows = blocks[0].shape[0] * len(blocks)
    specs = [VMEM] * len(blocks) + [pl.BlockSpec(memory_space=pltpu.HBM)]
    return call(
        base_kernel,
        jax.ShapeDtypeStruct((rows, weight.shape[1]), jnp.float32),
        (*blocks, weight),
        specs,
        (
            pltpu.VMEM(weight.shape, weight.dtype),
            pltpu.SemaphoreType.DMA((weight.shape[0] // CHUNK,)),
        ),
        48 << 20,
    )


def finish_kernel(places, rank, *refs):
    moved, refs = refs[:places], refs[places:]
    slot_count = len(refs) - places - 3
    bases, slots = refs[:places], refs[places : places + slot_count]
    own_ref, other_ref, out_ref = refs[places + slot_count :]
    depth, columns = own_ref.shape
    rows = SIDE * out_ref.shape[1]
    core = lax.axis_index("adapter") % CORES
    lanes = lax.broadcasted_iota(jnp.int32, (rows, depth), 1)
    slot = jnp.concatenate([ref[:, 0:1] for ref in slots], axis=0)
    for step in range(places):
        shrink = jnp.zeros((rows, rank), jnp.float32)
        for back in range(places):
            half, first = divmod((step - back) % places, places // 2)
            part = moved[back][first * rows : (first + 1) * rows, half * rank : (half + 1) * rank]
            shrink += part.astype(jnp.float32)
        wide = jnp.concatenate([shrink] * (depth // rank), axis=1)
        here = slot[step * rows : (step + 1) * rows]
        spread = jnp.where(lanes // rank == here, wide, 0.0).astype(jnp.bfloat16)
        for which, up_ref in enumerate((own_ref, other_ref)):
            update = jnp.dot(spread, up_ref[...], preferred_element_type=jnp.float32)
            base = bases[step // 2 * 2 + which][step % 2 * rows : (step % 2 + 1) * rows, :]
            query = (base + ADAPTER_SCALE * update).astype(jnp.bfloat16)
            at = pl.multiple_of((core ^ which) * columns, columns)
            for side in range(SIDE):
                chip = ring_chip(places, -step, side)
                out_ref[chip, :, pl.ds(at, columns)] = query[side * rows // SIDE : (side + 1) * rows // SIDE]


def finish(moved, bases, slots, own, other, own_rows):
    places, rank = len(moved), moved[0].shape[1] // 2
    return call(
        lambda *refs: finish_kernel(places, rank, *refs),
        jax.ShapeDtypeStruct((places * SIDE, own_rows, CORES * own.shape[1]), jnp.bfloat16),
        (*moved, *bases, *slots, own, other),
    )


def shards(
    hidden, norm_weight, query_weight, down_weights, up_weights, adapter_index, adapter_slot
):
    devices = lax.axis_size("adapter")
    me = lax.axis_index("adapter")
    places = devices // CORNERS
    own_rows, width = hidden.shape
    columns = query_weight.shape[1]
    rank = down_weights.shape[2]

    def move(x, steps, flip):
        return lax.ppermute(x, "adapter", pairs(places, steps, flip))

    down = down_weights[0].T
    up = up_weights.reshape(devices * rank, columns)
    down_other = move(down, 0, 1)
    up_other = move(up, 0, 1)
    weight_other = move(query_weight, 0, 1)

    block, other = [normalize(hidden, norm_weight, adapter_index, adapter_slot)], []
    parts, slots, bases = [], [], []
    last = places - 1
    for step in range(last):
        block.append(move(block[step], 1, 0))
        other.append(move(after(block[step], *other[-1:]), 0, 2))
        if step % 2 == 0 and step:
            rows = [block[step - 2], other[step - 2], block[step - 1], other[step - 1]]
            rows = after(rows, block[step])
            part, slot = shrink_rows(rows, down, down_other)
            parts.append(part)
            slots.append(slot)
            bases.append(base_rows(after(rows, part), query_weight))
            if step < last - 1:
                bases.append(base_rows(rows, weight_other))
    source = jnp.where((me & 1) == 0, after(block[last], *bases, other[-1]), other[-1])
    crossed = lax.ppermute(source, "adapter", split_pairs(places))
    part, slot = shrink_rows(after([block[last - 1], other[-1]], source), down, down_other)
    parts.append(part)
    slots.append(slot)
    bases.append(base_rows(after(rows, part), weight_other))
    crossed = after(crossed, *bases)
    part, slot = shrink_rows([block[last], crossed], down, down_other, parts)
    slots.append(slot)

    across = move(part, 0, 2)
    rows = [block[last - 1], other[-1], block[last], crossed]
    bases.append(base_rows(rows, query_weight))
    part = pack(part, after(across, bases[-1]), own_rows)
    moved = [part] + [move(part, steps, 0) for steps in range(1, places)]
    bases.append(base_rows(rows, weight_other))
    query = finish(moved, bases, slots, up, up_other, own_rows)
    groups = [list(range(core, devices, CORES)) for core in range(CORES)]
    query = lax.all_to_all(query, "adapter", 0, 0, axis_index_groups=groups, tiled=True)
    return query.transpose(1, 0, 2).reshape(own_rows, devices * columns)


def solution(mesh):
    in_specs = (
        P(("group", "adapter"), None),
        P(),
        P(None, "adapter"),
        P("adapter", None, None),
        P(None, None, "adapter"),
        P(("group", "adapter"), None),
        P(),
    )
    out_specs = P(("group", "adapter"), None)
    return jax.shard_map(shards, mesh=mesh, in_specs=in_specs, out_specs=out_specs, check_vma=False)
```

```python
import jax
import jax.numpy as jnp
from jax import lax
from jax.experimental import pallas as pl
from jax.experimental.pallas import tpu as pltpu
from jax.sharding import PartitionSpec as P

ADAPTER_SCALE = 0.5
EPS = 1e-05

SIDE = 2
CORES = 2
CORNERS = SIDE * CORES
LANES = 128
CHUNK = 1024
VMEM_LIMIT = 24 << 20
VMEM = pl.BlockSpec(memory_space=pltpu.VMEM)


def line_ring(places):
    odd = list(range(1, places, 2))
    even = list(range(0, places, 2))
    return [0] + odd + even[:0:-1]


def pairs(places, steps, flip):
    ring = line_ring(places)
    out = []
    for at, place in enumerate(ring):
        target = ring[(at + steps) % places]
        for corner in range(CORNERS):
            out.append((place * CORNERS + corner, target * CORNERS + (corner ^ flip)))
    return out


def split_pairs(places):
    flips, steps = pairs(places, 0, 2), pairs(places, 1, 0)
    return [pair for pair in flips if pair[0] % CORES == 0] + [
        pair for pair in steps if pair[0] % CORES
    ]


def ring_chip(places, steps, side):
    chip = lax.axis_index("adapter") // CORES
    ring = line_ring(places)
    target = jnp.int32(0)
    for at, name in enumerate(ring):
        target = jnp.where(chip // SIDE == name, jnp.int32(ring[(at + steps) % places]), target)
    return target * SIDE + ((chip % SIDE) ^ side)


def after(x, *others):
    return lax.optimization_barrier((x, *others))[0]


def call(kernel, out_shape, operands):
    return pl.pallas_call(
        kernel,
        out_shape=out_shape,
        in_specs=[VMEM] * len(operands),
        out_specs=jax.tree.map(lambda _: VMEM, out_shape),
        compiler_params=pltpu.CompilerParams(vmem_limit_bytes=VMEM_LIMIT),
        cost_estimate=pl.CostEstimate(flops=1, bytes_accessed=1, transcendentals=0),
    )(*operands)


def norm_kernel(*refs):
    sources, (out_ref, *buffers, sems) = refs[:4], refs[4:]
    copies = [
        pltpu.make_async_copy(source, buffer, sems.at[number])
        for number, (source, buffer) in enumerate(zip(sources, buffers))
    ]
    for copy in copies:
        copy.start()
    for copy in copies:
        copy.wait()
    hidden_ref, gain_ref, index_ref, slot_ref = buffers
    rows, width = hidden_ref.shape
    squares = jnp.zeros((rows, LANES), jnp.float32)
    for start in range(0, width, CHUNK):
        wide = hidden_ref[:, start : start + CHUNK].astype(jnp.float32)
        wide = wide * wide
        for lane in range(0, CHUNK, LANES):
            squares = squares + wide[:, lane : lane + LANES]
    inv_rms = lax.rsqrt(jnp.sum(squares, axis=1, keepdims=True) / width + EPS)
    for start in range(0, width, CHUNK):
        lanes = slice(start, start + CHUNK)
        wide = hidden_ref[:, lanes].astype(jnp.float32)
        out_ref[:, lanes] = (wide * inv_rms * gain_ref[:, lanes]).astype(jnp.bfloat16)
    index = index_ref[...]
    slot = jnp.zeros(index.shape, jnp.float32)
    for name in range(slot_ref.shape[1]):
        slot = jnp.where(index == name, slot_ref[0, name].astype(jnp.float32), slot)
    across = lax.broadcasted_iota(jnp.int32, (rows, rows), 1)
    down = lax.broadcasted_iota(jnp.int32, (rows, rows), 0)
    column = jnp.sum(jnp.where(across == down, slot, 0.0), axis=1, keepdims=True)
    out_ref[:, width:] = jnp.broadcast_to(column, (rows, LANES)).astype(jnp.bfloat16)


def normalize(hidden, norm_weight, adapter_index, adapter_slot):
    rows, width = hidden.shape
    sources = (
        hidden,
        norm_weight.reshape(1, width),
        adapter_index.reshape(1, rows),
        adapter_slot.reshape(1, -1),
    )
    spaces = (pltpu.VMEM, pltpu.VMEM, pltpu.VMEM, pltpu.SMEM)
    return pl.pallas_call(
        norm_kernel,
        out_shape=jax.ShapeDtypeStruct((rows, width + LANES), jnp.bfloat16),
        in_specs=[pl.BlockSpec(memory_space=pltpu.HBM)] * len(sources),
        out_specs=VMEM,
        scratch_shapes=[space(x.shape, x.dtype) for space, x in zip(spaces, sources)]
        + [pltpu.SemaphoreType.DMA((len(sources),))],
    )(*sources)


def stacked(blocks, lanes):
    wide = [block[:, lanes].astype(jnp.float32) for block in blocks]
    return jnp.concatenate(wide, axis=0).astype(jnp.bfloat16)


def shrink_kernel(count, *refs):
    blocks, (own_ref, other_ref, *before, part_ref, slot_ref, rows_ref) = refs[:count], refs[count:]
    rank, width = own_ref.shape
    rows = slot_ref.shape[0]
    part = jnp.zeros((rows, 2 * rank), jnp.float32)
    for start in range(0, width, CHUNK):
        lanes = slice(start, start + CHUNK)
        down = jnp.concatenate([own_ref[:, lanes], other_ref[:, lanes]], axis=0)
        chunk = stacked(blocks, lanes)
        rows_ref[:, lanes] = chunk
        part += lax.dot_general(
            chunk, down, (((1,), (1,)), ((), ())), preferred_element_type=jnp.float32
        )
    slot = jnp.concatenate(
        [block[:, width : width + 1].astype(jnp.float32) for block in blocks], axis=0
    ).astype(jnp.int32)
    slot_ref[...] = jnp.broadcast_to(slot, slot_ref.shape)
    me = lax.axis_index("adapter")
    lanes = lax.broadcasted_iota(jnp.int32, part.shape, 1)
    part = jnp.where(slot == jnp.where(lanes < rank, me, me ^ 1), part, 0.0)
    part = part[:, :rank] + part[:, rank:]
    first = 0
    for ref in before:
        part_ref[first : first + ref.shape[0], :] = ref[...]
        first += ref.shape[0]
    part_ref[first:, :] = part.astype(jnp.bfloat16)


def shrink_rows(blocks, own, other, before=()):
    rows = blocks[0].shape[0] * len(blocks)
    total = rows + sum(part.shape[0] for part in before)
    out_shape = (
        jax.ShapeDtypeStruct((total, own.shape[0]), jnp.bfloat16),
        jax.ShapeDtypeStruct((rows, LANES), jnp.int32),
        jax.ShapeDtypeStruct((rows, own.shape[1]), jnp.bfloat16),
    )
    return call(
        lambda *refs: shrink_kernel(len(blocks), *refs), out_shape, (*blocks, own, other, *before)
    )


def pack_kernel(own_rows, part_ref, across_ref, out_ref):
    rows, rank = part_ref.shape
    part = part_ref[...].astype(jnp.float32)
    across = across_ref[...].astype(jnp.float32)
    swapped = []
    for first in range(0, rows, SIDE * own_rows):
        middle, last = first + own_rows, first + SIDE * own_rows
        swapped += [across[middle:last], across[first:middle]]
    total = part + jnp.concatenate(swapped, axis=0)
    out_ref[...] = jnp.concatenate([total[: rows // 2], total[rows // 2 :]], axis=1).astype(jnp.bfloat16)


def pack(part, across, own_rows):
    rows, rank = part.shape
    out_shape = jax.ShapeDtypeStruct((rows // 2, 2 * rank), part.dtype)
    return call(lambda *refs: pack_kernel(own_rows, *refs), out_shape, (part, across))


def finish_kernel(places, rank, *refs):
    moved, refs = refs[:places], refs[places:]
    slot_count = len(refs) - places - 3
    bases, slots = refs[:places], refs[places : places + slot_count]
    own_ref, other_ref, out_ref = refs[places + slot_count :]
    depth, columns = own_ref.shape
    rows = SIDE * out_ref.shape[1]
    core = lax.axis_index("adapter") % CORES
    shrinks = []
    for step in range(places):
        shrink = jnp.zeros((rows, rank), jnp.float32)
        for back in range(places):
            half, first = divmod((step - back) % places, places // 2)
            part = moved[back][first * rows : (first + 1) * rows, half * rank : (half + 1) * rank]
            shrink += part.astype(jnp.float32)
        shrinks.append(shrink)
    shrink = jnp.concatenate(shrinks, axis=0)
    slot = jnp.concatenate([ref[:, 0:1] for ref in slots], axis=0)
    wide = jnp.concatenate([shrink] * (depth // rank), axis=1)
    lanes = lax.broadcasted_iota(jnp.int32, wide.shape, 1)
    spread = jnp.where(lanes // rank == slot, wide, 0.0).astype(jnp.bfloat16)
    for which, up_ref in enumerate((own_ref, other_ref)):
        update = jnp.dot(spread, up_ref[...], preferred_element_type=jnp.float32)
        at = pl.multiple_of((core ^ which) * columns, columns)
        for step in range(places):
            here = slice(step * rows, (step + 1) * rows)
            base = bases[step // 2 * 2 + which][step % 2 * rows : (step % 2 + 1) * rows, :]
            query = (base + ADAPTER_SCALE * update[here]).astype(jnp.bfloat16)
            for side in range(SIDE):
                chip = ring_chip(places, -step, side)
                out_ref[chip, :, pl.ds(at, columns)] = query[side * rows // SIDE : (side + 1) * rows // SIDE]


def finish(moved, bases, slots, own, other, own_rows):
    places, rank = len(moved), moved[0].shape[1] // 2
    return call(
        lambda *refs: finish_kernel(places, rank, *refs),
        jax.ShapeDtypeStruct((places * SIDE, own_rows, CORES * own.shape[1]), jnp.bfloat16),
        (*moved, *bases, *slots, own, other),
    )


def shards(
    hidden, norm_weight, query_weight, down_weights, up_weights, adapter_index, adapter_slot
):
    devices = lax.axis_size("adapter")
    me = lax.axis_index("adapter")
    places = devices // CORNERS
    own_rows, width = hidden.shape
    columns = query_weight.shape[1]
    rank = down_weights.shape[2]

    def move(x, steps, flip):
        return lax.ppermute(x, "adapter", pairs(places, steps, flip))

    def base_rows(rows, weight):
        return jnp.dot(rows, weight, preferred_element_type=jnp.float32)

    down = down_weights[0].T
    up = up_weights.reshape(devices * rank, columns)
    down_other = move(down, 0, 1)
    up_other = move(up, 0, 1)
    weight_other = move(query_weight, 0, 1)

    block, other = [normalize(hidden, norm_weight, adapter_index, adapter_slot)], []
    parts, slots, bases = [], [], []
    last = places - 1
    for step in range(last):
        block.append(move(block[step], 1, 0))
        other.append(move(after(block[step], *other[-1:]), 0, 2))
        if step % 2 == 0 and step:
            rows = [block[step - 2], other[step - 2], block[step - 1], other[step - 1]]
            rows = after(rows, block[step])
            part, slot, rows = shrink_rows(rows, down, down_other)
            parts.append(part)
            slots.append(slot)
            bases.append(base_rows(rows, query_weight))
            if step < last - 1:
                bases.append(base_rows(rows, weight_other))
    source = jnp.where((me & 1) == 0, after(block[last], *bases, other[-1]), other[-1])
    crossed = lax.ppermute(source, "adapter", split_pairs(places))
    bases.append(base_rows(after(rows, source), weight_other))
    crossed = after(crossed, *bases)
    rows = [block[last - 1], other[-1], block[last], crossed]
    part, slot, rows = shrink_rows(rows, down, down_other, parts)
    slots.append(slot)

    across = move(part, 0, 2)
    bases.append(base_rows(rows, query_weight))
    part = pack(part, after(across, bases[-1]), own_rows)
    moved = [part] + [move(part, steps, 0) for steps in range(1, places)]
    bases.append(base_rows(rows, weight_other))
    query = finish(moved, bases, slots, up, up_other, own_rows)
    groups = [list(range(core, devices, CORES)) for core in range(CORES)]
    query = lax.all_to_all(query, "adapter", 0, 0, axis_index_groups=groups, tiled=True)
    return query.transpose(1, 0, 2).reshape(own_rows, devices * columns)


def solution(mesh):
    in_specs = (
        P(("group", "adapter"), None),
        P(),
        P(None, "adapter"),
        P("adapter", None, None),
        P(None, None, "adapter"),
        P(("group", "adapter"), None),
        P(),
    )
    out_specs = P(("group", "adapter"), None)
    return jax.shard_map(shards, mesh=mesh, in_specs=in_specs, out_specs=out_specs, check_vma=False)
```

```python
import jax
import jax.numpy as jnp
from jax import lax
from jax.experimental import pallas as pl
from jax.experimental.pallas import tpu as pltpu
from jax.sharding import PartitionSpec as P

ADAPTER_SCALE = 0.5
EPS = 1e-05

SIDE = 2
CORES = 2
CORNERS = SIDE * CORES
LANES = 128
CHUNK = 1024
VMEM_LIMIT = 24 << 20
VMEM = pl.BlockSpec(memory_space=pltpu.VMEM)


def line_ring(places):
    odd = list(range(1, places, 2))
    even = list(range(0, places, 2))
    return [0] + odd + even[:0:-1]


def pairs(places, steps, flip):
    ring = line_ring(places)
    out = []
    for at, place in enumerate(ring):
        target = ring[(at + steps) % places]
        for corner in range(CORNERS):
            out.append((place * CORNERS + corner, target * CORNERS + (corner ^ flip)))
    return out


def split_pairs(places):
    flips, steps = pairs(places, 0, 2), pairs(places, 1, 0)
    return [pair for pair in flips if pair[0] % CORES == 0] + [
        pair for pair in steps if pair[0] % CORES
    ]


def ring_chip(places, steps, side):
    chip = lax.axis_index("adapter") // CORES
    ring = line_ring(places)
    target = jnp.int32(0)
    for at, name in enumerate(ring):
        target = jnp.where(chip // SIDE == name, jnp.int32(ring[(at + steps) % places]), target)
    return target * SIDE + ((chip % SIDE) ^ side)


def after(x, *others):
    return lax.optimization_barrier((x, *others))[0]


def call(kernel, out_shape, operands):
    return pl.pallas_call(
        kernel,
        out_shape=out_shape,
        in_specs=[VMEM] * len(operands),
        out_specs=jax.tree.map(lambda _: VMEM, out_shape),
        compiler_params=pltpu.CompilerParams(vmem_limit_bytes=VMEM_LIMIT),
        cost_estimate=pl.CostEstimate(flops=1, bytes_accessed=1, transcendentals=0),
    )(*operands)


def norm_kernel(*refs):
    sources, (out_ref, *buffers, sems) = refs[:4], refs[4:]
    copies = [
        pltpu.make_async_copy(source, buffer, sems.at[number])
        for number, (source, buffer) in enumerate(zip(sources, buffers))
    ]
    for copy in copies:
        copy.start()
    for copy in copies:
        copy.wait()
    hidden_ref, gain_ref, index_ref, slot_ref = buffers
    rows, width = hidden_ref.shape
    squares = jnp.zeros((rows, LANES), jnp.float32)
    for start in range(0, width, CHUNK):
        wide = hidden_ref[:, start : start + CHUNK].astype(jnp.float32)
        wide = wide * wide
        for lane in range(0, CHUNK, LANES):
            squares = squares + wide[:, lane : lane + LANES]
    inv_rms = lax.rsqrt(jnp.sum(squares, axis=1, keepdims=True) / width + EPS)
    for start in range(0, width, CHUNK):
        lanes = slice(start, start + CHUNK)
        wide = hidden_ref[:, lanes].astype(jnp.float32)
        out_ref[:, lanes] = (wide * inv_rms * gain_ref[:, lanes]).astype(jnp.bfloat16)
    index = index_ref[...]
    slot = jnp.zeros(index.shape, jnp.float32)
    for name in range(slot_ref.shape[1]):
        slot = jnp.where(index == name, slot_ref[0, name].astype(jnp.float32), slot)
    across = lax.broadcasted_iota(jnp.int32, (rows, rows), 1)
    down = lax.broadcasted_iota(jnp.int32, (rows, rows), 0)
    column = jnp.sum(jnp.where(across == down, slot, 0.0), axis=1, keepdims=True)
    out_ref[:, width:] = jnp.broadcast_to(column, (rows, LANES)).astype(jnp.bfloat16)


def normalize(hidden, norm_weight, adapter_index, adapter_slot):
    rows, width = hidden.shape
    sources = (
        hidden,
        norm_weight.reshape(1, width),
        adapter_index.reshape(1, rows),
        adapter_slot.reshape(1, -1),
    )
    spaces = (pltpu.VMEM, pltpu.VMEM, pltpu.VMEM, pltpu.SMEM)
    return pl.pallas_call(
        norm_kernel,
        out_shape=jax.ShapeDtypeStruct((rows, width + LANES), jnp.bfloat16),
        in_specs=[pl.BlockSpec(memory_space=pltpu.HBM)] * len(sources),
        out_specs=VMEM,
        scratch_shapes=[space(x.shape, x.dtype) for space, x in zip(spaces, sources)]
        + [pltpu.SemaphoreType.DMA((len(sources),))],
    )(*sources)


def stacked(blocks, lanes):
    wide = [block[:, lanes].astype(jnp.float32) for block in blocks]
    return jnp.concatenate(wide, axis=0).astype(jnp.bfloat16)


def shrink_kernel(count, *refs):
    blocks, (own_ref, other_ref, *before, part_ref, slot_ref, rows_ref) = refs[:count], refs[count:]
    rank, width = own_ref.shape
    rows = slot_ref.shape[0]
    part = jnp.zeros((rows, 2 * rank), jnp.float32)
    for start in range(0, width, CHUNK):
        lanes = slice(start, start + CHUNK)
        down = jnp.concatenate([own_ref[:, lanes], other_ref[:, lanes]], axis=0)
        chunk = stacked(blocks, lanes)
        rows_ref[:, lanes] = chunk
        part += lax.dot_general(
            chunk, down, (((1,), (1,)), ((), ())), preferred_element_type=jnp.float32
        )
    slot = jnp.concatenate(
        [block[:, width : width + 1].astype(jnp.float32) for block in blocks], axis=0
    ).astype(jnp.int32)
    slot_ref[...] = jnp.broadcast_to(slot, slot_ref.shape)
    me = lax.axis_index("adapter")
    lanes = lax.broadcasted_iota(jnp.int32, part.shape, 1)
    part = jnp.where(slot == jnp.where(lanes < rank, me, me ^ 1), part, 0.0)
    part = part[:, :rank] + part[:, rank:]
    first = 0
    for ref in before:
        part_ref[first : first + ref.shape[0], :] = ref[...]
        first += ref.shape[0]
    part_ref[first:, :] = part.astype(jnp.bfloat16)


def shrink_rows(blocks, own, other, before=(), tokens=()):
    rows = blocks[0].shape[0] * len(blocks)
    total = rows + sum(part.shape[0] for part in before)
    out_shape = (
        jax.ShapeDtypeStruct((total, own.shape[0]), jnp.bfloat16),
        jax.ShapeDtypeStruct((rows, LANES), jnp.int32),
        jax.ShapeDtypeStruct((rows, own.shape[1]), jnp.bfloat16),
    )
    return call(
        lambda *refs: shrink_kernel(len(blocks), *refs[len(tokens) :]),
        out_shape,
        (*tokens, *blocks, own, other, *before),
    )


def pack_kernel(own_rows, part_ref, across_ref, out_ref):
    rows, rank = part_ref.shape
    part = part_ref[...].astype(jnp.float32)
    across = across_ref[...].astype(jnp.float32)
    swapped = []
    for first in range(0, rows, SIDE * own_rows):
        middle, last = first + own_rows, first + SIDE * own_rows
        swapped += [across[middle:last], across[first:middle]]
    total = part + jnp.concatenate(swapped, axis=0)
    out_ref[...] = jnp.concatenate([total[: rows // 2], total[rows // 2 :]], axis=1).astype(jnp.bfloat16)


def pack(part, across, own_rows):
    rows, rank = part.shape
    out_shape = jax.ShapeDtypeStruct((rows // 2, 2 * rank), part.dtype)
    return call(lambda *refs: pack_kernel(own_rows, *refs), out_shape, (part, across))


def base_kernel(*refs):
    *blocks, weight_ref, out_ref, kept_ref, sems = refs
    width = weight_ref.shape[0]
    copies = []
    for number, start in enumerate(range(0, width, CHUNK)):
        rows = pl.ds(start, CHUNK)
        copies.append(
            pltpu.make_async_copy(weight_ref.at[rows], kept_ref.at[rows], sems.at[number])
        )
        copies[-1].start()
    out_ref[...] = jnp.zeros(out_ref.shape, jnp.float32)
    for number, start in enumerate(range(0, width, CHUNK)):
        lanes = slice(start, start + CHUNK)
        rows = stacked(blocks, lanes)
        copies[number].wait()
        out_ref[...] += jnp.dot(rows, kept_ref[lanes, :], preferred_element_type=jnp.float32)


def base_and_weight(blocks, weight):
    rows = blocks[0].shape[0] * len(blocks)
    return pl.pallas_call(
        base_kernel,
        out_shape=(
            jax.ShapeDtypeStruct((rows, weight.shape[1]), jnp.float32),
            jax.ShapeDtypeStruct(weight.shape, weight.dtype),
        ),
        in_specs=[VMEM] * len(blocks) + [pl.BlockSpec(memory_space=pltpu.HBM)],
        out_specs=(VMEM, VMEM),
        scratch_shapes=[pltpu.SemaphoreType.DMA((weight.shape[0] // CHUNK,))],
        compiler_params=pltpu.CompilerParams(vmem_limit_bytes=VMEM_LIMIT),
        cost_estimate=pl.CostEstimate(flops=1, bytes_accessed=1, transcendentals=0),
    )(*blocks, weight)


def token_kernel(block_ref, out_ref):
    out_ref[...] = jnp.zeros(out_ref.shape, out_ref.dtype)


def token(block):
    return pl.pallas_call(
        token_kernel,
        out_shape=jax.ShapeDtypeStruct((8, LANES), jnp.float32),
        in_specs=[pl.BlockSpec(memory_space=pl.ANY)],
        out_specs=VMEM,
        compiler_params=pltpu.CompilerParams(vmem_limit_bytes=VMEM_LIMIT),
        cost_estimate=pl.CostEstimate(flops=1000000, bytes_accessed=1, transcendentals=0),
    )(block)


def finish_kernel(places, rank, *refs):
    moved, refs = refs[:places], refs[places:]
    slot_count = len(refs) - places - 3
    bases, slots = refs[:places], refs[places : places + slot_count]
    own_ref, other_ref, out_ref = refs[places + slot_count :]
    depth, columns = own_ref.shape
    rows = SIDE * out_ref.shape[1]
    core = lax.axis_index("adapter") % CORES
    shrinks = []
    for step in range(places):
        shrink = jnp.zeros((rows, rank), jnp.float32)
        for back in range(places):
            half, first = divmod((step - back) % places, places // 2)
            part = moved[back][first * rows : (first + 1) * rows, half * rank : (half + 1) * rank]
            shrink += part.astype(jnp.float32)
        shrinks.append(shrink)
    shrink = jnp.concatenate(shrinks, axis=0)
    slot = jnp.concatenate([ref[:, 0:1] for ref in slots], axis=0)
    wide = jnp.concatenate([shrink] * (depth // rank), axis=1)
    lanes = lax.broadcasted_iota(jnp.int32, wide.shape, 1)
    spread = jnp.where(lanes // rank == slot, wide, 0.0).astype(jnp.bfloat16)
    for which, up_ref in enumerate((own_ref, other_ref)):
        update = jnp.dot(spread, up_ref[...], preferred_element_type=jnp.float32)
        at = pl.multiple_of((core ^ which) * columns, columns)
        for step in range(places):
            here = slice(step * rows, (step + 1) * rows)
            base = bases[step // 2 * 2 + which][step % 2 * rows : (step % 2 + 1) * rows, :]
            query = (base + ADAPTER_SCALE * update[here]).astype(jnp.bfloat16)
            for side in range(SIDE):
                chip = ring_chip(places, -step, side)
                out_ref[chip, :, pl.ds(at, columns)] = query[side * rows // SIDE : (side + 1) * rows // SIDE]


def finish(moved, bases, slots, own, other, own_rows):
    places, rank = len(moved), moved[0].shape[1] // 2
    return call(
        lambda *refs: finish_kernel(places, rank, *refs),
        jax.ShapeDtypeStruct((places * SIDE, own_rows, CORES * own.shape[1]), jnp.bfloat16),
        (*moved, *bases, *slots, own, other),
    )


def shards(
    hidden, norm_weight, query_weight, down_weights, up_weights, adapter_index, adapter_slot
):
    devices = lax.axis_size("adapter")
    me = lax.axis_index("adapter")
    places = devices // CORNERS
    own_rows, width = hidden.shape
    columns = query_weight.shape[1]
    rank = down_weights.shape[2]

    def move(x, steps, flip):
        return lax.ppermute(x, "adapter", pairs(places, steps, flip))

    def base_rows(rows, weight):
        return jnp.dot(rows, weight, preferred_element_type=jnp.float32)

    down = down_weights[0].T
    up = up_weights.reshape(devices * rank, columns)
    down_other = move(down, 0, 1)
    up_other = move(up, 0, 1)
    weight_other = move(query_weight, 0, 1)

    block, other = [normalize(hidden, norm_weight, adapter_index, adapter_slot)], []
    parts, slots, bases, tokens = [], [], [], []
    last = places - 1
    for step in range(last):
        if step:
            tokens.append(token(block[step]))
        block.append(move(after(block[step], *tokens[-1:]), 1, 0))
        other.append(move(after(block[step], *other[-1:]), 0, 2))
        if step % 2 == 0 and step:
            rows = [block[step - 2], other[step - 2], block[step - 1], other[step - 1]]
            blocks = after(rows, block[step])
            part, slot, rows = shrink_rows(blocks, down, down_other)
            parts.append(part)
            slots.append(slot)
            bases.append(base_rows(rows, query_weight))
            if step < last - 1:
                bases.append(base_rows(rows, weight_other))
    tokens.append(token(block[last]))
    source = jnp.where((me & 1) == 0, after(block[last], *bases, other[-1], tokens[-1]), other[-1])
    crossed = lax.ppermute(source, "adapter", split_pairs(places))
    base, weight_other = base_and_weight(after(blocks, source), weight_other)
    bases.append(base)
    crossed = after(crossed, *bases)
    rows = [block[last - 1], other[-1], block[last], crossed]
    part, slot, rows = shrink_rows(rows, down, down_other, parts, tokens)
    slots.append(slot)

    across = move(part, 0, 2)
    bases.append(base_rows(rows, query_weight))
    part = pack(part, after(across, bases[-1]), own_rows)
    moved = [part] + [move(part, steps, 0) for steps in range(1, places)]
    bases.append(base_rows(rows, weight_other))
    query = finish(moved, bases, slots, up, up_other, own_rows)
    groups = [list(range(core, devices, CORES)) for core in range(CORES)]
    query = lax.all_to_all(query, "adapter", 0, 0, axis_index_groups=groups, tiled=True)
    return query.transpose(1, 0, 2).reshape(own_rows, devices * columns)


def solution(mesh):
    in_specs = (
        P(("group", "adapter"), None),
        P(),
        P(None, "adapter"),
        P("adapter", None, None),
        P(None, None, "adapter"),
        P(("group", "adapter"), None),
        P(),
    )
    out_specs = P(("group", "adapter"), None)
    return jax.shard_map(shards, mesh=mesh, in_specs=in_specs, out_specs=out_specs, check_vma=False)
```

```python
import jax
import jax.numpy as jnp
from jax import lax
from jax.experimental import pallas as pl
from jax.experimental.pallas import tpu as pltpu
from jax.sharding import PartitionSpec as P

ADAPTER_SCALE = 0.5
EPS = 1e-05

SIDE = 2
CORES = 2
CORNERS = SIDE * CORES
LANES = 128
CHUNK = 1024
VMEM_LIMIT = 24 << 20
VMEM = pl.BlockSpec(memory_space=pltpu.VMEM)


def line_ring(places):
    odd = list(range(1, places, 2))
    even = list(range(0, places, 2))
    return [0] + odd + even[:0:-1]


def pairs(places, steps, flip):
    ring = line_ring(places)
    out = []
    for at, place in enumerate(ring):
        target = ring[(at + steps) % places]
        for corner in range(CORNERS):
            out.append((place * CORNERS + corner, target * CORNERS + (corner ^ flip)))
    return out


def split_pairs(places):
    flips, steps = pairs(places, 0, 2), pairs(places, 1, 0)
    return [pair for pair in flips if pair[0] % CORES] + [
        pair for pair in steps if pair[0] % CORES == 0
    ]


def ring_chip(places, steps, side):
    chip = lax.axis_index("adapter") // CORES
    ring = line_ring(places)
    target = jnp.int32(0)
    for at, name in enumerate(ring):
        target = jnp.where(chip // SIDE == name, jnp.int32(ring[(at + steps) % places]), target)
    return target * SIDE + ((chip % SIDE) ^ side)


def after(x, *others):
    return lax.optimization_barrier((x, *others))[0]


def call(kernel, out_shape, operands):
    return pl.pallas_call(
        kernel,
        out_shape=out_shape,
        in_specs=[VMEM] * len(operands),
        out_specs=jax.tree.map(lambda _: VMEM, out_shape),
        compiler_params=pltpu.CompilerParams(vmem_limit_bytes=VMEM_LIMIT),
        cost_estimate=pl.CostEstimate(flops=1, bytes_accessed=1, transcendentals=0),
    )(*operands)


def norm_kernel(*refs):
    sources, (out_ref, *buffers, sems) = refs[:4], refs[4:]
    copies = [
        pltpu.make_async_copy(source, buffer, sems.at[number])
        for number, (source, buffer) in enumerate(zip(sources, buffers))
    ]
    for copy in copies:
        copy.start()
    for copy in copies:
        copy.wait()
    hidden_ref, gain_ref, index_ref, slot_ref = buffers
    rows, width = hidden_ref.shape
    squares = jnp.zeros((rows, LANES), jnp.float32)
    for start in range(0, width, CHUNK):
        wide = hidden_ref[:, start : start + CHUNK].astype(jnp.float32)
        wide = wide * wide
        for lane in range(0, CHUNK, LANES):
            squares = squares + wide[:, lane : lane + LANES]
    inv_rms = lax.rsqrt(jnp.sum(squares, axis=1, keepdims=True) / width + EPS)
    for start in range(0, width, CHUNK):
        lanes = slice(start, start + CHUNK)
        wide = hidden_ref[:, lanes].astype(jnp.float32)
        out_ref[:, lanes] = (wide * inv_rms * gain_ref[:, lanes]).astype(jnp.bfloat16)
    index = index_ref[...]
    slot = jnp.zeros(index.shape, jnp.float32)
    for name in range(slot_ref.shape[1]):
        slot = jnp.where(index == name, slot_ref[0, name].astype(jnp.float32), slot)
    across = lax.broadcasted_iota(jnp.int32, (rows, rows), 1)
    down = lax.broadcasted_iota(jnp.int32, (rows, rows), 0)
    column = jnp.sum(jnp.where(across == down, slot, 0.0), axis=1, keepdims=True)
    out_ref[:, width:] = jnp.broadcast_to(column, (rows, LANES)).astype(jnp.bfloat16)


def normalize(hidden, norm_weight, adapter_index, adapter_slot):
    rows, width = hidden.shape
    sources = (
        hidden,
        norm_weight.reshape(1, width),
        adapter_index.reshape(1, rows),
        adapter_slot.reshape(1, -1),
    )
    spaces = (pltpu.VMEM, pltpu.VMEM, pltpu.VMEM, pltpu.SMEM)
    return pl.pallas_call(
        norm_kernel,
        out_shape=jax.ShapeDtypeStruct((rows, width + LANES), jnp.bfloat16),
        in_specs=[pl.BlockSpec(memory_space=pltpu.HBM)] * len(sources),
        out_specs=VMEM,
        scratch_shapes=[space(x.shape, x.dtype) for space, x in zip(spaces, sources)]
        + [pltpu.SemaphoreType.DMA((len(sources),))],
    )(*sources)


def stacked(blocks, lanes):
    wide = [block[:, lanes].astype(jnp.float32) for block in blocks]
    return jnp.concatenate(wide, axis=0).astype(jnp.bfloat16)


def shrink_kernel(count, *refs):
    blocks, (own_ref, other_ref, *before, part_ref, slot_ref, rows_ref) = refs[:count], refs[count:]
    rank, width = own_ref.shape
    rows = slot_ref.shape[0]
    part = jnp.zeros((rows, 2 * rank), jnp.float32)
    for start in range(0, width, CHUNK):
        lanes = slice(start, start + CHUNK)
        down = jnp.concatenate([own_ref[:, lanes], other_ref[:, lanes]], axis=0)
        chunk = stacked(blocks, lanes)
        rows_ref[:, lanes] = chunk
        part += lax.dot_general(
            chunk, down, (((1,), (1,)), ((), ())), preferred_element_type=jnp.float32
        )
    slot = jnp.concatenate(
        [block[:, width : width + 1].astype(jnp.float32) for block in blocks], axis=0
    ).astype(jnp.int32)
    slot_ref[...] = jnp.broadcast_to(slot, slot_ref.shape)
    me = lax.axis_index("adapter")
    lanes = lax.broadcasted_iota(jnp.int32, part.shape, 1)
    part = jnp.where(slot == jnp.where(lanes < rank, me, me ^ 1), part, 0.0)
    part = part[:, :rank] + part[:, rank:]
    first = 0
    for ref in before:
        part_ref[first : first + ref.shape[0], :] = ref[...]
        first += ref.shape[0]
    part_ref[first:, :] = part.astype(jnp.bfloat16)


def shrink_rows(blocks, own, other, before=(), tokens=()):
    rows = blocks[0].shape[0] * len(blocks)
    total = rows + sum(part.shape[0] for part in before)
    out_shape = (
        jax.ShapeDtypeStruct((total, own.shape[0]), jnp.bfloat16),
        jax.ShapeDtypeStruct((rows, LANES), jnp.int32),
        jax.ShapeDtypeStruct((rows, own.shape[1]), jnp.bfloat16),
    )
    return call(
        lambda *refs: shrink_kernel(len(blocks), *refs[len(tokens) :]),
        out_shape,
        (*tokens, *blocks, own, other, *before),
    )


def pack_kernel(own_rows, part_ref, across_ref, out_ref):
    rows, rank = part_ref.shape
    part = part_ref[...].astype(jnp.float32)
    across = across_ref[...].astype(jnp.float32)
    swapped = []
    for first in range(0, rows, SIDE * own_rows):
        middle, last = first + own_rows, first + SIDE * own_rows
        swapped += [across[middle:last], across[first:middle]]
    total = part + jnp.concatenate(swapped, axis=0)
    out_ref[...] = jnp.concatenate([total[: rows // 2], total[rows // 2 :]], axis=1).astype(jnp.bfloat16)


def pack(part, across, own_rows):
    rows, rank = part.shape
    out_shape = jax.ShapeDtypeStruct((rows // 2, 2 * rank), part.dtype)
    return call(lambda *refs: pack_kernel(own_rows, *refs), out_shape, (part, across))


def base_kernel(*refs):
    *blocks, weight_ref, out_ref, buffer, sems = refs
    width = weight_ref.shape[0]
    copies = []
    for number, start in enumerate(range(0, width, CHUNK)):
        here = pl.ds(start, CHUNK)
        copies.append(
            pltpu.make_async_copy(weight_ref.at[here], buffer.at[here], sems.at[number])
        )
        copies[-1].start()
    out_ref[...] = jnp.zeros(out_ref.shape, jnp.float32)
    for number, start in enumerate(range(0, width, CHUNK)):
        lanes = slice(start, start + CHUNK)
        rows = jnp.concatenate([block[:, lanes] for block in blocks], axis=0)
        copies[number].wait()
        out_ref[...] += jnp.dot(rows, buffer[lanes, :], preferred_element_type=jnp.float32)


def base_other(blocks, weight):
    rows = blocks[0].shape[0] * len(blocks)
    return pl.pallas_call(
        base_kernel,
        out_shape=jax.ShapeDtypeStruct((rows, weight.shape[1]), jnp.float32),
        in_specs=[VMEM] * len(blocks) + [pl.BlockSpec(memory_space=pltpu.HBM)],
        out_specs=VMEM,
        scratch_shapes=[
            pltpu.VMEM(weight.shape, weight.dtype),
            pltpu.SemaphoreType.DMA((weight.shape[0] // CHUNK,)),
        ],
        compiler_params=pltpu.CompilerParams(vmem_limit_bytes=VMEM_LIMIT),
        cost_estimate=pl.CostEstimate(flops=1, bytes_accessed=1, transcendentals=0),
    )(*blocks, weight)


def token_kernel(block_ref, out_ref):
    out_ref[...] = jnp.zeros(out_ref.shape, out_ref.dtype)


def token(block):
    return pl.pallas_call(
        token_kernel,
        out_shape=jax.ShapeDtypeStruct((8, LANES), jnp.float32),
        in_specs=[pl.BlockSpec(memory_space=pl.ANY)],
        out_specs=VMEM,
        compiler_params=pltpu.CompilerParams(vmem_limit_bytes=VMEM_LIMIT),
        cost_estimate=pl.CostEstimate(flops=1000000, bytes_accessed=1, transcendentals=0),
    )(block)


def finish_kernel(places, rank, *refs):
    moved, refs = refs[:places], refs[places:]
    bases, slots = refs[: places + 1], refs[places + 1 : 2 * places + 1]
    own_ref, other_ref, out_ref = refs[2 * places + 1 :]
    depth, columns = own_ref.shape
    rows = SIDE * out_ref.shape[1]
    core = lax.axis_index("adapter") % CORES
    shrinks = []
    for step in range(places):
        shrink = jnp.zeros((rows, rank), jnp.float32)
        for back in range(places):
            half, first = divmod((step - back) % places, places // 2)
            part = moved[back][first * rows : (first + 1) * rows, half * rank : (half + 1) * rank]
            shrink += part.astype(jnp.float32)
        shrinks.append(shrink)
    shrink = jnp.concatenate(shrinks, axis=0)
    slot = jnp.concatenate([ref[:, 0:1] for ref in slots], axis=0)
    wide = jnp.concatenate([shrink] * (depth // rank), axis=1)
    lanes = lax.broadcasted_iota(jnp.int32, wide.shape, 1)
    spread = jnp.where(lanes // rank == slot, wide, 0.0).astype(jnp.bfloat16)
    for which, up_ref in enumerate((own_ref, other_ref)):
        update = jnp.dot(spread, up_ref[...], preferred_element_type=jnp.float32)
        at = pl.multiple_of((core ^ which) * columns, columns)
        for step in range(places):
            here = slice(step * rows, (step + 1) * rows)
            base = bases[places][here, :] if which else bases[step][...]
            query = (base + ADAPTER_SCALE * update[here]).astype(jnp.bfloat16)
            for side in range(SIDE):
                chip = ring_chip(places, -step, side)
                out_ref[chip, :, pl.ds(at, columns)] = query[side * rows // SIDE : (side + 1) * rows // SIDE]


def finish(moved, bases, slots, own, other, own_rows):
    places, rank = len(moved), moved[0].shape[1] // 2
    return call(
        lambda *refs: finish_kernel(places, rank, *refs),
        jax.ShapeDtypeStruct((places * SIDE, own_rows, CORES * own.shape[1]), jnp.bfloat16),
        (*moved, *bases, *slots, own, other),
    )


def shards(
    hidden, norm_weight, query_weight, down_weights, up_weights, adapter_index, adapter_slot
):
    devices = lax.axis_size("adapter")
    me = lax.axis_index("adapter")
    places = devices // CORNERS
    own_rows, width = hidden.shape
    columns = query_weight.shape[1]
    rank = down_weights.shape[2]

    def move(x, steps, flip):
        return lax.ppermute(x, "adapter", pairs(places, steps, flip))

    def base_rows(rows, weight):
        return jnp.dot(rows, weight, preferred_element_type=jnp.float32)

    down = down_weights[0].T
    up = up_weights.reshape(devices * rank, columns)
    down_other = move(down, 0, 1)
    up_other = move(up, 0, 1)
    weight_other = move(query_weight, 0, 1)

    block, other = [normalize(hidden, norm_weight, adapter_index, adapter_slot)], []
    parts, slots, rows, bases, tokens = [], [], [], [], []
    last = places - 1

    def meet(blocks, before=()):
        part, slot, here = shrink_rows(blocks, down, down_other, before, tokens if before else ())
        parts.append(part)
        slots.append(slot)
        rows.append(here)

    for step in range(last):
        if step:
            block[step] = after(block[step], *bases[-1:])
            tokens.append(token(block[step]))
        block.append(move(after(block[step], *tokens[-1:]), 1, 0))
        other.append(move(after(block[step], *other[-1:]), 0, 2))
        if step:
            meet(after([block[step - 1], other[step - 1]], block[step]))
            bases.append(base_rows(rows[-1], query_weight))
    block[last] = after(block[last], bases[-1])
    tokens.append(token(block[last]))
    source = after(block[last], other[-1], tokens[-1])
    source = jnp.where((me & 1) == 1, source, other[-1])
    crossed = lax.ppermute(source, "adapter", split_pairs(places))
    meet(after([block[last - 1], other[-1]], source))
    bases.append(base_rows(rows[-1], query_weight))
    meet([block[last], after(crossed, bases[-1])], parts)

    across = move(parts[-1], 0, 2)
    bases.append(base_rows(rows[-1], query_weight))
    part = pack(parts[-1], after(across, bases[-1]), own_rows)
    moved = [part] + [move(part, steps, 0) for steps in range(1, places)]
    bases.append(base_other(rows, weight_other))
    query = finish(moved, bases, slots, up, up_other, own_rows)
    groups = [list(range(core, devices, CORES)) for core in range(CORES)]
    query = lax.all_to_all(query, "adapter", 0, 0, axis_index_groups=groups, tiled=True)
    return query.transpose(1, 0, 2).reshape(own_rows, devices * columns)


def solution(mesh):
    in_specs = (
        P(("group", "adapter"), None),
        P(),
        P(None, "adapter"),
        P("adapter", None, None),
        P(None, None, "adapter"),
        P(("group", "adapter"), None),
        P(),
    )
    out_specs = P(("group", "adapter"), None)
    return jax.shard_map(shards, mesh=mesh, in_specs=in_specs, out_specs=out_specs, check_vma=False)
```

```python
import jax
import jax.numpy as jnp
from jax import lax
from jax.experimental import pallas as pl
from jax.experimental.pallas import tpu as pltpu
from jax.sharding import PartitionSpec as P

ADAPTER_SCALE = 0.5
EPS = 1e-05

SIDE = 2
CORES = 2
CORNERS = SIDE * CORES
LANES = 128
CHUNK = 1024
VMEM_LIMIT = 24 << 20
VMEM = pl.BlockSpec(memory_space=pltpu.VMEM)


def line_ring(places):
    odd = list(range(1, places, 2))
    even = list(range(0, places, 2))
    return [0] + odd + even[:0:-1]


def pairs(places, steps, flip):
    ring = line_ring(places)
    out = []
    for at, place in enumerate(ring):
        target = ring[(at + steps) % places]
        for corner in range(CORNERS):
            out.append((place * CORNERS + corner, target * CORNERS + (corner ^ flip)))
    return out


def ring_chip(places, steps, side):
    chip = lax.axis_index("adapter") // CORES
    ring = line_ring(places)
    target = jnp.int32(0)
    for at, name in enumerate(ring):
        target = jnp.where(chip // SIDE == name, jnp.int32(ring[(at + steps) % places]), target)
    return target * SIDE + ((chip % SIDE) ^ side)


def after(x, *others):
    return lax.optimization_barrier((x, *others))[0]


def call(kernel, out_shape, operands):
    return pl.pallas_call(
        kernel,
        out_shape=out_shape,
        in_specs=[VMEM] * len(operands),
        out_specs=jax.tree.map(lambda _: VMEM, out_shape),
        compiler_params=pltpu.CompilerParams(vmem_limit_bytes=VMEM_LIMIT),
        cost_estimate=pl.CostEstimate(flops=1, bytes_accessed=1, transcendentals=0),
    )(*operands)


def norm_kernel(*refs):
    sources, (out_ref, *buffers, sems) = refs[:4], refs[4:]
    copies = [
        pltpu.make_async_copy(source, buffer, sems.at[number])
        for number, (source, buffer) in enumerate(zip(sources, buffers))
    ]
    for copy in copies:
        copy.start()
    for copy in copies:
        copy.wait()
    hidden_ref, gain_ref, index_ref, slot_ref = buffers
    rows, width = hidden_ref.shape
    squares = jnp.zeros((rows, LANES), jnp.float32)
    for start in range(0, width, CHUNK):
        wide = hidden_ref[:, start : start + CHUNK].astype(jnp.float32)
        wide = wide * wide
        for lane in range(0, CHUNK, LANES):
            squares = squares + wide[:, lane : lane + LANES]
    inv_rms = lax.rsqrt(jnp.sum(squares, axis=1, keepdims=True) / width + EPS)
    for start in range(0, width, CHUNK):
        lanes = slice(start, start + CHUNK)
        wide = hidden_ref[:, lanes].astype(jnp.float32)
        out_ref[:, lanes] = (wide * inv_rms * gain_ref[:, lanes]).astype(jnp.bfloat16)
    index = index_ref[...]
    slot = jnp.zeros(index.shape, jnp.float32)
    for name in range(slot_ref.shape[1]):
        slot = jnp.where(index == name, slot_ref[0, name].astype(jnp.float32), slot)
    across = lax.broadcasted_iota(jnp.int32, (rows, rows), 1)
    down = lax.broadcasted_iota(jnp.int32, (rows, rows), 0)
    column = jnp.sum(jnp.where(across == down, slot, 0.0), axis=1, keepdims=True)
    out_ref[:, width:] = jnp.broadcast_to(column, (rows, LANES)).astype(jnp.bfloat16)


def normalize(hidden, norm_weight, adapter_index, adapter_slot):
    rows, width = hidden.shape
    sources = (
        hidden,
        norm_weight.reshape(1, width),
        adapter_index.reshape(1, rows),
        adapter_slot.reshape(1, -1),
    )
    spaces = (pltpu.VMEM, pltpu.VMEM, pltpu.VMEM, pltpu.SMEM)
    return pl.pallas_call(
        norm_kernel,
        out_shape=jax.ShapeDtypeStruct((rows, width + LANES), jnp.bfloat16),
        in_specs=[pl.BlockSpec(memory_space=pltpu.HBM)] * len(sources),
        out_specs=VMEM,
        scratch_shapes=[space(x.shape, x.dtype) for space, x in zip(spaces, sources)]
        + [pltpu.SemaphoreType.DMA((len(sources),))],
    )(*sources)


def columns_of(pieces, start):
    for piece in pieces:
        if start < piece.shape[1]:
            return piece[:, start : start + CHUNK].astype(jnp.float32)
        start -= piece.shape[1]


def shrink_kernel(counts, halves, *refs):
    blocks, refs = [], list(refs)
    for count in counts:
        blocks.append(refs[:count])
        refs = refs[count:]
    own_ref, other_ref, *before, part_ref, slot_ref, rows_ref = refs
    rank, width = own_ref.shape
    rows = slot_ref.shape[0]
    part = jnp.zeros((rows, 2 * rank), jnp.float32)
    for start in range(0, width, CHUNK):
        lanes = slice(start, start + CHUNK)
        wide = [columns_of(block, start) for block in blocks]
        chunk = jnp.concatenate(wide, axis=0).astype(jnp.bfloat16)
        rows_ref[:, lanes] = chunk
        down = jnp.concatenate([own_ref[:, lanes], other_ref[:, lanes]], axis=0)
        part += lax.dot_general(
            chunk, down, (((1,), (1,)), ((), ())), preferred_element_type=jnp.float32
        )
    slot = [block[-1][:, block[-1].shape[1] - LANES :].astype(jnp.float32) for block in blocks]
    slot = jnp.concatenate(slot, axis=0)[:, 0:1].astype(jnp.int32)
    slot_ref[...] = jnp.broadcast_to(slot, slot_ref.shape)
    me = lax.axis_index("adapter")
    lanes = lax.broadcasted_iota(jnp.int32, part.shape, 1)
    part = jnp.where(slot == jnp.where(lanes < rank, me, me ^ 1), part, 0.0)
    part = part[:, :rank] + part[:, rank:]
    if halves:
        steps = [ref[...].astype(jnp.float32) for ref in before] + [part]
        middle = len(steps) // 2
        halves = [jnp.concatenate(steps[:middle], axis=0), jnp.concatenate(steps[middle:], axis=0)]
        part = jnp.concatenate(halves, axis=1)
    part_ref[...] = part.astype(jnp.bfloat16)


def shrink_rows(blocks, own, other, before=(), tokens=()):
    rows = blocks[0][0].shape[0] * len(blocks)
    rank, width = own.shape
    packed = (rows * (len(before) + 1) // 2, 2 * rank) if before else (rows, rank)
    out_shape = (
        jax.ShapeDtypeStruct(packed, jnp.bfloat16),
        jax.ShapeDtypeStruct((rows, LANES), jnp.int32),
        jax.ShapeDtypeStruct((rows, width), jnp.bfloat16),
    )
    counts = [len(block) for block in blocks]
    pieces = [piece for block in blocks for piece in block]
    return call(
        lambda *refs: shrink_kernel(counts, bool(before), *refs[len(tokens) :]),
        out_shape,
        (*tokens, *pieces, own, other, *before),
    )


def sum_kernel(places, *refs):
    *moved, out_ref = refs
    half, rank = moved[0].shape[0], moved[0].shape[1] // 2
    rows = half // (places // 2)
    for step in range(places):
        shrink = jnp.zeros((rows, rank), jnp.float32)
        for back in range(places):
            shrink += packed_step(moved[back], (step - back) % places, places)
        side, first = divmod(step, places // 2)
        out_ref[first * rows : (first + 1) * rows, side * rank : (side + 1) * rank] = shrink.astype(
            jnp.bfloat16
        )


def packed_step(ref, step, places):
    rank = ref.shape[1] // 2
    rows = ref.shape[0] // (places // 2)
    side, first = divmod(step, places // 2)
    return ref[first * rows : (first + 1) * rows, side * rank : (side + 1) * rank].astype(jnp.float32)


def cut_kernel(first, block_ref, out_ref):
    out_ref[...] = block_ref[:, first : first + out_ref.shape[1]]


def cut(block, first, last):
    return call(
        lambda *refs: cut_kernel(first, *refs),
        jax.ShapeDtypeStruct((block.shape[0], last - first), block.dtype),
        (block,),
    )


def base_kernel(*refs):
    *blocks, weight_ref, out_ref, kept_ref, sems = refs
    width = weight_ref.shape[0]
    copies = []
    for number, start in enumerate(range(0, width, CHUNK)):
        here = pl.ds(start, CHUNK)
        copies.append(
            pltpu.make_async_copy(weight_ref.at[here], kept_ref.at[here], sems.at[number])
        )
        copies[-1].start()
    out_ref[...] = jnp.zeros(out_ref.shape, jnp.float32)
    for number, start in enumerate(range(0, width, CHUNK)):
        lanes = slice(start, start + CHUNK)
        rows = jnp.concatenate([block[:, lanes] for block in blocks], axis=0)
        copies[number].wait()
        out_ref[...] += jnp.dot(rows, kept_ref[lanes, :], preferred_element_type=jnp.float32)


def base_and_weight(blocks, weight):
    rows = blocks[0].shape[0] * len(blocks)
    return pl.pallas_call(
        base_kernel,
        out_shape=(
            jax.ShapeDtypeStruct((rows, weight.shape[1]), jnp.float32),
            jax.ShapeDtypeStruct(weight.shape, weight.dtype),
        ),
        in_specs=[VMEM] * len(blocks) + [pl.BlockSpec(memory_space=pltpu.HBM)],
        out_specs=(VMEM, VMEM),
        scratch_shapes=[pltpu.SemaphoreType.DMA((weight.shape[0] // CHUNK,))],
        compiler_params=pltpu.CompilerParams(vmem_limit_bytes=VMEM_LIMIT),
        cost_estimate=pl.CostEstimate(flops=1, bytes_accessed=1, transcendentals=0),
    )(*blocks, weight)


def token_kernel(block_ref, out_ref):
    out_ref[...] = jnp.zeros(out_ref.shape, out_ref.dtype)


def token(block):
    return pl.pallas_call(
        token_kernel,
        out_shape=jax.ShapeDtypeStruct((8, LANES), jnp.float32),
        in_specs=[pl.BlockSpec(memory_space=pl.ANY)],
        out_specs=VMEM,
        compiler_params=pltpu.CompilerParams(vmem_limit_bytes=VMEM_LIMIT),
        cost_estimate=pl.CostEstimate(flops=1000000, bytes_accessed=1, transcendentals=0),
    )(block)


def finish_kernel(places, *refs):
    shrink_ref, across_ref, *refs = refs
    bases, slots = refs[: places + 2], refs[places + 2 : 2 * places + 2]
    own_ref, other_ref, out_ref = refs[2 * places + 2 :]
    depth, columns = own_ref.shape
    own_rows = out_ref.shape[1]
    rows = SIDE * own_rows
    core = lax.axis_index("adapter") % CORES
    shrinks = []
    for step in range(places):
        across = packed_step(across_ref, step, places)
        swapped = jnp.concatenate([across[own_rows:], across[:own_rows]], axis=0)
        shrinks.append(packed_step(shrink_ref, step, places) + swapped)
    shrink = jnp.concatenate(shrinks, axis=0)
    slot = jnp.concatenate([ref[:, 0:1] for ref in slots], axis=0)
    wide = jnp.concatenate([shrink] * (depth // shrink.shape[1]), axis=1)
    lanes = lax.broadcasted_iota(jnp.int32, wide.shape, 1)
    spread = jnp.where(lanes // shrink.shape[1] == slot, wide, 0.0).astype(jnp.bfloat16)
    for which, up_ref in enumerate((own_ref, other_ref)):
        update = jnp.dot(spread, up_ref[...], preferred_element_type=jnp.float32)
        at = pl.multiple_of((core ^ which) * columns, columns)
        for step in range(places):
            here = slice(step * rows, (step + 1) * rows)
            if which == 0:
                base = bases[step][...]
            elif step == places - 1:
                base = bases[places + 1][...]
            else:
                base = bases[places][here, :]
            query = (base + ADAPTER_SCALE * update[here]).astype(jnp.bfloat16)
            for side in range(SIDE):
                chip = ring_chip(places, -step, side)
                out_ref[chip, :, pl.ds(at, columns)] = query[side * own_rows : (side + 1) * own_rows]


def finish(shrink, across, bases, slots, own, other, own_rows):
    places = len(slots)
    return call(
        lambda *refs: finish_kernel(places, *refs),
        jax.ShapeDtypeStruct((places * SIDE, own_rows, CORES * own.shape[1]), jnp.bfloat16),
        (shrink, across, *bases, *slots, own, other),
    )


def shards(
    hidden, norm_weight, query_weight, down_weights, up_weights, adapter_index, adapter_slot
):
    devices = lax.axis_size("adapter")
    places = devices // CORNERS
    own_rows, width = hidden.shape
    half = width // 2
    columns = query_weight.shape[1]
    rank = down_weights.shape[2]

    def move(x, steps, flip):
        return lax.ppermute(x, "adapter", pairs(places, steps, flip))

    def base_rows(rows, weight):
        return jnp.dot(rows, weight, preferred_element_type=jnp.float32)

    down = down_weights[0].T
    up = up_weights.reshape(devices * rank, columns)
    down_other = move(down, 0, 1)
    up_other = move(up, 0, 1)
    weight_other = move(query_weight, 0, 1)

    block, other = [normalize(hidden, norm_weight, adapter_index, adapter_slot)], []
    parts, slots, rows, bases, tokens = [], [], [], [], []
    last = places - 1

    def meet(blocks, before=()):
        part, slot, here = shrink_rows(blocks, down, down_other, before, tokens if before else ())
        parts.append(part)
        slots.append(slot)
        rows.append(here)

    for step in range(last):
        if step:
            block[step] = after(block[step], *bases[-1:])
            tokens.append(token(block[step]))
        block.append(move(after(block[step], *tokens[-1:]), 1, 0))
        other.append(move(after(block[step], *other[-1:]), 0, 2))
        if step:
            meet(after([[block[step - 1]], [other[step - 1]]], block[step]))
            bases.append(base_rows(rows[-1], query_weight))
    block[last] = after(block[last], bases[-1])
    tokens.append(token(block[last]))
    low = move(cut(after(other[-1], tokens[-1]), 0, half), 1, 0)
    high = move(cut(after(block[last], tokens[-1]), half, block[last].shape[1]), 0, 2)
    meet(after([[block[last - 1]], [other[-1]]], block[last]))
    base, weight_other = base_and_weight(after(rows, block[last]), weight_other)
    low, high = after(low, base), after(high, base)
    meet([[block[last]], [low, high]], parts)

    part = parts[-1]
    moved = [part] + [move(part, steps, 0) for steps in range(1, places)]
    bases.append(base_rows(rows[-1], query_weight))
    moved = after(moved, bases[-1])
    shrink = call(
        lambda *refs: sum_kernel(places, *refs), jax.ShapeDtypeStruct(part.shape, part.dtype), moved
    )
    across = move(shrink, 0, 2)
    bases.insert(last - 1, base_rows(after(rows[last - 1], shrink), query_weight))
    bases += [base, base_rows(after(rows[-1], shrink), weight_other)]
    query = finish(shrink, across, bases, slots, up, up_other, own_rows)
    groups = [list(range(core, devices, CORES)) for core in range(CORES)]
    query = lax.all_to_all(query, "adapter", 0, 0, axis_index_groups=groups, tiled=True)
    return query.transpose(1, 0, 2).reshape(own_rows, devices * columns)


def solution(mesh):
    in_specs = (
        P(("group", "adapter"), None),
        P(),
        P(None, "adapter"),
        P("adapter", None, None),
        P(None, None, "adapter"),
        P(("group", "adapter"), None),
        P(),
    )
    out_specs = P(("group", "adapter"), None)
    return jax.shard_map(shards, mesh=mesh, in_specs=in_specs, out_specs=out_specs, check_vma=False)
```

```python
import jax
import jax.numpy as jnp
from jax import lax
from jax.experimental import pallas as pl
from jax.experimental.pallas import tpu as pltpu
from jax.sharding import PartitionSpec as P

ADAPTER_SCALE = 0.5
EPS = 1e-05

SIDE = 2
CORES = 2
CORNERS = SIDE * CORES
LANES = 128
CHUNK = 1024
VMEM_LIMIT = 24 << 20
VMEM = pl.BlockSpec(memory_space=pltpu.VMEM)


def line_ring(places):
    odd = list(range(1, places, 2))
    even = list(range(0, places, 2))
    return [0] + odd + even[:0:-1]


def pairs(places, steps, flip):
    ring = line_ring(places)
    out = []
    for at, place in enumerate(ring):
        target = ring[(at + steps) % places]
        for corner in range(CORNERS):
            out.append((place * CORNERS + corner, target * CORNERS + (corner ^ flip)))
    return out


def split_pairs(places):
    flips, steps = pairs(places, 0, 2), pairs(places, 1, 0)
    return [pair for pair in flips if pair[0] % CORES == 0] + [
        pair for pair in steps if pair[0] % CORES
    ]


def ring_chip(places, steps, side):
    chip = lax.axis_index("adapter") // CORES
    ring = line_ring(places)
    target = jnp.int32(0)
    for at, name in enumerate(ring):
        target = jnp.where(chip // SIDE == name, jnp.int32(ring[(at + steps) % places]), target)
    return target * SIDE + ((chip % SIDE) ^ side)


def after(x, *others):
    return lax.optimization_barrier((x, *others))[0]


def call(kernel, out_shape, operands):
    return pl.pallas_call(
        kernel,
        out_shape=out_shape,
        in_specs=[VMEM] * len(operands),
        out_specs=jax.tree.map(lambda _: VMEM, out_shape),
        compiler_params=pltpu.CompilerParams(vmem_limit_bytes=VMEM_LIMIT),
        cost_estimate=pl.CostEstimate(flops=1, bytes_accessed=1, transcendentals=0),
    )(*operands)


def norm_kernel(*refs):
    sources, (out_ref, *buffers, sems) = refs[:4], refs[4:]
    copies = [
        pltpu.make_async_copy(source, buffer, sems.at[number])
        for number, (source, buffer) in enumerate(zip(sources, buffers))
    ]
    for copy in copies:
        copy.start()
    for copy in copies:
        copy.wait()
    hidden_ref, gain_ref, index_ref, slot_ref = buffers
    rows, width = hidden_ref.shape
    squares = jnp.zeros((rows, LANES), jnp.float32)
    for start in range(0, width, CHUNK):
        wide = hidden_ref[:, start : start + CHUNK].astype(jnp.float32)
        wide = wide * wide
        for lane in range(0, CHUNK, LANES):
            squares = squares + wide[:, lane : lane + LANES]
    inv_rms = lax.rsqrt(jnp.sum(squares, axis=1, keepdims=True) / width + EPS)
    for start in range(0, width, CHUNK):
        lanes = slice(start, start + CHUNK)
        wide = hidden_ref[:, lanes].astype(jnp.float32)
        out_ref[:, lanes] = (wide * inv_rms * gain_ref[:, lanes]).astype(jnp.bfloat16)
    index = index_ref[...]
    slot = jnp.zeros(index.shape, jnp.float32)
    for name in range(slot_ref.shape[1]):
        slot = jnp.where(index == name, slot_ref[0, name].astype(jnp.float32), slot)
    across = lax.broadcasted_iota(jnp.int32, (rows, rows), 1)
    down = lax.broadcasted_iota(jnp.int32, (rows, rows), 0)
    column = jnp.sum(jnp.where(across == down, slot, 0.0), axis=1, keepdims=True)
    out_ref[:, width:] = jnp.broadcast_to(column, (rows, LANES)).astype(jnp.bfloat16)


def normalize(hidden, norm_weight, adapter_index, adapter_slot):
    rows, width = hidden.shape
    sources = (
        hidden,
        norm_weight.reshape(1, width),
        adapter_index.reshape(1, rows),
        adapter_slot.reshape(1, -1),
    )
    spaces = (pltpu.VMEM, pltpu.VMEM, pltpu.VMEM, pltpu.SMEM)
    return pl.pallas_call(
        norm_kernel,
        out_shape=jax.ShapeDtypeStruct((rows, width + LANES), jnp.bfloat16),
        in_specs=[pl.BlockSpec(memory_space=pltpu.HBM)] * len(sources),
        out_specs=VMEM,
        scratch_shapes=[space(x.shape, x.dtype) for space, x in zip(spaces, sources)]
        + [pltpu.SemaphoreType.DMA((len(sources),))],
    )(*sources)


def shrink_kernel(halves, *refs):
    blocks, (own_ref, other_ref, *before, part_ref, slot_ref, rows_ref) = refs[:SIDE], refs[SIDE:]
    rank, width = own_ref.shape
    rows = slot_ref.shape[0]
    part = jnp.zeros((rows, 2 * rank), jnp.float32)
    for start in range(0, width, CHUNK):
        lanes = slice(start, start + CHUNK)
        wide = [block[:, lanes].astype(jnp.float32) for block in blocks]
        chunk = jnp.concatenate(wide, axis=0).astype(jnp.bfloat16)
        rows_ref[:, lanes] = chunk
        down = jnp.concatenate([own_ref[:, lanes], other_ref[:, lanes]], axis=0)
        part += lax.dot_general(
            chunk, down, (((1,), (1,)), ((), ())), preferred_element_type=jnp.float32
        )
    slot = [block[:, width:].astype(jnp.float32) for block in blocks]
    slot = jnp.concatenate(slot, axis=0)[:, 0:1].astype(jnp.int32)
    slot_ref[...] = jnp.broadcast_to(slot, slot_ref.shape)
    me = lax.axis_index("adapter")
    lanes = lax.broadcasted_iota(jnp.int32, part.shape, 1)
    part = jnp.where(slot == jnp.where(lanes < rank, me, me ^ 1), part, 0.0)
    part = part[:, :rank] + part[:, rank:]
    if halves:
        steps = [ref[...].astype(jnp.float32) for ref in before] + [part]
        middle = len(steps) // 2
        halves = [jnp.concatenate(steps[:middle], axis=0), jnp.concatenate(steps[middle:], axis=0)]
        part = jnp.concatenate(halves, axis=1)
    part_ref[...] = part.astype(jnp.bfloat16)


def shrink_rows(blocks, own, other, before=(), tokens=()):
    rows = blocks[0].shape[0] * SIDE
    rank, width = own.shape
    packed = (rows * (len(before) + 1) // 2, 2 * rank) if before else (rows, rank)
    out_shape = (
        jax.ShapeDtypeStruct(packed, jnp.bfloat16),
        jax.ShapeDtypeStruct((rows, LANES), jnp.int32),
        jax.ShapeDtypeStruct((rows, width), jnp.bfloat16),
    )
    return call(
        lambda *refs: shrink_kernel(bool(before), *refs[len(tokens) :]),
        out_shape,
        (*tokens, *blocks, own, other, *before),
    )


def sum_kernel(places, *refs):
    *moved, out_ref = refs
    half, rank = moved[0].shape[0], moved[0].shape[1] // 2
    rows = half // (places // 2)
    for step in range(places):
        shrink = jnp.zeros((rows, rank), jnp.float32)
        for back in range(places):
            shrink += packed_step(moved[back], (step - back) % places, places)
        side, first = divmod(step, places // 2)
        out_ref[first * rows : (first + 1) * rows, side * rank : (side + 1) * rank] = shrink.astype(
            jnp.bfloat16
        )


def packed_step(ref, step, places):
    rank = ref.shape[1] // 2
    rows = ref.shape[0] // (places // 2)
    side, first = divmod(step, places // 2)
    return ref[first * rows : (first + 1) * rows, side * rank : (side + 1) * rank].astype(jnp.float32)


def base_kernel(*refs):
    *blocks, weight_ref, out_ref, kept_ref, sems = refs
    width = weight_ref.shape[0]
    copies = []
    for number, start in enumerate(range(0, width, CHUNK)):
        here = pl.ds(start, CHUNK)
        copies.append(
            pltpu.make_async_copy(weight_ref.at[here], kept_ref.at[here], sems.at[number])
        )
        copies[-1].start()
    out_ref[...] = jnp.zeros(out_ref.shape, jnp.float32)
    for number, start in enumerate(range(0, width, CHUNK)):
        lanes = slice(start, start + CHUNK)
        rows = jnp.concatenate([block[:, lanes] for block in blocks], axis=0)
        copies[number].wait()
        out_ref[...] += jnp.dot(rows, kept_ref[lanes, :], preferred_element_type=jnp.float32)


def base_and_weight(blocks, weight):
    rows = blocks[0].shape[0] * len(blocks)
    return pl.pallas_call(
        base_kernel,
        out_shape=(
            jax.ShapeDtypeStruct((rows, weight.shape[1]), jnp.float32),
            jax.ShapeDtypeStruct(weight.shape, weight.dtype),
        ),
        in_specs=[VMEM] * len(blocks) + [pl.BlockSpec(memory_space=pltpu.HBM)],
        out_specs=(VMEM, VMEM),
        scratch_shapes=[pltpu.SemaphoreType.DMA((weight.shape[0] // CHUNK,))],
        compiler_params=pltpu.CompilerParams(vmem_limit_bytes=VMEM_LIMIT),
        cost_estimate=pl.CostEstimate(flops=1, bytes_accessed=1, transcendentals=0),
    )(*blocks, weight)


def token_kernel(block_ref, out_ref):
    out_ref[...] = jnp.zeros(out_ref.shape, out_ref.dtype)


def token(block):
    return pl.pallas_call(
        token_kernel,
        out_shape=jax.ShapeDtypeStruct((8, LANES), jnp.float32),
        in_specs=[pl.BlockSpec(memory_space=pl.ANY)],
        out_specs=VMEM,
        compiler_params=pltpu.CompilerParams(vmem_limit_bytes=VMEM_LIMIT),
        cost_estimate=pl.CostEstimate(flops=1000000, bytes_accessed=1, transcendentals=0),
    )(block)


def finish_kernel(places, *refs):
    shrink_ref, across_ref, *refs = refs
    bases, slots = refs[: places + 3], refs[places + 3 : 2 * places + 3]
    own_ref, other_ref, out_ref = refs[2 * places + 3 :]
    depth, columns = own_ref.shape
    own_rows = out_ref.shape[1]
    rows = SIDE * own_rows
    core = lax.axis_index("adapter") % CORES
    shrinks = []
    for step in range(places):
        across = packed_step(across_ref, step, places)
        swapped = jnp.concatenate([across[own_rows:], across[:own_rows]], axis=0)
        shrinks.append(packed_step(shrink_ref, step, places) + swapped)
    shrink = jnp.concatenate(shrinks, axis=0)
    slot = jnp.concatenate([ref[:, 0:1] for ref in slots], axis=0)
    wide = jnp.concatenate([shrink] * (depth // shrink.shape[1]), axis=1)
    lanes = lax.broadcasted_iota(jnp.int32, wide.shape, 1)
    spread = jnp.where(lanes // shrink.shape[1] == slot, wide, 0.0).astype(jnp.bfloat16)
    for which, up_ref in enumerate((own_ref, other_ref)):
        update = jnp.dot(spread, up_ref[...], preferred_element_type=jnp.float32)
        at = pl.multiple_of((core ^ which) * columns, columns)
        for step in range(places):
            here = slice(step * rows, (step + 1) * rows)
            if which == 0:
                base = bases[step][...]
            elif step < places - 2:
                base = bases[places][here, :]
            else:
                base = bases[step + 3][...]
            query = (base + ADAPTER_SCALE * update[here]).astype(jnp.bfloat16)
            for side in range(SIDE):
                chip = ring_chip(places, -step, side)
                out_ref[chip, :, pl.ds(at, columns)] = query[side * own_rows : (side + 1) * own_rows]


def finish(shrink, across, bases, slots, own, other, own_rows):
    places = len(slots)
    return call(
        lambda *refs: finish_kernel(places, *refs),
        jax.ShapeDtypeStruct((places * SIDE, own_rows, CORES * own.shape[1]), jnp.bfloat16),
        (shrink, across, *bases, *slots, own, other),
    )


def shards(
    hidden, norm_weight, query_weight, down_weights, up_weights, adapter_index, adapter_slot
):
    devices = lax.axis_size("adapter")
    me = lax.axis_index("adapter")
    places = devices // CORNERS
    own_rows, width = hidden.shape
    columns = query_weight.shape[1]
    rank = down_weights.shape[2]

    def move(x, steps, flip):
        return lax.ppermute(x, "adapter", pairs(places, steps, flip))

    def base_rows(rows, weight):
        return jnp.dot(rows, weight, preferred_element_type=jnp.float32)

    down = down_weights[0].T
    up = up_weights.reshape(devices * rank, columns)
    down_other = move(down, 0, 1)
    up_other = move(up, 0, 1)
    weight_other = move(query_weight, 0, 1)

    block, other = [normalize(hidden, norm_weight, adapter_index, adapter_slot)], []
    parts, slots, rows, bases, tokens = [], [], [], [], []
    last = places - 1

    def meet(blocks, before=()):
        part, slot, here = shrink_rows(blocks, down, down_other, before, tokens if before else ())
        parts.append(part)
        slots.append(slot)
        rows.append(here)

    for step in range(last):
        if step:
            block[step] = after(block[step], *bases[-1:])
            tokens.append(token(block[step]))
        block.append(move(after(block[step], *tokens[-1:]), 1, 0))
        other.append(move(after(block[step], *other[-1:]), 0, 2))
        if step:
            meet(after([block[step - 1], other[step - 1]], block[step]))
            bases.append(base_rows(rows[-1], query_weight))
    base, weight_other = base_and_weight(after(rows, bases[-1]), weight_other)
    block[last] = after(block[last], base)
    tokens.append(token(block[last]))
    source = after(block[last], other[-1], tokens[-1])
    source = jnp.where((me & 1) == 0, source, other[-1])
    crossed = lax.ppermute(source, "adapter", split_pairs(places))
    meet(after([block[last - 1], other[-1]], source))
    bases.append(base_rows(rows[-1], query_weight))
    bases_other = [base, base_rows(rows[-1], weight_other)]
    meet([block[last], after(crossed, bases[-1], bases_other[-1])], parts)

    part = parts[-1]
    moved = [part] + [move(part, steps, 0) for steps in range(1, places)]
    bases.append(base_rows(rows[-1], query_weight))
    moved = after(moved, bases[-1])
    shrink = call(
        lambda *refs: sum_kernel(places, *refs), jax.ShapeDtypeStruct(part.shape, part.dtype), moved
    )
    across = move(shrink, 0, 2)
    bases_other.append(base_rows(after(rows[-1], shrink), weight_other))
    query = finish(shrink, across, bases + bases_other, slots, up, up_other, own_rows)
    groups = [list(range(core, devices, CORES)) for core in range(CORES)]
    query = lax.all_to_all(query, "adapter", 0, 0, axis_index_groups=groups, tiled=True)
    return query.transpose(1, 0, 2).reshape(own_rows, devices * columns)


def solution(mesh):
    in_specs = (
        P(("group", "adapter"), None),
        P(),
        P(None, "adapter"),
        P("adapter", None, None),
        P(None, None, "adapter"),
        P(("group", "adapter"), None),
        P(),
    )
    out_specs = P(("group", "adapter"), None)
    return jax.shard_map(shards, mesh=mesh, in_specs=in_specs, out_specs=out_specs, check_vma=False)
```

```python
import jax
import jax.numpy as jnp
from jax import lax
from jax.experimental import pallas as pl
from jax.experimental.pallas import tpu as pltpu
from jax.sharding import PartitionSpec as P

ADAPTER_SCALE = 0.5
EPS = 1e-05

SIDE = 2
CORES = 2
CORNERS = SIDE * CORES
LANES = 128
CHUNK = 1024
PIECES = 4
VMEM_LIMIT = 24 << 20
VMEM = pl.BlockSpec(memory_space=pltpu.VMEM)


def line_ring(places):
    odd = list(range(1, places, 2))
    even = list(range(0, places, 2))
    return [0] + odd + even[:0:-1]


def pairs(places, steps, flip):
    ring = line_ring(places)
    out = []
    for at, place in enumerate(ring):
        target = ring[(at + steps) % places]
        for corner in range(CORNERS):
            out.append((place * CORNERS + corner, target * CORNERS + (corner ^ flip)))
    return out


def split_pairs(places):
    flips, steps = pairs(places, 0, 2), pairs(places, 1, 0)
    return [pair for pair in flips if pair[0] % CORES == 0] + [
        pair for pair in steps if pair[0] % CORES
    ]


def ring_chip(places, steps, side):
    chip = lax.axis_index("adapter") // CORES
    ring = line_ring(places)
    target = jnp.int32(0)
    for at, name in enumerate(ring):
        target = jnp.where(chip // SIDE == name, jnp.int32(ring[(at + steps) % places]), target)
    return target * SIDE + ((chip % SIDE) ^ side)


def after(x, *others):
    return lax.optimization_barrier((x, *others))[0]


def call(kernel, out_shape, operands):
    return pl.pallas_call(
        kernel,
        out_shape=out_shape,
        in_specs=[VMEM] * len(operands),
        out_specs=jax.tree.map(lambda _: VMEM, out_shape),
        compiler_params=pltpu.CompilerParams(vmem_limit_bytes=VMEM_LIMIT),
        cost_estimate=pl.CostEstimate(flops=1, bytes_accessed=1, transcendentals=0),
    )(*operands)


def norm_kernel(*refs):
    sources, (out_ref, *buffers, sems) = refs[:4], refs[4:]
    copies = [
        pltpu.make_async_copy(source, buffer, sems.at[number])
        for number, (source, buffer) in enumerate(zip(sources, buffers))
    ]
    for copy in copies:
        copy.start()
    for copy in copies:
        copy.wait()
    hidden_ref, gain_ref, index_ref, slot_ref = buffers
    rows, width = hidden_ref.shape
    squares = jnp.zeros((rows, LANES), jnp.float32)
    for start in range(0, width, CHUNK):
        wide = hidden_ref[:, start : start + CHUNK].astype(jnp.float32)
        wide = wide * wide
        for lane in range(0, CHUNK, LANES):
            squares = squares + wide[:, lane : lane + LANES]
    inv_rms = lax.rsqrt(jnp.sum(squares, axis=1, keepdims=True) / width + EPS)
    for start in range(0, width, CHUNK):
        lanes = slice(start, start + CHUNK)
        wide = hidden_ref[:, lanes].astype(jnp.float32)
        out_ref[:, lanes] = (wide * inv_rms * gain_ref[:, lanes]).astype(jnp.bfloat16)
    index = index_ref[...]
    slot = jnp.zeros(index.shape, jnp.float32)
    for name in range(slot_ref.shape[1]):
        slot = jnp.where(index == name, slot_ref[0, name].astype(jnp.float32), slot)
    across = lax.broadcasted_iota(jnp.int32, (rows, rows), 1)
    down = lax.broadcasted_iota(jnp.int32, (rows, rows), 0)
    column = jnp.sum(jnp.where(across == down, slot, 0.0), axis=1, keepdims=True)
    out_ref[:, width:] = jnp.broadcast_to(column, (rows, LANES)).astype(jnp.bfloat16)


def normalize(hidden, norm_weight, adapter_index, adapter_slot):
    rows, width = hidden.shape
    sources = (
        hidden,
        norm_weight.reshape(1, width),
        adapter_index.reshape(1, rows),
        adapter_slot.reshape(1, -1),
    )
    spaces = (pltpu.VMEM, pltpu.VMEM, pltpu.VMEM, pltpu.SMEM)
    return pl.pallas_call(
        norm_kernel,
        out_shape=jax.ShapeDtypeStruct((rows, width + LANES), jnp.bfloat16),
        in_specs=[pl.BlockSpec(memory_space=pltpu.HBM)] * len(sources),
        out_specs=VMEM,
        scratch_shapes=[space(x.shape, x.dtype) for space, x in zip(spaces, sources)]
        + [pltpu.SemaphoreType.DMA((len(sources),))],
    )(*sources)


def shrink_kernel(halves, *refs):
    blocks, (own_ref, other_ref, *before, part_ref, slot_ref, rows_ref) = refs[:SIDE], refs[SIDE:]
    rank, width = own_ref.shape
    rows = slot_ref.shape[0]
    part = jnp.zeros((rows, 2 * rank), jnp.float32)
    for start in range(0, width, CHUNK):
        lanes = slice(start, start + CHUNK)
        wide = [block[:, lanes].astype(jnp.float32) for block in blocks]
        chunk = jnp.concatenate(wide, axis=0).astype(jnp.bfloat16)
        rows_ref[:, lanes] = chunk
        down = jnp.concatenate([own_ref[:, lanes], other_ref[:, lanes]], axis=0)
        part += lax.dot_general(
            chunk, down, (((1,), (1,)), ((), ())), preferred_element_type=jnp.float32
        )
    slot = [block[:, width:].astype(jnp.float32) for block in blocks]
    slot = jnp.concatenate(slot, axis=0)[:, 0:1].astype(jnp.int32)
    slot_ref[...] = jnp.broadcast_to(slot, slot_ref.shape)
    me = lax.axis_index("adapter")
    lanes = lax.broadcasted_iota(jnp.int32, part.shape, 1)
    part = jnp.where(slot == jnp.where(lanes < rank, me, me ^ 1), part, 0.0)
    part = part[:, :rank] + part[:, rank:]
    if halves:
        steps = [ref[...].astype(jnp.float32) for ref in before] + [part]
        middle = len(steps) // 2
        halves = [jnp.concatenate(steps[:middle], axis=0), jnp.concatenate(steps[middle:], axis=0)]
        part = jnp.concatenate(halves, axis=1)
    part_ref[...] = part.astype(jnp.bfloat16)


def shrink_rows(blocks, own, other, before=(), tokens=()):
    rows = blocks[0].shape[0] * SIDE
    rank, width = own.shape
    packed = (rows * (len(before) + 1) // 2, 2 * rank) if before else (rows, rank)
    out_shape = (
        jax.ShapeDtypeStruct(packed, jnp.bfloat16),
        jax.ShapeDtypeStruct((rows, LANES), jnp.int32),
        jax.ShapeDtypeStruct((rows, width), jnp.bfloat16),
    )
    return call(
        lambda *refs: shrink_kernel(bool(before), *refs[len(tokens) :]),
        out_shape,
        (*tokens, *blocks, own, other, *before),
    )


def sum_kernel(places, *refs):
    *moved, out_ref = refs
    half, rank = moved[0].shape[0], moved[0].shape[1] // 2
    rows = half // (places // 2)
    for step in range(places):
        shrink = jnp.zeros((rows, rank), jnp.float32)
        for back in range(places):
            shrink += packed_step(moved[back], (step - back) % places, places)
        side, first = divmod(step, places // 2)
        out_ref[first * rows : (first + 1) * rows, side * rank : (side + 1) * rank] = shrink.astype(
            jnp.bfloat16
        )


def packed_step(ref, step, places):
    rank = ref.shape[1] // 2
    rows = ref.shape[0] // (places // 2)
    side, first = divmod(step, places // 2)
    return ref[first * rows : (first + 1) * rows, side * rank : (side + 1) * rank].astype(jnp.float32)


def base_kernel(*refs):
    *blocks, weight_ref, out_ref, kept_ref, sems = refs
    width = weight_ref.shape[0]
    copies = []
    for number, start in enumerate(range(0, width, CHUNK)):
        here = pl.ds(start, CHUNK)
        copies.append(
            pltpu.make_async_copy(weight_ref.at[here], kept_ref.at[here], sems.at[number])
        )
        copies[-1].start()
    out_ref[...] = jnp.zeros(out_ref.shape, jnp.float32)
    for number, start in enumerate(range(0, width, CHUNK)):
        lanes = slice(start, start + CHUNK)
        rows = jnp.concatenate([block[:, lanes] for block in blocks], axis=0)
        copies[number].wait()
        out_ref[...] += jnp.dot(rows, kept_ref[lanes, :], preferred_element_type=jnp.float32)


def base_and_weight(blocks, weight):
    rows = blocks[0].shape[0] * len(blocks)
    return pl.pallas_call(
        base_kernel,
        out_shape=(
            jax.ShapeDtypeStruct((rows, weight.shape[1]), jnp.float32),
            jax.ShapeDtypeStruct(weight.shape, weight.dtype),
        ),
        in_specs=[VMEM] * len(blocks) + [pl.BlockSpec(memory_space=pltpu.HBM)],
        out_specs=(VMEM, VMEM),
        scratch_shapes=[pltpu.SemaphoreType.DMA((weight.shape[0] // CHUNK,))],
        compiler_params=pltpu.CompilerParams(vmem_limit_bytes=VMEM_LIMIT),
        cost_estimate=pl.CostEstimate(flops=1, bytes_accessed=1, transcendentals=0),
    )(*blocks, weight)


def load_kernel(*refs):
    *refs, sems = refs
    count = len(refs) // 2
    copies = []
    for number, (source, target) in enumerate(zip(refs[:count], refs[count:])):
        size = source.shape[0] // PIECES
        for piece in range(PIECES):
            here = pl.ds(piece * size, size)
            copies.append(
                pltpu.make_async_copy(source.at[here], target.at[here], sems.at[number, piece])
            )
    for copy in copies:
        copy.start()
    for copy in copies:
        copy.wait()


def load(*arrays):
    return pl.pallas_call(
        load_kernel,
        out_shape=[jax.ShapeDtypeStruct(x.shape, x.dtype) for x in arrays],
        in_specs=[pl.BlockSpec(memory_space=pltpu.HBM)] * len(arrays),
        out_specs=[VMEM] * len(arrays),
        scratch_shapes=[pltpu.SemaphoreType.DMA((len(arrays), PIECES))],
        compiler_params=pltpu.CompilerParams(vmem_limit_bytes=VMEM_LIMIT),
        cost_estimate=pl.CostEstimate(flops=1, bytes_accessed=1, transcendentals=0),
    )(*arrays)


def token_kernel(block_ref, out_ref):
    out_ref[...] = jnp.zeros(out_ref.shape, out_ref.dtype)


def token(block):
    return pl.pallas_call(
        token_kernel,
        out_shape=jax.ShapeDtypeStruct((8, LANES), jnp.float32),
        in_specs=[pl.BlockSpec(memory_space=pl.ANY)],
        out_specs=VMEM,
        compiler_params=pltpu.CompilerParams(vmem_limit_bytes=VMEM_LIMIT),
        cost_estimate=pl.CostEstimate(flops=1000000, bytes_accessed=1, transcendentals=0),
    )(block)


def finish_kernel(places, *refs):
    shrink_ref, across_ref, *refs = refs
    bases, slots = refs[: places + 3], refs[places + 3 : 2 * places + 3]
    own_ref, other_ref, out_ref = refs[2 * places + 3 :]
    depth, columns = own_ref.shape
    own_rows = out_ref.shape[1]
    rows = SIDE * own_rows
    core = lax.axis_index("adapter") % CORES
    shrinks = []
    for step in range(places):
        across = packed_step(across_ref, step, places)
        swapped = jnp.concatenate([across[own_rows:], across[:own_rows]], axis=0)
        shrinks.append(packed_step(shrink_ref, step, places) + swapped)
    shrink = jnp.concatenate(shrinks, axis=0)
    slot = jnp.concatenate([ref[:, 0:1] for ref in slots], axis=0)
    wide = jnp.concatenate([shrink] * (depth // shrink.shape[1]), axis=1)
    lanes = lax.broadcasted_iota(jnp.int32, wide.shape, 1)
    spread = jnp.where(lanes // shrink.shape[1] == slot, wide, 0.0).astype(jnp.bfloat16)
    for which, up_ref in enumerate((own_ref, other_ref)):
        update = jnp.dot(spread, up_ref[...], preferred_element_type=jnp.float32)
        at = pl.multiple_of((core ^ which) * columns, columns)
        for step in range(places):
            here = slice(step * rows, (step + 1) * rows)
            if which == 0:
                base = bases[step][...]
            elif step < places - 2:
                base = bases[places][here, :]
            else:
                base = bases[step + 3][...]
            query = (base + ADAPTER_SCALE * update[here]).astype(jnp.bfloat16)
            for side in range(SIDE):
                chip = ring_chip(places, -step, side)
                out_ref[chip, :, pl.ds(at, columns)] = query[side * own_rows : (side + 1) * own_rows]


def finish(shrink, across, bases, slots, own, other, own_rows):
    places = len(slots)
    return call(
        lambda *refs: finish_kernel(places, *refs),
        jax.ShapeDtypeStruct((places * SIDE, own_rows, CORES * own.shape[1]), jnp.bfloat16),
        (shrink, across, *bases, *slots, own, other),
    )


def shards(
    hidden, norm_weight, query_weight, down_weights, up_weights, adapter_index, adapter_slot
):
    devices = lax.axis_size("adapter")
    me = lax.axis_index("adapter")
    places = devices // CORNERS
    own_rows, width = hidden.shape
    columns = query_weight.shape[1]
    rank = down_weights.shape[2]

    def move(x, steps, flip):
        return lax.ppermute(x, "adapter", pairs(places, steps, flip))

    def base_rows(rows, weight):
        return jnp.dot(rows, weight, preferred_element_type=jnp.float32)

    down = down_weights[0].T
    up = up_weights.reshape(devices * rank, columns)
    down_other = move(down, 0, 1)
    up_other = move(up, 0, 1)
    weight_other = move(query_weight, 0, 1)

    block, other = [normalize(hidden, norm_weight, adapter_index, adapter_slot)], []
    parts, slots, rows, bases, tokens = [], [], [], [], []
    last = places - 1
    query_weight, down = load(*after([query_weight, down], block[0]))

    def meet(blocks, before=()):
        part, slot, here = shrink_rows(blocks, down, down_other, before, tokens if before else ())
        parts.append(part)
        slots.append(slot)
        rows.append(here)

    for step in range(last):
        if step:
            block[step] = after(block[step], *(bases[-1:] or [query_weight]))
            tokens.append(token(block[step]))
        block.append(move(after(block[step], *tokens[-1:]), 1, 0))
        other.append(move(after(block[step], *other[-1:]), 0, 2))
        if step:
            meet(after([block[step - 1], other[step - 1]], block[step]))
            bases.append(base_rows(rows[-1], query_weight))
    base, weight_other = base_and_weight(after(rows, bases[-1]), weight_other)
    block[last] = after(block[last], base)
    tokens.append(token(block[last]))
    source = after(block[last], other[-1], tokens[-1])
    source = jnp.where((me & 1) == 0, source, other[-1])
    crossed = lax.ppermute(source, "adapter", split_pairs(places))
    meet(after([block[last - 1], other[-1]], source))
    bases.append(base_rows(rows[-1], query_weight))
    bases_other = [base, base_rows(rows[-1], weight_other)]
    meet([block[last], after(crossed, bases[-1], bases_other[-1])], parts)

    part = parts[-1]
    moved = [part] + [move(part, steps, 0) for steps in range(1, places)]
    bases.append(base_rows(rows[-1], query_weight))
    moved = after(moved, bases[-1])
    shrink = call(
        lambda *refs: sum_kernel(places, *refs), jax.ShapeDtypeStruct(part.shape, part.dtype), moved
    )
    across = move(shrink, 0, 2)
    bases_other.append(base_rows(after(rows[-1], shrink), weight_other))
    query = finish(shrink, across, bases + bases_other, slots, up, up_other, own_rows)
    groups = [list(range(core, devices, CORES)) for core in range(CORES)]
    query = lax.all_to_all(query, "adapter", 0, 0, axis_index_groups=groups, tiled=True)
    return query.transpose(1, 0, 2).reshape(own_rows, devices * columns)


def solution(mesh):
    in_specs = (
        P(("group", "adapter"), None),
        P(),
        P(None, "adapter"),
        P("adapter", None, None),
        P(None, None, "adapter"),
        P(("group", "adapter"), None),
        P(),
    )
    out_specs = P(("group", "adapter"), None)
    return jax.shard_map(shards, mesh=mesh, in_specs=in_specs, out_specs=out_specs, check_vma=False)
```

```python
import jax
import jax.numpy as jnp
from jax import lax
from jax.experimental import pallas as pl
from jax.experimental.pallas import tpu as pltpu
from jax.sharding import PartitionSpec as P

ADAPTER_SCALE = 0.5
EPS = 1e-05

SIDE = 2
CORES = 2
CORNERS = SIDE * CORES
LANES = 128
CHUNK = 1024
VMEM_LIMIT = 24 << 20
VMEM = pl.BlockSpec(memory_space=pltpu.VMEM)


def line_ring(places):
    odd = list(range(1, places, 2))
    even = list(range(0, places, 2))
    return [0] + odd + even[:0:-1]


def pairs(places, steps, flip):
    ring = line_ring(places)
    out = []
    for at, place in enumerate(ring):
        target = ring[(at + steps) % places]
        for corner in range(CORNERS):
            out.append((place * CORNERS + corner, target * CORNERS + (corner ^ flip)))
    return out


def split_pairs(places):
    flips, steps = pairs(places, 0, 2), pairs(places, 1, 0)
    return [pair for pair in flips if pair[0] % CORES == 0] + [
        pair for pair in steps if pair[0] % CORES
    ]


def ring_chip(places, steps, side):
    chip = lax.axis_index("adapter") // CORES
    ring = line_ring(places)
    target = jnp.int32(0)
    for at, name in enumerate(ring):
        target = jnp.where(chip // SIDE == name, jnp.int32(ring[(at + steps) % places]), target)
    return target * SIDE + ((chip % SIDE) ^ side)


def after(x, *others):
    return lax.optimization_barrier((x, *others))[0]


def call(kernel, out_shape, operands):
    return pl.pallas_call(
        kernel,
        out_shape=out_shape,
        in_specs=[VMEM] * len(operands),
        out_specs=jax.tree.map(lambda _: VMEM, out_shape),
        compiler_params=pltpu.CompilerParams(vmem_limit_bytes=VMEM_LIMIT),
        cost_estimate=pl.CostEstimate(flops=1, bytes_accessed=1, transcendentals=0),
    )(*operands)


def slots_kernel(index_hbm, slot_hbm, out_ref, index_ref, slot_ref, sems):
    copies = [
        pltpu.make_async_copy(index_hbm, index_ref, sems.at[0]),
        pltpu.make_async_copy(slot_hbm, slot_ref, sems.at[1]),
    ]
    for copy in copies:
        copy.start()
    for copy in copies:
        copy.wait()
    index = index_ref[...]
    slot = jnp.zeros(index.shape, jnp.float32)
    for name in range(slot_ref.shape[1]):
        slot = jnp.where(index == name, slot_ref[0, name].astype(jnp.float32), slot)
    out_ref[...] = jnp.zeros(out_ref.shape, jnp.float32)
    out_ref[0:1, 0 : index.shape[1]] = slot


def own_slots(adapter_index, adapter_slot, places):
    sources = (adapter_index.reshape(1, -1), adapter_slot.reshape(1, -1))
    return pl.pallas_call(
        slots_kernel,
        out_shape=jax.ShapeDtypeStruct((-(-places // 8) * 8, LANES), jnp.float32),
        in_specs=[pl.BlockSpec(memory_space=pltpu.HBM)] * 2,
        out_specs=VMEM,
        scratch_shapes=[
            pltpu.VMEM(sources[0].shape, sources[0].dtype),
            pltpu.SMEM(sources[1].shape, sources[1].dtype),
            pltpu.SemaphoreType.DMA((2,)),
        ],
    )(*sources)


def merge_kernel(count, near_ref, far_ref, out_ref):
    out_ref[...] = near_ref[...]
    out_ref[count : 2 * count, :] = far_ref[0:count, :]


def merge(near, far, count):
    out_shape = jax.ShapeDtypeStruct(near.shape, near.dtype)
    return call(lambda *refs: merge_kernel(count, *refs), out_shape, (near, far))


def slot_column(step, near_ref, across_ref, own_rows):
    across = lax.broadcasted_iota(jnp.int32, (own_rows, LANES), 1)
    down = lax.broadcasted_iota(jnp.int32, (own_rows, LANES), 0)
    column = [
        jnp.sum(jnp.where(across == down, ref[step : step + 1, :], 0.0), axis=1, keepdims=True)
        for ref in (near_ref, across_ref)
    ]
    return jnp.concatenate(column, axis=0).astype(jnp.int32)


def inverse_rms(block):
    rows, width = block.shape
    squares = jnp.zeros((rows, LANES), jnp.float32)
    for start in range(0, width, CHUNK):
        wide = block[:, start : start + CHUNK].astype(jnp.float32)
        wide = wide * wide
        for lane in range(0, CHUNK, LANES):
            squares = squares + wide[:, lane : lane + LANES]
    return lax.rsqrt(jnp.sum(squares, axis=1, keepdims=True) / width + EPS)


def normalized(blocks, inverse, gain_ref, lanes):
    gain = gain_ref[:, lanes]
    wide = [block[:, lanes].astype(jnp.float32) * inv * gain for block, inv in zip(blocks, inverse)]
    return jnp.concatenate(wide, axis=0).astype(jnp.bfloat16)


def norm_kernel(*refs):
    *blocks, gain_ref, rows_ref = refs
    inverse = [inverse_rms(block) for block in blocks]
    for start in range(0, rows_ref.shape[1], CHUNK):
        lanes = slice(start, start + CHUNK)
        rows_ref[:, lanes] = normalized(blocks, inverse, gain_ref, lanes)


def norm_rows(blocks, gain):
    rows, width = blocks[0].shape
    out_shape = jax.ShapeDtypeStruct((rows * len(blocks), width), jnp.bfloat16)
    return call(norm_kernel, out_shape, (*blocks, gain))


def held(part, slot):
    rank = part.shape[1] // 2
    me = lax.axis_index("adapter")
    lanes = lax.broadcasted_iota(jnp.int32, part.shape, 1)
    part = jnp.where(slot == jnp.where(lanes < rank, me, me ^ 1), part, 0.0)
    return part[:, :rank] + part[:, rank:]


def down_chunk(own_ref, other_ref, lanes):
    return jnp.concatenate([own_ref[:, lanes], other_ref[:, lanes]], axis=0)


def times_down(rows, down):
    return lax.dot_general(rows, down, (((1,), (1,)), ((), ())), preferred_element_type=jnp.float32)


def shrink_kernel(*refs):
    *rows, own_ref, other_ref, near_ref, across_ref, part_ref = refs
    rank, width = own_ref.shape
    part = jnp.zeros((part_ref.shape[0], 2 * rank), jnp.float32)
    for start in range(0, width, CHUNK):
        lanes = slice(start, start + CHUNK)
        chunk = jnp.concatenate([ref[:, lanes] for ref in rows], axis=0)
        part += times_down(chunk, down_chunk(own_ref, other_ref, lanes))
    own_rows = rows[0].shape[0] // SIDE
    slot = [slot_column(step, near_ref, across_ref, own_rows) for step in range(len(rows))]
    part_ref[...] = held(part, jnp.concatenate(slot, axis=0)).astype(jnp.bfloat16)


def shrink_rows(rows, own, other, near, across):
    out_shape = jax.ShapeDtypeStruct((sum(x.shape[0] for x in rows), own.shape[0]), jnp.bfloat16)
    return call(shrink_kernel, out_shape, (*rows, own, other, near, across))


def last_kernel(*refs):
    block, crossed, gain_ref, rows_ref, own_ref, other_ref, before, near_ref, across_ref, *outs = refs
    part_ref, out_ref = outs[-2:]
    rank, width = own_ref.shape
    blocks = (block, crossed)
    inverse = [inverse_rms(block) for block in blocks]
    part = jnp.zeros((2 * out_ref.shape[0], 2 * rank), jnp.float32)
    for start in range(0, width, CHUNK):
        lanes = slice(start, start + CHUNK)
        here = normalized(blocks, inverse, gain_ref, lanes)
        out_ref[:, lanes] = here
        chunk = jnp.concatenate([rows_ref[:, lanes], here], axis=0)
        part += times_down(chunk, down_chunk(own_ref, other_ref, lanes))
    own_rows = block.shape[0]
    first = before.shape[0] // rows_ref.shape[0]
    slot = [slot_column(step, near_ref, across_ref, own_rows) for step in (first, first + 1)]
    part = held(part, jnp.concatenate(slot, axis=0))
    part = jnp.concatenate([before[...].astype(jnp.float32), part], axis=0)
    half = part.shape[0] // 2
    part_ref[...] = jnp.concatenate([part[:half], part[half:]], axis=1).astype(jnp.bfloat16)


def last_rows(blocks, gain, rows, own, other, before, near, across, tokens):
    rank, width = own.shape
    total = before.shape[0] + 2 * rows.shape[0]
    out_shape = (
        jax.ShapeDtypeStruct((total // 2, 2 * rank), jnp.bfloat16),
        jax.ShapeDtypeStruct(rows.shape, jnp.bfloat16),
    )
    operands = (*blocks, gain, rows, own, other, before, near, across, *tokens)
    return call(last_kernel, out_shape, operands)


def sum_kernel(places, *refs):
    *moved, out_ref = refs
    half, rank = moved[0].shape[0], moved[0].shape[1] // 2
    rows = half // (places // 2)
    for step in range(places):
        shrink = jnp.zeros((rows, rank), jnp.float32)
        for back in range(places):
            shrink += packed_step(moved[back], (step - back) % places, places)
        side, first = divmod(step, places // 2)
        out_ref[first * rows : (first + 1) * rows, side * rank : (side + 1) * rank] = shrink.astype(
            jnp.bfloat16
        )


def packed_step(ref, step, places):
    rank = ref.shape[1] // 2
    rows = ref.shape[0] // (places // 2)
    side, first = divmod(step, places // 2)
    return ref[first * rows : (first + 1) * rows, side * rank : (side + 1) * rank].astype(jnp.float32)


def base_kernel(*refs):
    *blocks, weight_ref, out_ref, kept_ref, sems = refs
    width = weight_ref.shape[0]
    copies = []
    for number, start in enumerate(range(0, width, CHUNK)):
        here = pl.ds(start, CHUNK)
        copies.append(
            pltpu.make_async_copy(weight_ref.at[here], kept_ref.at[here], sems.at[number])
        )
        copies[-1].start()
    out_ref[...] = jnp.zeros(out_ref.shape, jnp.float32)
    for number, start in enumerate(range(0, width, CHUNK)):
        lanes = slice(start, start + CHUNK)
        rows = jnp.concatenate([block[:, lanes] for block in blocks], axis=0)
        copies[number].wait()
        out_ref[...] += jnp.dot(rows, kept_ref[lanes, :], preferred_element_type=jnp.float32)


def base_and_weight(blocks, weight):
    rows = blocks[0].shape[0] * len(blocks)
    return pl.pallas_call(
        base_kernel,
        out_shape=(
            jax.ShapeDtypeStruct((rows, weight.shape[1]), jnp.float32),
            jax.ShapeDtypeStruct(weight.shape, weight.dtype),
        ),
        in_specs=[VMEM] * len(blocks) + [pl.BlockSpec(memory_space=pltpu.HBM)],
        out_specs=(VMEM, VMEM),
        scratch_shapes=[pltpu.SemaphoreType.DMA((weight.shape[0] // CHUNK,))],
        compiler_params=pltpu.CompilerParams(vmem_limit_bytes=VMEM_LIMIT),
        cost_estimate=pl.CostEstimate(flops=1, bytes_accessed=1, transcendentals=0),
    )(*blocks, weight)


def token_kernel(block_ref, out_ref):
    out_ref[...] = jnp.zeros(out_ref.shape, out_ref.dtype)


def token(block):
    return pl.pallas_call(
        token_kernel,
        out_shape=jax.ShapeDtypeStruct((8, LANES), jnp.float32),
        in_specs=[pl.BlockSpec(memory_space=pl.ANY)],
        out_specs=VMEM,
        compiler_params=pltpu.CompilerParams(vmem_limit_bytes=VMEM_LIMIT),
        cost_estimate=pl.CostEstimate(flops=1000000, bytes_accessed=1, transcendentals=0),
    )(block)


def finish_kernel(places, *refs):
    shrink_ref, across_ref, near_slots, across_slots, *bases, own_ref, other_ref, out_ref = refs
    depth, columns = own_ref.shape
    own_rows = out_ref.shape[1]
    rows = SIDE * own_rows
    core = lax.axis_index("adapter") % CORES
    shrinks = []
    for step in range(places):
        across = packed_step(across_ref, step, places)
        swapped = jnp.concatenate([across[own_rows:], across[:own_rows]], axis=0)
        shrinks.append(packed_step(shrink_ref, step, places) + swapped)
    shrink = jnp.concatenate(shrinks, axis=0)
    slot = [slot_column(step, near_slots, across_slots, own_rows) for step in range(places)]
    slot = jnp.concatenate(slot, axis=0)
    wide = jnp.concatenate([shrink] * (depth // shrink.shape[1]), axis=1)
    lanes = lax.broadcasted_iota(jnp.int32, wide.shape, 1)
    spread = jnp.where(lanes // shrink.shape[1] == slot, wide, 0.0).astype(jnp.bfloat16)
    for which, up_ref in enumerate((own_ref, other_ref)):
        update = jnp.dot(spread, up_ref[...], preferred_element_type=jnp.float32)
        at = pl.multiple_of((core ^ which) * columns, columns)
        for step in range(places):
            here = slice(step * rows, (step + 1) * rows)
            if which == 0:
                base = bases[step][...]
            elif step < places - 2:
                base = bases[places][here, :]
            else:
                base = bases[step + 3][...]
            query = (base + ADAPTER_SCALE * update[here]).astype(jnp.bfloat16)
            for side in range(SIDE):
                chip = ring_chip(places, -step, side)
                out_ref[chip, :, pl.ds(at, columns)] = query[side * own_rows : (side + 1) * own_rows]


def finish(places, shrink, across, slots, bases, own, other, own_rows):
    return call(
        lambda *refs: finish_kernel(places, *refs),
        jax.ShapeDtypeStruct((places * SIDE, own_rows, CORES * own.shape[1]), jnp.bfloat16),
        (shrink, across, *slots, *bases, own, other),
    )


def shards(
    hidden, norm_weight, query_weight, down_weights, up_weights, adapter_index, adapter_slot
):
    devices = lax.axis_size("adapter")
    me = lax.axis_index("adapter")
    places = devices // CORNERS
    own_rows, width = hidden.shape
    columns = query_weight.shape[1]
    rank = down_weights.shape[2]

    def move(x, steps, flip):
        return lax.ppermute(x, "adapter", pairs(places, steps, flip))

    def base_rows(rows, weight):
        return jnp.dot(rows, weight, preferred_element_type=jnp.float32)

    down = down_weights[0].T
    up = up_weights.reshape(devices * rank, columns)
    block, other = [hidden], []
    rows, bases, tokens = [], [], []
    gain = norm_weight.reshape(1, width)
    last = places - 1

    weight_other = move(query_weight, 0, 1)
    near, count = own_slots(adapter_index, adapter_slot, places), 1
    far = move(near, count, 0)

    for step in range(last):
        if step:
            block[step] = after(block[step], *bases[-1:])
            tokens.append(token(block[step]))
        block.append(move(after(block[step], *tokens[-1:]), 1, 0))
        other.append(move(after(block[step], *other[-1:]), 0, 2))
        if step:
            rows.append(norm_rows(after([block[step - 1], other[step - 1]], block[step]), gain))
            bases.append(base_rows(rows[-1], query_weight))
            if count < places:
                near, count = merge(near, after(far, block[step]), count), 2 * count
                far = move(near, count, 0) if count < places else None
    across_slots = move(near, 0, 2)
    up_other = move(after(up, bases[-1]), 0, 1)
    down_other = move(after(down, bases[0]), 0, 1)
    base, weight_other = base_and_weight(after(rows, bases[-1]), weight_other)
    block[last] = after(block[last], base)
    tokens.append(token(block[last]))
    source = after(block[last], other[-1], tokens[-1])
    source = jnp.where((me & 1) == 0, source, other[-1])
    crossed = lax.ppermute(source, "adapter", split_pairs(places))
    part = shrink_rows(after(rows, source), down, down_other, near, across_slots)
    rows.append(norm_rows(after([block[last - 1], other[-1]], source), gain))
    bases.append(base_rows(rows[-1], query_weight))
    bases_other = [base, base_rows(rows[-1], weight_other)]
    ends = [block[last], after(crossed, part, bases[-1], bases_other[-1])]
    part, here = last_rows(ends, gain, rows[-1], down, down_other, part, near, across_slots, tokens)
    rows.append(here)

    moved = [part] + [move(part, steps, 0) for steps in range(1, places)]
    bases.append(base_rows(rows[-1], query_weight))
    moved = after(moved, bases[-1])
    shrink = call(
        lambda *refs: sum_kernel(places, *refs), jax.ShapeDtypeStruct(part.shape, part.dtype), moved
    )
    across = move(shrink, 0, 2)
    bases_other.append(base_rows(after(rows[-1], shrink), weight_other))
    slots = (near, across_slots)
    query = finish(places, shrink, across, slots, bases + bases_other, up, up_other, own_rows)
    groups = [list(range(core, devices, CORES)) for core in range(CORES)]
    query = lax.all_to_all(query, "adapter", 0, 0, axis_index_groups=groups, tiled=True)
    return query.transpose(1, 0, 2).reshape(own_rows, devices * columns)


def solution(mesh):
    in_specs = (
        P(("group", "adapter"), None),
        P(),
        P(None, "adapter"),
        P("adapter", None, None),
        P(None, None, "adapter"),
        P(("group", "adapter"), None),
        P(),
    )
    out_specs = P(("group", "adapter"), None)
    return jax.shard_map(shards, mesh=mesh, in_specs=in_specs, out_specs=out_specs, check_vma=False)
```

```python
import jax
import jax.numpy as jnp
from jax import lax
from jax.experimental import pallas as pl
from jax.experimental.pallas import tpu as pltpu
from jax.sharding import PartitionSpec as P

ADAPTER_SCALE = 0.5
EPS = 1e-05

SIDE = 2
CORES = 2
CORNERS = SIDE * CORES
LANES = 128
CHUNK = 1024
VMEM_LIMIT = 24 << 20
VMEM = pl.BlockSpec(memory_space=pltpu.VMEM)


def line_ring(places):
    odd = list(range(1, places, 2))
    even = list(range(0, places, 2))
    return [0] + odd + even[:0:-1]


def pairs(places, steps, flip):
    ring = line_ring(places)
    out = []
    for at, place in enumerate(ring):
        target = ring[(at + steps) % places]
        for corner in range(CORNERS):
            out.append((place * CORNERS + corner, target * CORNERS + (corner ^ flip)))
    return out


def split_pairs(places):
    flips, steps = pairs(places, 0, 2), pairs(places, 1, 0)
    return [pair for pair in flips if pair[0] % CORES == 0] + [
        pair for pair in steps if pair[0] % CORES
    ]


def ring_chip(places, steps, side):
    chip = lax.axis_index("adapter") // CORES
    ring = line_ring(places)
    target = jnp.int32(0)
    for at, name in enumerate(ring):
        target = jnp.where(chip // SIDE == name, jnp.int32(ring[(at + steps) % places]), target)
    return target * SIDE + ((chip % SIDE) ^ side)


def after(x, *others):
    return lax.optimization_barrier((x, *others))[0]


def call(kernel, out_shape, operands):
    return pl.pallas_call(
        kernel,
        out_shape=out_shape,
        in_specs=[VMEM] * len(operands),
        out_specs=jax.tree.map(lambda _: VMEM, out_shape),
        compiler_params=pltpu.CompilerParams(vmem_limit_bytes=VMEM_LIMIT),
        cost_estimate=pl.CostEstimate(flops=1, bytes_accessed=1, transcendentals=0),
    )(*operands)


def slots_kernel(index_hbm, slot_hbm, out_ref, index_ref, slot_ref, sems):
    copies = [
        pltpu.make_async_copy(index_hbm, index_ref, sems.at[0]),
        pltpu.make_async_copy(slot_hbm, slot_ref, sems.at[1]),
    ]
    for copy in copies:
        copy.start()
    for copy in copies:
        copy.wait()
    index = index_ref[...]
    slot = jnp.zeros(index.shape, jnp.float32)
    for name in range(slot_ref.shape[1]):
        slot = jnp.where(index == name, slot_ref[0, name].astype(jnp.float32), slot)
    out_ref[...] = jnp.zeros(out_ref.shape, jnp.float32)
    out_ref[0:1, 0 : index.shape[1]] = slot


def own_slots(adapter_index, adapter_slot, places):
    sources = (adapter_index.reshape(1, -1), adapter_slot.reshape(1, -1))
    return pl.pallas_call(
        slots_kernel,
        out_shape=jax.ShapeDtypeStruct((-(-places // 8) * 8, LANES), jnp.float32),
        in_specs=[pl.BlockSpec(memory_space=pltpu.HBM)] * 2,
        out_specs=VMEM,
        scratch_shapes=[
            pltpu.VMEM(sources[0].shape, sources[0].dtype),
            pltpu.SMEM(sources[1].shape, sources[1].dtype),
            pltpu.SemaphoreType.DMA((2,)),
        ],
    )(*sources)


def merge_kernel(count, near_ref, far_ref, out_ref):
    out_ref[...] = near_ref[...]
    out_ref[count : 2 * count, :] = far_ref[0:count, :]


def merge(near, far, count):
    out_shape = jax.ShapeDtypeStruct(near.shape, near.dtype)
    return call(lambda *refs: merge_kernel(count, *refs), out_shape, (near, far))


def slot_column(step, near_ref, across_ref, own_rows):
    across = lax.broadcasted_iota(jnp.int32, (own_rows, LANES), 1)
    down = lax.broadcasted_iota(jnp.int32, (own_rows, LANES), 0)
    column = [
        jnp.sum(jnp.where(across == down, ref[step : step + 1, :], 0.0), axis=1, keepdims=True)
        for ref in (near_ref, across_ref)
    ]
    return jnp.concatenate(column, axis=0).astype(jnp.int32)


def inverse_rms(block):
    rows, width = block.shape
    squares = jnp.zeros((rows, LANES), jnp.float32)
    for start in range(0, width, CHUNK):
        wide = block[:, start : start + CHUNK].astype(jnp.float32)
        wide = wide * wide
        for lane in range(0, CHUNK, LANES):
            squares = squares + wide[:, lane : lane + LANES]
    return lax.rsqrt(jnp.sum(squares, axis=1, keepdims=True) / width + EPS)


def normalized(blocks, inverse, gain_ref, lanes):
    gain = gain_ref[:, lanes]
    wide = [block[:, lanes].astype(jnp.float32) * inv * gain for block, inv in zip(blocks, inverse)]
    return jnp.concatenate(wide, axis=0).astype(jnp.bfloat16)


def norm_kernel(*refs):
    *blocks, gain_ref, rows_ref = refs
    inverse = [inverse_rms(block) for block in blocks]
    for start in range(0, rows_ref.shape[1], CHUNK):
        lanes = slice(start, start + CHUNK)
        rows_ref[:, lanes] = normalized(blocks, inverse, gain_ref, lanes)


def norm_rows(blocks, gain):
    rows, width = blocks[0].shape
    out_shape = jax.ShapeDtypeStruct((rows * len(blocks), width), jnp.bfloat16)
    return call(norm_kernel, out_shape, (*blocks, gain))


def held(part, slot):
    rank = part.shape[1] // 2
    me = lax.axis_index("adapter")
    lanes = lax.broadcasted_iota(jnp.int32, part.shape, 1)
    part = jnp.where(slot == jnp.where(lanes < rank, me, me ^ 1), part, 0.0)
    return part[:, :rank] + part[:, rank:]


def down_chunk(own_ref, other_ref, lanes):
    return jnp.concatenate([own_ref[:, lanes], other_ref[:, lanes]], axis=0)


def times_down(rows, down):
    return lax.dot_general(rows, down, (((1,), (1,)), ((), ())), preferred_element_type=jnp.float32)


def shrink_kernel(*refs):
    *rows, own_ref, other_ref, near_ref, across_ref, part_ref = refs
    rank, width = own_ref.shape
    part = jnp.zeros((part_ref.shape[0], 2 * rank), jnp.float32)
    for start in range(0, width, CHUNK):
        lanes = slice(start, start + CHUNK)
        chunk = jnp.concatenate([ref[:, lanes] for ref in rows], axis=0)
        part += times_down(chunk, down_chunk(own_ref, other_ref, lanes))
    own_rows = rows[0].shape[0] // SIDE
    slot = [slot_column(step, near_ref, across_ref, own_rows) for step in range(len(rows))]
    part_ref[...] = held(part, jnp.concatenate(slot, axis=0)).astype(jnp.bfloat16)


def shrink_rows(rows, own, other, near, across):
    out_shape = jax.ShapeDtypeStruct((sum(x.shape[0] for x in rows), own.shape[0]), jnp.bfloat16)
    return call(shrink_kernel, out_shape, (*rows, own, other, near, across))


def last_kernel(*refs):
    block, crossed, gain_ref, rows_ref, own_ref, other_ref, before, near_ref, across_ref, *outs = refs
    part_ref, out_ref = outs[-2:]
    rank, width = own_ref.shape
    blocks = (block, crossed)
    inverse = [inverse_rms(block) for block in blocks]
    part = jnp.zeros((2 * out_ref.shape[0], 2 * rank), jnp.float32)
    for start in range(0, width, CHUNK):
        lanes = slice(start, start + CHUNK)
        here = normalized(blocks, inverse, gain_ref, lanes)
        out_ref[:, lanes] = here
        chunk = jnp.concatenate([rows_ref[:, lanes], here], axis=0)
        part += times_down(chunk, down_chunk(own_ref, other_ref, lanes))
    own_rows = block.shape[0]
    first = before.shape[0] // rows_ref.shape[0]
    slot = [slot_column(step, near_ref, across_ref, own_rows) for step in (first, first + 1)]
    part = held(part, jnp.concatenate(slot, axis=0))
    part = jnp.concatenate([before[...].astype(jnp.float32), part], axis=0)
    half = part.shape[0] // 2
    part_ref[...] = jnp.concatenate([part[:half], part[half:]], axis=1).astype(jnp.bfloat16)


def last_rows(blocks, gain, rows, own, other, before, near, across, tokens):
    rank, width = own.shape
    total = before.shape[0] + 2 * rows.shape[0]
    out_shape = (
        jax.ShapeDtypeStruct((total // 2, 2 * rank), jnp.bfloat16),
        jax.ShapeDtypeStruct(rows.shape, jnp.bfloat16),
    )
    operands = (*blocks, gain, rows, own, other, before, near, across, *tokens)
    return call(last_kernel, out_shape, operands)


def sum_kernel(places, *refs):
    *moved, out_ref = refs
    half, rank = moved[0].shape[0], moved[0].shape[1] // 2
    rows = half // (places // 2)
    for step in range(places):
        shrink = jnp.zeros((rows, rank), jnp.float32)
        for back in range(places):
            shrink += packed_step(moved[back], (step - back) % places, places)
        side, first = divmod(step, places // 2)
        out_ref[first * rows : (first + 1) * rows, side * rank : (side + 1) * rank] = shrink.astype(
            jnp.bfloat16
        )


def packed_step(ref, step, places):
    rank = ref.shape[1] // 2
    rows = ref.shape[0] // (places // 2)
    side, first = divmod(step, places // 2)
    return ref[first * rows : (first + 1) * rows, side * rank : (side + 1) * rank].astype(jnp.float32)


def base_kernel(*refs):
    *blocks, weight_ref, out_ref, kept_ref, sems = refs
    width = weight_ref.shape[0]
    copies = []
    for number, start in enumerate(range(0, width, CHUNK)):
        here = pl.ds(start, CHUNK)
        copies.append(
            pltpu.make_async_copy(weight_ref.at[here], kept_ref.at[here], sems.at[number])
        )
        copies[-1].start()
    out_ref[...] = jnp.zeros(out_ref.shape, jnp.float32)
    for number, start in enumerate(range(0, width, CHUNK)):
        lanes = slice(start, start + CHUNK)
        rows = jnp.concatenate([block[:, lanes] for block in blocks], axis=0)
        copies[number].wait()
        out_ref[...] += jnp.dot(rows, kept_ref[lanes, :], preferred_element_type=jnp.float32)


def base_and_weight(blocks, weight):
    rows = blocks[0].shape[0] * len(blocks)
    return pl.pallas_call(
        base_kernel,
        out_shape=(
            jax.ShapeDtypeStruct((rows, weight.shape[1]), jnp.float32),
            jax.ShapeDtypeStruct(weight.shape, weight.dtype),
        ),
        in_specs=[VMEM] * len(blocks) + [pl.BlockSpec(memory_space=pltpu.HBM)],
        out_specs=(VMEM, VMEM),
        scratch_shapes=[pltpu.SemaphoreType.DMA((weight.shape[0] // CHUNK,))],
        compiler_params=pltpu.CompilerParams(vmem_limit_bytes=VMEM_LIMIT),
        cost_estimate=pl.CostEstimate(flops=1, bytes_accessed=1, transcendentals=0),
    )(*blocks, weight)


def token_kernel(block_ref, out_ref):
    out_ref[...] = jnp.zeros(out_ref.shape, out_ref.dtype)


def token(block):
    return pl.pallas_call(
        token_kernel,
        out_shape=jax.ShapeDtypeStruct((8, LANES), jnp.float32),
        in_specs=[pl.BlockSpec(memory_space=pl.ANY)],
        out_specs=VMEM,
        compiler_params=pltpu.CompilerParams(vmem_limit_bytes=VMEM_LIMIT),
        cost_estimate=pl.CostEstimate(flops=1000000, bytes_accessed=1, transcendentals=0),
    )(block)


def finish_kernel(places, *refs):
    shrink_ref, across_ref, near_slots, across_slots, *bases, own_ref, other_ref, out_ref = refs
    depth, columns = own_ref.shape
    own_rows = out_ref.shape[1]
    rows = SIDE * own_rows
    core = lax.axis_index("adapter") % CORES
    shrinks = []
    for step in range(places):
        across = packed_step(across_ref, step, places)
        swapped = jnp.concatenate([across[own_rows:], across[:own_rows]], axis=0)
        shrinks.append(packed_step(shrink_ref, step, places) + swapped)
    shrink = jnp.concatenate(shrinks, axis=0)
    slot = [slot_column(step, near_slots, across_slots, own_rows) for step in range(places)]
    slot = jnp.concatenate(slot, axis=0)
    wide = jnp.concatenate([shrink] * (depth // shrink.shape[1]), axis=1)
    lanes = lax.broadcasted_iota(jnp.int32, wide.shape, 1)
    spread = jnp.where(lanes // shrink.shape[1] == slot, wide, 0.0).astype(jnp.bfloat16)
    for which, up_ref in enumerate((own_ref, other_ref)):
        update = jnp.dot(spread, up_ref[...], preferred_element_type=jnp.float32)
        at = pl.multiple_of((core ^ which) * columns, columns)
        for step in range(places):
            here = slice(step * rows, (step + 1) * rows)
            if which == 0 and step:
                base = bases[step + 1][...]
            elif which == 0:
                base = jnp.concatenate([bases[0][...], bases[1][...]], axis=0)
            elif step < places - 2:
                base = bases[places + 1][here, :]
            else:
                base = bases[step + 4][...]
            query = (base + ADAPTER_SCALE * update[here]).astype(jnp.bfloat16)
            for side in range(SIDE):
                chip = ring_chip(places, -step, side)
                out_ref[chip, :, pl.ds(at, columns)] = query[side * own_rows : (side + 1) * own_rows]


def finish(places, shrink, across, slots, bases, own, other, own_rows):
    return call(
        lambda *refs: finish_kernel(places, *refs),
        jax.ShapeDtypeStruct((places * SIDE, own_rows, CORES * own.shape[1]), jnp.bfloat16),
        (shrink, across, *slots, *bases, own, other),
    )


def shards(
    hidden, norm_weight, query_weight, down_weights, up_weights, adapter_index, adapter_slot
):
    devices = lax.axis_size("adapter")
    me = lax.axis_index("adapter")
    places = devices // CORNERS
    own_rows, width = hidden.shape
    columns = query_weight.shape[1]
    rank = down_weights.shape[2]

    def move(x, steps, flip):
        return lax.ppermute(x, "adapter", pairs(places, steps, flip))

    def base_rows(rows, weight):
        return jnp.dot(rows, weight, preferred_element_type=jnp.float32)

    down = down_weights[0].T
    up = up_weights.reshape(devices * rank, columns)
    block, other = [hidden], []
    rows, tokens = [], []
    gain = norm_weight.reshape(1, width)
    bases = [base_rows(norm_rows([hidden], gain), query_weight)]
    last = places - 1

    weight_other = move(query_weight, 0, 1)
    down_other = move(down, 0, 1)
    near, count = own_slots(adapter_index, adapter_slot, places), 1
    far = move(near, count, 0)

    for step in range(last):
        if step:
            block[step] = after(block[step], bases[-1])
            tokens.append(token(block[step]))
        block.append(move(after(block[step], *tokens[-1:]), 1, 0))
        other.append(move(after(block[step], *other[-1:]), 0, 2))
        if step:
            rows.append(norm_rows(after([block[step - 1], other[step - 1]], block[step]), gain))
            here = rows[-1] if len(rows) > 1 else rows[0][own_rows:]
            bases.append(base_rows(here, query_weight))
            if count < places:
                near, count = merge(near, after(far, block[step]), count), 2 * count
                far = move(near, count, 0) if count < places else None
    across_slots = move(near, 0, 2)
    base, weight_other = base_and_weight(after(rows, bases[-1]), weight_other)
    block[last] = after(block[last], base)
    tokens.append(token(block[last]))
    source = after(block[last], other[-1], tokens[-1])
    source = jnp.where((me & 1) == 0, source, other[-1])
    crossed = lax.ppermute(source, "adapter", split_pairs(places))
    part = shrink_rows(after(rows, source), down, down_other, near, across_slots)
    rows.append(norm_rows(after([block[last - 1], other[-1]], source), gain))
    bases.append(base_rows(rows[-1], query_weight))
    bases_other = [base, base_rows(rows[-1], weight_other)]
    up_other = move(after(up, part), 0, 1)
    ends = [block[last], after(crossed, part, bases[-1], bases_other[-1])]
    part, here = last_rows(ends, gain, rows[-1], down, down_other, part, near, across_slots, tokens)
    rows.append(here)

    moved = [part] + [move(part, steps, 0) for steps in range(1, places)]
    bases.append(base_rows(rows[-1], query_weight))
    moved = after(moved, bases[-1])
    shrink = call(
        lambda *refs: sum_kernel(places, *refs), jax.ShapeDtypeStruct(part.shape, part.dtype), moved
    )
    across = move(shrink, 0, 2)
    bases_other.append(base_rows(after(rows[-1], shrink), weight_other))
    slots = (near, across_slots)
    query = finish(places, shrink, across, slots, bases + bases_other, up, up_other, own_rows)
    groups = [list(range(core, devices, CORES)) for core in range(CORES)]
    query = lax.all_to_all(query, "adapter", 0, 0, axis_index_groups=groups, tiled=True)
    return query.transpose(1, 0, 2).reshape(own_rows, devices * columns)


def solution(mesh):
    in_specs = (
        P(("group", "adapter"), None),
        P(),
        P(None, "adapter"),
        P("adapter", None, None),
        P(None, None, "adapter"),
        P(("group", "adapter"), None),
        P(),
    )
    out_specs = P(("group", "adapter"), None)
    return jax.shard_map(shards, mesh=mesh, in_specs=in_specs, out_specs=out_specs, check_vma=False)
```

```python
import jax
import jax.numpy as jnp
from jax import lax
from jax.experimental import pallas as pl
from jax.experimental.pallas import tpu as pltpu
from jax.sharding import PartitionSpec as P

ADAPTER_SCALE = 0.5
EPS = 1e-05

SIDE = 2
CORES = 2
CORNERS = SIDE * CORES
LANES = 128
CHUNK = 1024
PIECES = 4
VMEM_LIMIT = 12 << 20
VMEM = pl.BlockSpec(memory_space=pltpu.VMEM)


def line_ring(places):
    odd = list(range(1, places, 2))
    even = list(range(0, places, 2))
    return [0] + odd + even[:0:-1]


def pairs(places, steps, flip):
    ring = line_ring(places)
    out = []
    for at, place in enumerate(ring):
        target = ring[(at + steps) % places]
        for corner in range(CORNERS):
            out.append((place * CORNERS + corner, target * CORNERS + (corner ^ flip)))
    return out


def split_pairs(places):
    flips, steps = pairs(places, 0, 2), pairs(places, 1, 0)
    return [pair for pair in flips if pair[0] % CORES == 0] + [
        pair for pair in steps if pair[0] % CORES
    ]


def ring_chip(places, steps, side):
    chip = lax.axis_index("adapter") // CORES
    ring = line_ring(places)
    target = jnp.int32(0)
    for at, name in enumerate(ring):
        target = jnp.where(chip // SIDE == name, jnp.int32(ring[(at + steps) % places]), target)
    return target * SIDE + ((chip % SIDE) ^ side)


def after(x, *others):
    return lax.optimization_barrier((x, *others))[0]


def call(kernel, out_shape, operands):
    return pl.pallas_call(
        kernel,
        out_shape=out_shape,
        in_specs=[VMEM] * len(operands),
        out_specs=jax.tree.map(lambda _: VMEM, out_shape),
        compiler_params=pltpu.CompilerParams(vmem_limit_bytes=VMEM_LIMIT),
        cost_estimate=pl.CostEstimate(flops=1, bytes_accessed=1, transcendentals=0),
    )(*operands)


def norm_kernel(*refs):
    sources, (out_ref, *buffers, sems) = refs[:4], refs[4:]
    copies = [
        pltpu.make_async_copy(source, buffer, sems.at[number])
        for number, (source, buffer) in enumerate(zip(sources, buffers))
    ]
    for copy in copies:
        copy.start()
    for copy in copies:
        copy.wait()
    hidden_ref, gain_ref, index_ref, slot_ref = buffers
    rows, width = hidden_ref.shape
    squares = jnp.zeros((rows, LANES), jnp.float32)
    for start in range(0, width, CHUNK):
        wide = hidden_ref[:, start : start + CHUNK].astype(jnp.float32)
        wide = wide * wide
        for lane in range(0, CHUNK, LANES):
            squares = squares + wide[:, lane : lane + LANES]
    inv_rms = lax.rsqrt(jnp.sum(squares, axis=1, keepdims=True) / width + EPS)
    for start in range(0, width, CHUNK):
        lanes = slice(start, start + CHUNK)
        wide = hidden_ref[:, lanes].astype(jnp.float32)
        out_ref[:, lanes] = (wide * inv_rms * gain_ref[:, lanes]).astype(jnp.bfloat16)
    index = index_ref[...]
    slot = jnp.zeros(index.shape, jnp.float32)
    for name in range(slot_ref.shape[1]):
        slot = jnp.where(index == name, slot_ref[0, name].astype(jnp.float32), slot)
    across = lax.broadcasted_iota(jnp.int32, (rows, rows), 1)
    down = lax.broadcasted_iota(jnp.int32, (rows, rows), 0)
    column = jnp.sum(jnp.where(across == down, slot, 0.0), axis=1, keepdims=True)
    out_ref[:, width:] = jnp.broadcast_to(column, (rows, LANES)).astype(jnp.bfloat16)


def normalize(hidden, norm_weight, adapter_index, adapter_slot):
    rows, width = hidden.shape
    sources = (
        hidden,
        norm_weight.reshape(1, width),
        adapter_index.reshape(1, rows),
        adapter_slot.reshape(1, -1),
    )
    spaces = (pltpu.VMEM, pltpu.VMEM, pltpu.VMEM, pltpu.SMEM)
    return pl.pallas_call(
        norm_kernel,
        out_shape=jax.ShapeDtypeStruct((rows, width + LANES), jnp.bfloat16),
        in_specs=[pl.BlockSpec(memory_space=pltpu.HBM)] * len(sources),
        out_specs=VMEM,
        scratch_shapes=[space(x.shape, x.dtype) for space, x in zip(spaces, sources)]
        + [pltpu.SemaphoreType.DMA((len(sources),))],
    )(*sources)


def shrink_kernel(halves, *refs):
    blocks, (own_ref, other_ref, *before, part_ref, slot_ref, rows_ref) = refs[:SIDE], refs[SIDE:]
    rank, width = own_ref.shape
    rows = slot_ref.shape[0]
    part = jnp.zeros((rows, 2 * rank), jnp.float32)
    for start in range(0, width, CHUNK):
        lanes = slice(start, start + CHUNK)
        wide = [block[:, lanes].astype(jnp.float32) for block in blocks]
        chunk = jnp.concatenate(wide, axis=0).astype(jnp.bfloat16)
        rows_ref[:, lanes] = chunk
        down = jnp.concatenate([own_ref[:, lanes], other_ref[:, lanes]], axis=0)
        part += lax.dot_general(
            chunk, down, (((1,), (1,)), ((), ())), preferred_element_type=jnp.float32
        )
    slot = [block[:, width:].astype(jnp.float32) for block in blocks]
    slot = jnp.concatenate(slot, axis=0)[:, 0:1].astype(jnp.int32)
    slot_ref[...] = jnp.broadcast_to(slot, slot_ref.shape)
    me = lax.axis_index("adapter")
    lanes = lax.broadcasted_iota(jnp.int32, part.shape, 1)
    part = jnp.where(slot == jnp.where(lanes < rank, me, me ^ 1), part, 0.0)
    part = part[:, :rank] + part[:, rank:]
    if halves:
        steps = [ref[...].astype(jnp.float32) for ref in before] + [part]
        middle = len(steps) // 2
        halves = [jnp.concatenate(steps[:middle], axis=0), jnp.concatenate(steps[middle:], axis=0)]
        part = jnp.concatenate(halves, axis=1)
    part_ref[...] = part.astype(jnp.bfloat16)


def shrink_rows(blocks, own, other, before=(), tokens=()):
    rows = blocks[0].shape[0] * SIDE
    rank, width = own.shape
    packed = (rows * (len(before) + 1) // 2, 2 * rank) if before else (rows, rank)
    out_shape = (
        jax.ShapeDtypeStruct(packed, jnp.bfloat16),
        jax.ShapeDtypeStruct((rows, LANES), jnp.int32),
        jax.ShapeDtypeStruct((rows, width), jnp.bfloat16),
    )
    return call(
        lambda *refs: shrink_kernel(bool(before), *refs[len(tokens) :]),
        out_shape,
        (*tokens, *blocks, own, other, *before),
    )


def sum_kernel(places, *refs):
    *moved, out_ref = refs
    half, rank = moved[0].shape[0], moved[0].shape[1] // 2
    rows = half // (places // 2)
    for step in range(places):
        shrink = jnp.zeros((rows, rank), jnp.float32)
        for back in range(places):
            shrink += packed_step(moved[back], (step - back) % places, places)
        side, first = divmod(step, places // 2)
        out_ref[first * rows : (first + 1) * rows, side * rank : (side + 1) * rank] = shrink.astype(
            jnp.bfloat16
        )


def packed_step(ref, step, places):
    rank = ref.shape[1] // 2
    rows = ref.shape[0] // (places // 2)
    side, first = divmod(step, places // 2)
    return ref[first * rows : (first + 1) * rows, side * rank : (side + 1) * rank].astype(jnp.float32)


def base_kernel(*refs):
    *blocks, weight_ref, out_ref, kept_ref, sems = refs
    width = weight_ref.shape[0]
    copies = []
    for number, start in enumerate(range(0, width, CHUNK)):
        here = pl.ds(start, CHUNK)
        copies.append(
            pltpu.make_async_copy(weight_ref.at[here], kept_ref.at[here], sems.at[number])
        )
        copies[-1].start()
    out_ref[...] = jnp.zeros(out_ref.shape, jnp.float32)
    for number, start in enumerate(range(0, width, CHUNK)):
        lanes = slice(start, start + CHUNK)
        rows = jnp.concatenate([block[:, lanes] for block in blocks], axis=0)
        copies[number].wait()
        out_ref[...] += jnp.dot(rows, kept_ref[lanes, :], preferred_element_type=jnp.float32)


def base_and_weight(blocks, weight):
    rows = blocks[0].shape[0] * len(blocks)
    return pl.pallas_call(
        base_kernel,
        out_shape=(
            jax.ShapeDtypeStruct((rows, weight.shape[1]), jnp.float32),
            jax.ShapeDtypeStruct(weight.shape, weight.dtype),
        ),
        in_specs=[VMEM] * len(blocks) + [pl.BlockSpec(memory_space=pltpu.HBM)],
        out_specs=(VMEM, VMEM),
        scratch_shapes=[pltpu.SemaphoreType.DMA((weight.shape[0] // CHUNK,))],
        compiler_params=pltpu.CompilerParams(vmem_limit_bytes=VMEM_LIMIT),
        cost_estimate=pl.CostEstimate(flops=1, bytes_accessed=1, transcendentals=0),
    )(*blocks, weight)


def load_kernel(*refs):
    *refs, sems = refs
    count = len(refs) // 2
    copies = []
    for number, (source, target) in enumerate(zip(refs[:count], refs[count:])):
        size = source.shape[0] // PIECES
        for piece in range(PIECES):
            here = pl.ds(piece * size, size)
            copies.append(
                pltpu.make_async_copy(source.at[here], target.at[here], sems.at[number, piece])
            )
    for copy in copies:
        copy.start()
    for copy in copies:
        copy.wait()


def load(*arrays):
    return pl.pallas_call(
        load_kernel,
        out_shape=[jax.ShapeDtypeStruct(x.shape, x.dtype) for x in arrays],
        in_specs=[pl.BlockSpec(memory_space=pltpu.HBM)] * len(arrays),
        out_specs=[VMEM] * len(arrays),
        scratch_shapes=[pltpu.SemaphoreType.DMA((len(arrays), PIECES))],
        compiler_params=pltpu.CompilerParams(vmem_limit_bytes=VMEM_LIMIT),
        cost_estimate=pl.CostEstimate(flops=1, bytes_accessed=1, transcendentals=0),
    )(*arrays)


def token_kernel(block_ref, out_ref):
    out_ref[...] = jnp.zeros(out_ref.shape, out_ref.dtype)


def token(block):
    return pl.pallas_call(
        token_kernel,
        out_shape=jax.ShapeDtypeStruct((8, LANES), jnp.float32),
        in_specs=[pl.BlockSpec(memory_space=pl.ANY)],
        out_specs=VMEM,
        compiler_params=pltpu.CompilerParams(vmem_limit_bytes=VMEM_LIMIT),
        cost_estimate=pl.CostEstimate(flops=1000000, bytes_accessed=1, transcendentals=0),
    )(block)


def finish_kernel(places, *refs):
    shrink_ref, across_ref, *refs = refs
    bases, slots = refs[: places + 3], refs[places + 3 : 2 * places + 3]
    own_ref, other_ref, out_ref = refs[2 * places + 3 :]
    depth, columns = own_ref.shape
    own_rows = out_ref.shape[1]
    rows = SIDE * own_rows
    core = lax.axis_index("adapter") % CORES
    shrinks = []
    for step in range(places):
        across = packed_step(across_ref, step, places)
        swapped = jnp.concatenate([across[own_rows:], across[:own_rows]], axis=0)
        shrinks.append(packed_step(shrink_ref, step, places) + swapped)
    shrink = jnp.concatenate(shrinks, axis=0)
    slot = jnp.concatenate([ref[:, 0:1] for ref in slots], axis=0)
    wide = jnp.concatenate([shrink] * (depth // shrink.shape[1]), axis=1)
    lanes = lax.broadcasted_iota(jnp.int32, wide.shape, 1)
    spread = jnp.where(lanes // shrink.shape[1] == slot, wide, 0.0).astype(jnp.bfloat16)
    for which, up_ref in enumerate((own_ref, other_ref)):
        update = jnp.dot(spread, up_ref[...], preferred_element_type=jnp.float32)
        at = pl.multiple_of((core ^ which) * columns, columns)
        for step in range(places):
            here = slice(step * rows, (step + 1) * rows)
            if which == 0:
                base = bases[step][...]
            elif step < places - 2:
                base = bases[places][here, :]
            else:
                base = bases[step + 3][...]
            query = (base + ADAPTER_SCALE * update[here]).astype(jnp.bfloat16)
            for side in range(SIDE):
                chip = ring_chip(places, -step, side)
                out_ref[chip, :, pl.ds(at, columns)] = query[side * own_rows : (side + 1) * own_rows]


def finish(shrink, across, bases, slots, own, other, own_rows):
    places = len(slots)
    return call(
        lambda *refs: finish_kernel(places, *refs),
        jax.ShapeDtypeStruct((places * SIDE, own_rows, CORES * own.shape[1]), jnp.bfloat16),
        (shrink, across, *bases, *slots, own, other),
    )


def shards(
    hidden, norm_weight, query_weight, down_weights, up_weights, adapter_index, adapter_slot
):
    devices = lax.axis_size("adapter")
    me = lax.axis_index("adapter")
    places = devices // CORNERS
    own_rows, width = hidden.shape
    columns = query_weight.shape[1]
    rank = down_weights.shape[2]

    def move(x, steps, flip):
        return lax.ppermute(x, "adapter", pairs(places, steps, flip))

    def base_rows(rows, weight):
        return jnp.dot(rows, weight, preferred_element_type=jnp.float32)

    down = down_weights[0].T
    up = up_weights.reshape(devices * rank, columns)
    down_other = move(down, 0, 1)
    up_other = move(up, 0, 1)
    weight_other = move(query_weight, 0, 1)

    block, other = [normalize(hidden, norm_weight, adapter_index, adapter_slot)], []
    parts, slots, rows, bases, tokens = [], [], [], [], []
    last = places - 1
    query_weight, down = load(*after([query_weight, down], block[0]))

    def meet(blocks, before=()):
        part, slot, here = shrink_rows(blocks, down, down_other, before, tokens if before else ())
        parts.append(part)
        slots.append(slot)
        rows.append(here)

    for step in range(last):
        if step:
            block[step] = after(block[step], *(bases[-1:] or [query_weight]))
            tokens.append(token(block[step]))
        block.append(move(after(block[step], *tokens[-1:]), 1, 0))
        other.append(move(after(block[step], *other[-1:]), 0, 2))
        if step:
            meet(after([block[step - 1], other[step - 1]], block[step]))
            bases.append(base_rows(rows[-1], query_weight))
    base, weight_other = base_and_weight(after(rows, bases[-1]), weight_other)
    block[last] = after(block[last], base)
    tokens.append(token(block[last]))
    source = after(block[last], other[-1], tokens[-1])
    source = jnp.where((me & 1) == 0, source, other[-1])
    crossed = lax.ppermute(source, "adapter", split_pairs(places))
    meet(after([block[last - 1], other[-1]], source))
    bases.append(base_rows(rows[-1], query_weight))
    bases_other = [base, base_rows(rows[-1], weight_other)]
    meet([block[last], after(crossed, bases[-1], bases_other[-1])], parts)

    part = parts[-1]
    moved = [part] + [move(part, steps, 0) for steps in range(1, places)]
    bases.append(base_rows(rows[-1], query_weight))
    moved = after(moved, bases[-1])
    shrink = call(
        lambda *refs: sum_kernel(places, *refs), jax.ShapeDtypeStruct(part.shape, part.dtype), moved
    )
    across = move(shrink, 0, 2)
    bases_other.append(base_rows(after(rows[-1], shrink), weight_other))
    query = finish(shrink, across, bases + bases_other, slots, up, up_other, own_rows)
    groups = [list(range(core, devices, CORES)) for core in range(CORES)]
    query = lax.all_to_all(query, "adapter", 0, 0, axis_index_groups=groups, tiled=True)
    return query.transpose(1, 0, 2).reshape(own_rows, devices * columns)


def solution(mesh):
    in_specs = (
        P(("group", "adapter"), None),
        P(),
        P(None, "adapter"),
        P("adapter", None, None),
        P(None, None, "adapter"),
        P(("group", "adapter"), None),
        P(),
    )
    out_specs = P(("group", "adapter"), None)
    return jax.shard_map(shards, mesh=mesh, in_specs=in_specs, out_specs=out_specs, check_vma=False)
```

```python
import jax
import jax.numpy as jnp
from jax import lax
from jax.experimental import pallas as pl
from jax.experimental.pallas import tpu as pltpu
from jax.sharding import PartitionSpec as P

ADAPTER_SCALE = 0.5
EPS = 1e-05

SIDE = 2
CORES = 2
CORNERS = SIDE * CORES
LANES = 128
CHUNK = 1024
PIECE = 2048
VMEM_LIMIT = 24 << 20
VMEM = pl.BlockSpec(memory_space=pltpu.VMEM)


def line_ring(places):
    odd = list(range(1, places, 2))
    even = list(range(0, places, 2))
    return [0] + odd + even[:0:-1]


def pairs(places, steps, flip):
    ring = line_ring(places)
    out = []
    for at, place in enumerate(ring):
        target = ring[(at + steps) % places]
        for corner in range(CORNERS):
            out.append((place * CORNERS + corner, target * CORNERS + (corner ^ flip)))
    return out


def split_pairs(places):
    flips, steps = pairs(places, 0, 2), pairs(places, 1, 0)
    return [pair for pair in flips if pair[0] % CORES == 0] + [
        pair for pair in steps if pair[0] % CORES
    ]


def ring_chip(places, steps, side):
    chip = lax.axis_index("adapter") // CORES
    ring = line_ring(places)
    target = jnp.int32(0)
    for at, name in enumerate(ring):
        target = jnp.where(chip // SIDE == name, jnp.int32(ring[(at + steps) % places]), target)
    return target * SIDE + ((chip % SIDE) ^ side)


def after(x, *others):
    return lax.optimization_barrier((x, *others))[0]


def call(kernel, out_shape, operands):
    return pl.pallas_call(
        kernel,
        out_shape=out_shape,
        in_specs=[VMEM] * len(operands),
        out_specs=jax.tree.map(lambda _: VMEM, out_shape),
        compiler_params=pltpu.CompilerParams(vmem_limit_bytes=VMEM_LIMIT),
        cost_estimate=pl.CostEstimate(flops=1, bytes_accessed=1, transcendentals=0),
    )(*operands)


def norm_kernel(*refs):
    sources, out_hbm, buffers, out_ref, in_sems, out_sems = refs[:4], refs[4], refs[5:9], *refs[9:]
    hidden_ref, gain_ref, index_ref, slot_ref = buffers
    rows, width = hidden_ref.shape
    chunks = [pl.ds(start, PIECE) for start in range(0, width, PIECE)]
    arriving = [
        pltpu.make_async_copy(
            sources[0].at[:, chunk], hidden_ref.at[:, chunk], in_sems.at[len(buffers) + number]
        )
        for number, chunk in enumerate(chunks)
    ]
    others = [
        pltpu.make_async_copy(source, buffer, in_sems.at[number])
        for number, (source, buffer) in enumerate(zip(sources, buffers))
        if number
    ]
    for copy in arriving + others:
        copy.start()
    squares = jnp.zeros((rows, LANES), jnp.float32)
    for number, copy in enumerate(arriving):
        copy.wait()
        for start in range(number * PIECE, (number + 1) * PIECE, CHUNK):
            wide = hidden_ref[:, start : start + CHUNK].astype(jnp.float32)
            wide = wide * wide
            for lane in range(0, CHUNK, LANES):
                squares = squares + wide[:, lane : lane + LANES]
    inv_rms = lax.rsqrt(jnp.sum(squares, axis=1, keepdims=True) / width + EPS)
    for copy in others:
        copy.wait()
    leaving = []
    for number, chunk in enumerate(chunks):
        for start in range(number * PIECE, (number + 1) * PIECE, CHUNK):
            lanes = slice(start, start + CHUNK)
            wide = hidden_ref[:, lanes].astype(jnp.float32)
            out_ref[:, lanes] = (wide * inv_rms * gain_ref[:, lanes]).astype(jnp.bfloat16)
        leaving.append(
            pltpu.make_async_copy(out_ref.at[:, chunk], out_hbm.at[:, chunk], out_sems.at[number])
        )
        leaving[-1].start()
    index = index_ref[...]
    slot = jnp.zeros(index.shape, jnp.float32)
    for name in range(slot_ref.shape[1]):
        slot = jnp.where(index == name, slot_ref[0, name].astype(jnp.float32), slot)
    across = lax.broadcasted_iota(jnp.int32, (rows, rows), 1)
    down = lax.broadcasted_iota(jnp.int32, (rows, rows), 0)
    column = jnp.sum(jnp.where(across == down, slot, 0.0), axis=1, keepdims=True)
    out_ref[:, width:] = jnp.broadcast_to(column, (rows, LANES)).astype(jnp.bfloat16)
    end = pl.ds(width, LANES)
    leaving.append(
        pltpu.make_async_copy(out_ref.at[:, end], out_hbm.at[:, end], out_sems.at[len(chunks)])
    )
    leaving[-1].start()
    for copy in leaving:
        copy.wait()


def normalize(hidden, norm_weight, adapter_index, adapter_slot):
    rows, width = hidden.shape
    sources = (
        hidden,
        norm_weight.reshape(1, width),
        adapter_index.reshape(1, rows),
        adapter_slot.reshape(1, -1),
    )
    spaces = (pltpu.VMEM, pltpu.VMEM, pltpu.VMEM, pltpu.SMEM)
    out_shape = jax.ShapeDtypeStruct((rows, width + LANES), jnp.bfloat16)
    pieces = width // PIECE
    return pl.pallas_call(
        norm_kernel,
        out_shape=out_shape,
        in_specs=[pl.BlockSpec(memory_space=pltpu.HBM)] * len(sources),
        out_specs=pl.BlockSpec(memory_space=pltpu.HBM),
        scratch_shapes=[space(x.shape, x.dtype) for space, x in zip(spaces, sources)]
        + [
            pltpu.VMEM(out_shape.shape, out_shape.dtype),
            pltpu.SemaphoreType.DMA((len(sources) + pieces,)),
            pltpu.SemaphoreType.DMA((pieces + 1,)),
        ],
    )(*sources)


def shrink_kernel(halves, *refs):
    blocks, (own_ref, other_ref, *before, part_ref, slot_ref, rows_ref) = refs[:SIDE], refs[SIDE:]
    rank, width = own_ref.shape
    rows = slot_ref.shape[0]
    part = jnp.zeros((rows, 2 * rank), jnp.float32)
    for start in range(0, width, CHUNK):
        lanes = slice(start, start + CHUNK)
        wide = [block[:, lanes].astype(jnp.float32) for block in blocks]
        chunk = jnp.concatenate(wide, axis=0).astype(jnp.bfloat16)
        rows_ref[:, lanes] = chunk
        down = jnp.concatenate([own_ref[:, lanes], other_ref[:, lanes]], axis=0)
        part += lax.dot_general(
            chunk, down, (((1,), (1,)), ((), ())), preferred_element_type=jnp.float32
        )
    slot = [block[:, width:].astype(jnp.float32) for block in blocks]
    slot = jnp.concatenate(slot, axis=0)[:, 0:1].astype(jnp.int32)
    slot_ref[...] = jnp.broadcast_to(slot, slot_ref.shape)
    me = lax.axis_index("adapter")
    lanes = lax.broadcasted_iota(jnp.int32, part.shape, 1)
    part = jnp.where(slot == jnp.where(lanes < rank, me, me ^ 1), part, 0.0)
    part = part[:, :rank] + part[:, rank:]
    if halves:
        steps = [ref[...].astype(jnp.float32) for ref in before] + [part]
        middle = len(steps) // 2
        halves = [jnp.concatenate(steps[:middle], axis=0), jnp.concatenate(steps[middle:], axis=0)]
        part = jnp.concatenate(halves, axis=1)
    part_ref[...] = part.astype(jnp.bfloat16)


def shrink_rows(blocks, own, other, before=(), tokens=()):
    rows = blocks[0].shape[0] * SIDE
    rank, width = own.shape
    packed = (rows * (len(before) + 1) // 2, 2 * rank) if before else (rows, rank)
    out_shape = (
        jax.ShapeDtypeStruct(packed, jnp.bfloat16),
        jax.ShapeDtypeStruct((rows, LANES), jnp.int32),
        jax.ShapeDtypeStruct((rows, width), jnp.bfloat16),
    )
    return call(
        lambda *refs: shrink_kernel(bool(before), *refs[len(tokens) :]),
        out_shape,
        (*tokens, *blocks, own, other, *before),
    )


def sum_kernel(places, *refs):
    *moved, out_ref = refs
    half, rank = moved[0].shape[0], moved[0].shape[1] // 2
    rows = half // (places // 2)
    for step in range(places):
        shrink = jnp.zeros((rows, rank), jnp.float32)
        for back in range(places):
            shrink += packed_step(moved[back], (step - back) % places, places)
        side, first = divmod(step, places // 2)
        out_ref[first * rows : (first + 1) * rows, side * rank : (side + 1) * rank] = shrink.astype(
            jnp.bfloat16
        )


def packed_step(ref, step, places):
    rank = ref.shape[1] // 2
    rows = ref.shape[0] // (places // 2)
    side, first = divmod(step, places // 2)
    return ref[first * rows : (first + 1) * rows, side * rank : (side + 1) * rank].astype(jnp.float32)


def base_kernel(*refs):
    *blocks, weight_ref, out_ref, kept_ref, sems = refs
    width = weight_ref.shape[0]
    copies = []
    for number, start in enumerate(range(0, width, CHUNK)):
        here = pl.ds(start, CHUNK)
        copies.append(
            pltpu.make_async_copy(weight_ref.at[here], kept_ref.at[here], sems.at[number])
        )
        copies[-1].start()
    out_ref[...] = jnp.zeros(out_ref.shape, jnp.float32)
    for number, start in enumerate(range(0, width, CHUNK)):
        lanes = slice(start, start + CHUNK)
        rows = jnp.concatenate([block[:, lanes] for block in blocks], axis=0)
        copies[number].wait()
        out_ref[...] += jnp.dot(rows, kept_ref[lanes, :], preferred_element_type=jnp.float32)


def base_and_weight(blocks, weight):
    rows = blocks[0].shape[0] * len(blocks)
    return pl.pallas_call(
        base_kernel,
        out_shape=(
            jax.ShapeDtypeStruct((rows, weight.shape[1]), jnp.float32),
            jax.ShapeDtypeStruct(weight.shape, weight.dtype),
        ),
        in_specs=[VMEM] * len(blocks) + [pl.BlockSpec(memory_space=pltpu.HBM)],
        out_specs=(VMEM, VMEM),
        scratch_shapes=[pltpu.SemaphoreType.DMA((weight.shape[0] // CHUNK,))],
        compiler_params=pltpu.CompilerParams(vmem_limit_bytes=VMEM_LIMIT),
        cost_estimate=pl.CostEstimate(flops=1, bytes_accessed=1, transcendentals=0),
    )(*blocks, weight)


def token_kernel(block_ref, out_ref):
    out_ref[...] = jnp.zeros(out_ref.shape, out_ref.dtype)


def token(block):
    return pl.pallas_call(
        token_kernel,
        out_shape=jax.ShapeDtypeStruct((8, LANES), jnp.float32),
        in_specs=[pl.BlockSpec(memory_space=pl.ANY)],
        out_specs=VMEM,
        compiler_params=pltpu.CompilerParams(vmem_limit_bytes=VMEM_LIMIT),
        cost_estimate=pl.CostEstimate(flops=1000000, bytes_accessed=1, transcendentals=0),
    )(block)


def finish_kernel(places, *refs):
    shrink_ref, across_ref, *refs = refs
    bases, slots = refs[: places + 3], refs[places + 3 : 2 * places + 3]
    own_ref, other_ref, out_ref = refs[2 * places + 3 :]
    depth, columns = own_ref.shape
    own_rows = out_ref.shape[1]
    rows = SIDE * own_rows
    core = lax.axis_index("adapter") % CORES
    shrinks = []
    for step in range(places):
        across = packed_step(across_ref, step, places)
        swapped = jnp.concatenate([across[own_rows:], across[:own_rows]], axis=0)
        shrinks.append(packed_step(shrink_ref, step, places) + swapped)
    shrink = jnp.concatenate(shrinks, axis=0)
    slot = jnp.concatenate([ref[:, 0:1] for ref in slots], axis=0)
    wide = jnp.concatenate([shrink] * (depth // shrink.shape[1]), axis=1)
    lanes = lax.broadcasted_iota(jnp.int32, wide.shape, 1)
    spread = jnp.where(lanes // shrink.shape[1] == slot, wide, 0.0).astype(jnp.bfloat16)
    for which, up_ref in enumerate((own_ref, other_ref)):
        update = jnp.dot(spread, up_ref[...], preferred_element_type=jnp.float32)
        at = pl.multiple_of((core ^ which) * columns, columns)
        for step in range(places):
            here = slice(step * rows, (step + 1) * rows)
            if which == 0:
                base = bases[step][...]
            elif step < places - 2:
                base = bases[places][here, :]
            else:
                base = bases[step + 3][...]
            query = (base + ADAPTER_SCALE * update[here]).astype(jnp.bfloat16)
            for side in range(SIDE):
                chip = ring_chip(places, -step, side)
                out_ref[chip, :, pl.ds(at, columns)] = query[side * own_rows : (side + 1) * own_rows]


def finish(shrink, across, bases, slots, own, other, own_rows):
    places = len(slots)
    return call(
        lambda *refs: finish_kernel(places, *refs),
        jax.ShapeDtypeStruct((places * SIDE, own_rows, CORES * own.shape[1]), jnp.bfloat16),
        (shrink, across, *bases, *slots, own, other),
    )


def shards(
    hidden, norm_weight, query_weight, down_weights, up_weights, adapter_index, adapter_slot
):
    devices = lax.axis_size("adapter")
    me = lax.axis_index("adapter")
    places = devices // CORNERS
    own_rows, width = hidden.shape
    columns = query_weight.shape[1]
    rank = down_weights.shape[2]

    def move(x, steps, flip):
        return lax.ppermute(x, "adapter", pairs(places, steps, flip))

    def base_rows(rows, weight):
        return jnp.dot(rows, weight, preferred_element_type=jnp.float32)

    down = down_weights[0].T
    up = up_weights.reshape(devices * rank, columns)
    down_other = move(down, 0, 1)
    up_other = move(up, 0, 1)
    weight_other = move(query_weight, 0, 1)

    block, other = [normalize(hidden, norm_weight, adapter_index, adapter_slot)], []
    parts, slots, rows, bases, tokens = [], [], [], [], []
    last = places - 1

    def meet(blocks, before=()):
        part, slot, here = shrink_rows(blocks, down, down_other, before, tokens if before else ())
        parts.append(part)
        slots.append(slot)
        rows.append(here)

    for step in range(last):
        if step:
            block[step] = after(block[step], *bases[-1:])
            tokens.append(token(block[step]))
        block.append(move(after(block[step], *tokens[-1:]), 1, 0))
        other.append(move(after(block[step], *other[-1:]), 0, 2))
        if step:
            meet(after([block[step - 1], other[step - 1]], block[step]))
            bases.append(base_rows(rows[-1], query_weight))
    base, weight_other = base_and_weight(after(rows, bases[-1]), weight_other)
    block[last] = after(block[last], base)
    tokens.append(token(block[last]))
    source = after(block[last], other[-1], tokens[-1])
    source = jnp.where((me & 1) == 0, source, other[-1])
    crossed = lax.ppermute(source, "adapter", split_pairs(places))
    meet(after([block[last - 1], other[-1]], source))
    bases.append(base_rows(rows[-1], query_weight))
    bases_other = [base, base_rows(rows[-1], weight_other)]
    meet([block[last], after(crossed, bases[-1], bases_other[-1])], parts)

    part = parts[-1]
    moved = [part] + [move(part, steps, 0) for steps in range(1, places)]
    bases.append(base_rows(rows[-1], query_weight))
    moved = after(moved, bases[-1])
    shrink = call(
        lambda *refs: sum_kernel(places, *refs), jax.ShapeDtypeStruct(part.shape, part.dtype), moved
    )
    across = move(shrink, 0, 2)
    bases_other.append(base_rows(after(rows[-1], shrink), weight_other))
    query = finish(shrink, across, bases + bases_other, slots, up, up_other, own_rows)
    groups = [list(range(core, devices, CORES)) for core in range(CORES)]
    query = lax.all_to_all(query, "adapter", 0, 0, axis_index_groups=groups, tiled=True)
    return query.transpose(1, 0, 2).reshape(own_rows, devices * columns)


def solution(mesh):
    in_specs = (
        P(("group", "adapter"), None),
        P(),
        P(None, "adapter"),
        P("adapter", None, None),
        P(None, None, "adapter"),
        P(("group", "adapter"), None),
        P(),
    )
    out_specs = P(("group", "adapter"), None)
    return jax.shard_map(shards, mesh=mesh, in_specs=in_specs, out_specs=out_specs, check_vma=False)
```

```python
import jax
import jax.numpy as jnp
from jax import lax
from jax.experimental import pallas as pl
from jax.experimental.pallas import tpu as pltpu
from jax.sharding import PartitionSpec as P

ADAPTER_SCALE = 0.5
EPS = 1e-05

SIDE = 2
CORES = 2
CORNERS = SIDE * CORES
LANES = 128
CHUNK = 1024
VMEM_LIMIT = 24 << 20
LARGE = 44 << 20
VMEM = pl.BlockSpec(memory_space=pltpu.VMEM)


def line_ring(places):
    odd = list(range(1, places, 2))
    even = list(range(0, places, 2))
    return [0] + odd + even[:0:-1]


def pairs(places, steps, flip):
    ring = line_ring(places)
    out = []
    for at, place in enumerate(ring):
        target = ring[(at + steps) % places]
        for corner in range(CORNERS):
            out.append((place * CORNERS + corner, target * CORNERS + (corner ^ flip)))
    return out


def split_pairs(places):
    flips, steps = pairs(places, 0, 2), pairs(places, 1, 0)
    return [pair for pair in flips if pair[0] % CORES == 0] + [
        pair for pair in steps if pair[0] % CORES
    ]


def ring_chip(places, steps, side):
    chip = lax.axis_index("adapter") // CORES
    ring = line_ring(places)
    target = jnp.int32(0)
    for at, name in enumerate(ring):
        target = jnp.where(chip // SIDE == name, jnp.int32(ring[(at + steps) % places]), target)
    return target * SIDE + ((chip % SIDE) ^ side)


def after(x, *others):
    return lax.optimization_barrier((x, *others))[0]


def call(kernel, out_shape, operands):
    return pl.pallas_call(
        kernel,
        out_shape=out_shape,
        in_specs=[VMEM] * len(operands),
        out_specs=jax.tree.map(lambda _: VMEM, out_shape),
        compiler_params=pltpu.CompilerParams(vmem_limit_bytes=VMEM_LIMIT),
        cost_estimate=pl.CostEstimate(flops=1, bytes_accessed=1, transcendentals=0),
    )(*operands)


def norm_kernel(*refs):
    sources, (out_ref, *buffers, sems) = refs[:4], refs[4:]
    copies = [
        pltpu.make_async_copy(source, buffer, sems.at[number])
        for number, (source, buffer) in enumerate(zip(sources, buffers))
    ]
    for copy in copies:
        copy.start()
    for copy in copies:
        copy.wait()
    hidden_ref, gain_ref, index_ref, slot_ref = buffers
    rows, width = hidden_ref.shape
    squares = jnp.zeros((rows, LANES), jnp.float32)
    for start in range(0, width, CHUNK):
        wide = hidden_ref[:, start : start + CHUNK].astype(jnp.float32)
        wide = wide * wide
        for lane in range(0, CHUNK, LANES):
            squares = squares + wide[:, lane : lane + LANES]
    inv_rms = lax.rsqrt(jnp.sum(squares, axis=1, keepdims=True) / width + EPS)
    for start in range(0, width, CHUNK):
        lanes = slice(start, start + CHUNK)
        wide = hidden_ref[:, lanes].astype(jnp.float32)
        out_ref[:, lanes] = (wide * inv_rms * gain_ref[:, lanes]).astype(jnp.bfloat16)
    index = index_ref[...]
    slot = jnp.zeros(index.shape, jnp.float32)
    for name in range(slot_ref.shape[1]):
        slot = jnp.where(index == name, slot_ref[0, name].astype(jnp.float32), slot)
    across = lax.broadcasted_iota(jnp.int32, (rows, rows), 1)
    down = lax.broadcasted_iota(jnp.int32, (rows, rows), 0)
    column = jnp.sum(jnp.where(across == down, slot, 0.0), axis=1, keepdims=True)
    out_ref[:, width:] = jnp.broadcast_to(column, (rows, LANES)).astype(jnp.bfloat16)


def normalize(hidden, norm_weight, adapter_index, adapter_slot):
    rows, width = hidden.shape
    sources = (
        hidden,
        norm_weight.reshape(1, width),
        adapter_index.reshape(1, rows),
        adapter_slot.reshape(1, -1),
    )
    spaces = (pltpu.VMEM, pltpu.VMEM, pltpu.VMEM, pltpu.SMEM)
    return pl.pallas_call(
        norm_kernel,
        out_shape=jax.ShapeDtypeStruct((rows, width + LANES), jnp.bfloat16),
        in_specs=[pl.BlockSpec(memory_space=pltpu.HBM)] * len(sources),
        out_specs=VMEM,
        scratch_shapes=[space(x.shape, x.dtype) for space, x in zip(spaces, sources)]
        + [pltpu.SemaphoreType.DMA((len(sources),))],
    )(*sources)


def shrink_kernel(halves, *refs):
    blocks, (own_ref, other_ref, *before, part_ref, slot_ref, rows_ref) = refs[:SIDE], refs[SIDE:]
    rank, width = own_ref.shape
    rows = slot_ref.shape[0]
    part = jnp.zeros((rows, 2 * rank), jnp.float32)
    for start in range(0, width, CHUNK):
        lanes = slice(start, start + CHUNK)
        wide = [block[:, lanes].astype(jnp.float32) for block in blocks]
        chunk = jnp.concatenate(wide, axis=0).astype(jnp.bfloat16)
        rows_ref[:, lanes] = chunk
        down = jnp.concatenate([own_ref[:, lanes], other_ref[:, lanes]], axis=0)
        part += lax.dot_general(
            chunk, down, (((1,), (1,)), ((), ())), preferred_element_type=jnp.float32
        )
    slot = [block[:, width:].astype(jnp.float32) for block in blocks]
    slot = jnp.concatenate(slot, axis=0)[:, 0:1].astype(jnp.int32)
    slot_ref[...] = jnp.broadcast_to(slot, slot_ref.shape)
    me = lax.axis_index("adapter")
    lanes = lax.broadcasted_iota(jnp.int32, part.shape, 1)
    part = jnp.where(slot == jnp.where(lanes < rank, me, me ^ 1), part, 0.0)
    part = part[:, :rank] + part[:, rank:]
    if halves:
        steps = [ref[...].astype(jnp.float32) for ref in before] + [part]
        middle = len(steps) // 2
        halves = [jnp.concatenate(steps[:middle], axis=0), jnp.concatenate(steps[middle:], axis=0)]
        part = jnp.concatenate(halves, axis=1)
    part_ref[...] = part.astype(jnp.bfloat16)


def shrink_rows(blocks, own, other, before=(), tokens=()):
    rows = blocks[0].shape[0] * SIDE
    rank, width = own.shape
    packed = (rows * (len(before) + 1) // 2, 2 * rank) if before else (rows, rank)
    out_shape = (
        jax.ShapeDtypeStruct(packed, jnp.bfloat16),
        jax.ShapeDtypeStruct((rows, LANES), jnp.int32),
        jax.ShapeDtypeStruct((rows, width), jnp.bfloat16),
    )
    return call(
        lambda *refs: shrink_kernel(bool(before), *refs[len(tokens) :]),
        out_shape,
        (*tokens, *blocks, own, other, *before),
    )


def sum_kernel(places, *refs):
    *moved, out_ref = refs
    half, rank = moved[0].shape[0], moved[0].shape[1] // 2
    rows = half // (places // 2)
    for step in range(places):
        shrink = jnp.zeros((rows, rank), jnp.float32)
        for back in range(places):
            shrink += packed_step(moved[back], (step - back) % places, places)
        side, first = divmod(step, places // 2)
        out_ref[first * rows : (first + 1) * rows, side * rank : (side + 1) * rank] = shrink.astype(
            jnp.bfloat16
        )


def packed_step(ref, step, places):
    rank = ref.shape[1] // 2
    rows = ref.shape[0] // (places // 2)
    side, first = divmod(step, places // 2)
    return ref[first * rows : (first + 1) * rows, side * rank : (side + 1) * rank].astype(jnp.float32)


def base_kernel(*refs):
    *blocks, weight_ref, out_ref, kept_ref, sems = refs
    width = weight_ref.shape[0]
    copies = []
    for number, start in enumerate(range(0, width, CHUNK)):
        here = pl.ds(start, CHUNK)
        copies.append(
            pltpu.make_async_copy(weight_ref.at[here], kept_ref.at[here], sems.at[number])
        )
        copies[-1].start()
    out_ref[...] = jnp.zeros(out_ref.shape, jnp.float32)
    for number, start in enumerate(range(0, width, CHUNK)):
        lanes = slice(start, start + CHUNK)
        rows = jnp.concatenate([block[:, lanes] for block in blocks], axis=0)
        copies[number].wait()
        out_ref[...] += jnp.dot(rows, kept_ref[lanes, :], preferred_element_type=jnp.float32)


def base_and_weight(blocks, weight, limit=VMEM_LIMIT):
    rows = blocks[0].shape[0] * len(blocks)
    return pl.pallas_call(
        base_kernel,
        out_shape=(
            jax.ShapeDtypeStruct((rows, weight.shape[1]), jnp.float32),
            jax.ShapeDtypeStruct(weight.shape, weight.dtype),
        ),
        in_specs=[VMEM] * len(blocks) + [pl.BlockSpec(memory_space=pltpu.HBM)],
        out_specs=(VMEM, VMEM),
        scratch_shapes=[pltpu.SemaphoreType.DMA((weight.shape[0] // CHUNK,))],
        compiler_params=pltpu.CompilerParams(vmem_limit_bytes=limit),
        cost_estimate=pl.CostEstimate(flops=1, bytes_accessed=1, transcendentals=0),
    )(*blocks, weight)


def token_kernel(block_ref, out_ref):
    out_ref[...] = jnp.zeros(out_ref.shape, out_ref.dtype)


def token(block):
    return pl.pallas_call(
        token_kernel,
        out_shape=jax.ShapeDtypeStruct((8, LANES), jnp.float32),
        in_specs=[pl.BlockSpec(memory_space=pl.ANY)],
        out_specs=VMEM,
        compiler_params=pltpu.CompilerParams(vmem_limit_bytes=VMEM_LIMIT),
        cost_estimate=pl.CostEstimate(flops=1000000, bytes_accessed=1, transcendentals=0),
    )(block)


def finish_kernel(places, *refs):
    shrink_ref, across_ref, *refs = refs
    bases, slots = refs[: places + 3], refs[places + 3 : 2 * places + 3]
    own_ref, other_ref, out_ref = refs[2 * places + 3 :]
    depth, columns = own_ref.shape
    own_rows = out_ref.shape[1]
    rows = SIDE * own_rows
    core = lax.axis_index("adapter") % CORES
    shrinks = []
    for step in range(places):
        across = packed_step(across_ref, step, places)
        swapped = jnp.concatenate([across[own_rows:], across[:own_rows]], axis=0)
        shrinks.append(packed_step(shrink_ref, step, places) + swapped)
    shrink = jnp.concatenate(shrinks, axis=0)
    slot = jnp.concatenate([ref[:, 0:1] for ref in slots], axis=0)
    wide = jnp.concatenate([shrink] * (depth // shrink.shape[1]), axis=1)
    lanes = lax.broadcasted_iota(jnp.int32, wide.shape, 1)
    spread = jnp.where(lanes // shrink.shape[1] == slot, wide, 0.0).astype(jnp.bfloat16)
    for which, up_ref in enumerate((own_ref, other_ref)):
        update = jnp.dot(spread, up_ref[...], preferred_element_type=jnp.float32)
        at = pl.multiple_of((core ^ which) * columns, columns)
        for step in range(places):
            here = slice(step * rows, (step + 1) * rows)
            if which == 0:
                base = bases[step][...]
            elif step < places - 2:
                base = bases[places][here, :]
            else:
                base = bases[step + 3][...]
            query = (base + ADAPTER_SCALE * update[here]).astype(jnp.bfloat16)
            for side in range(SIDE):
                chip = ring_chip(places, -step, side)
                out_ref[chip, :, pl.ds(at, columns)] = query[side * own_rows : (side + 1) * own_rows]


def finish(shrink, across, bases, slots, own, other, own_rows):
    places = len(slots)
    return call(
        lambda *refs: finish_kernel(places, *refs),
        jax.ShapeDtypeStruct((places * SIDE, own_rows, CORES * own.shape[1]), jnp.bfloat16),
        (shrink, across, *bases, *slots, own, other),
    )


def shards(
    hidden, norm_weight, query_weight, down_weights, up_weights, adapter_index, adapter_slot
):
    devices = lax.axis_size("adapter")
    me = lax.axis_index("adapter")
    places = devices // CORNERS
    own_rows, width = hidden.shape
    columns = query_weight.shape[1]
    rank = down_weights.shape[2]

    def move(x, steps, flip):
        return lax.ppermute(x, "adapter", pairs(places, steps, flip))

    def base_rows(rows, weight):
        return jnp.dot(rows, weight, preferred_element_type=jnp.float32)

    down = down_weights[0].T
    up = up_weights.reshape(devices * rank, columns)
    down_other = move(down, 0, 1)
    up_other = move(up, 0, 1)
    weight_other = move(query_weight, 0, 1)

    block, other = [normalize(hidden, norm_weight, adapter_index, adapter_slot)], []
    parts, slots, rows, bases, tokens = [], [], [], [], []
    last = places - 1

    def meet(blocks, before=()):
        part, slot, here = shrink_rows(blocks, down, down_other, before, tokens if before else ())
        parts.append(part)
        slots.append(slot)
        rows.append(here)

    for step in range(last):
        if step:
            block[step] = after(block[step], *bases[-1:])
            tokens.append(token(block[step]))
        block.append(move(after(block[step], *tokens[-1:]), 1, 0))
        other.append(move(after(block[step], *other[-1:]), 0, 2))
        if step:
            meet(after([block[step - 1], other[step - 1]], block[step]))
            if step == 1:
                base, query_weight = base_and_weight(rows, query_weight, LARGE)
            else:
                base = base_rows(rows[-1], query_weight)
            bases.append(base)
    base, weight_other = base_and_weight(after(rows, bases[-1]), weight_other)
    block[last] = after(block[last], base)
    tokens.append(token(block[last]))
    source = after(block[last], other[-1], tokens[-1])
    source = jnp.where((me & 1) == 0, source, other[-1])
    crossed = lax.ppermute(source, "adapter", split_pairs(places))
    meet(after([block[last - 1], other[-1]], source))
    bases.append(base_rows(rows[-1], query_weight))
    bases_other = [base, base_rows(rows[-1], weight_other)]
    meet([block[last], after(crossed, bases[-1], bases_other[-1])], parts)

    part = parts[-1]
    moved = [part] + [move(part, steps, 0) for steps in range(1, places)]
    bases.append(base_rows(rows[-1], query_weight))
    moved = after(moved, bases[-1])
    shrink = call(
        lambda *refs: sum_kernel(places, *refs), jax.ShapeDtypeStruct(part.shape, part.dtype), moved
    )
    across = move(shrink, 0, 2)
    bases_other.append(base_rows(after(rows[-1], shrink), weight_other))
    query = finish(shrink, across, bases + bases_other, slots, up, up_other, own_rows)
    groups = [list(range(core, devices, CORES)) for core in range(CORES)]
    query = lax.all_to_all(query, "adapter", 0, 0, axis_index_groups=groups, tiled=True)
    return query.transpose(1, 0, 2).reshape(own_rows, devices * columns)


def solution(mesh):
    in_specs = (
        P(("group", "adapter"), None),
        P(),
        P(None, "adapter"),
        P("adapter", None, None),
        P(None, None, "adapter"),
        P(("group", "adapter"), None),
        P(),
    )
    out_specs = P(("group", "adapter"), None)
    return jax.shard_map(shards, mesh=mesh, in_specs=in_specs, out_specs=out_specs, check_vma=False)
```

```python
import jax
import jax.numpy as jnp
from jax import lax
from jax.experimental import pallas as pl
from jax.experimental.pallas import tpu as pltpu
from jax.sharding import PartitionSpec as P

ADAPTER_SCALE = 0.5
EPS = 1e-05

SIDE = 2
CORES = 2
CORNERS = SIDE * CORES
LANES = 128
CHUNK = 1024
VMEM_LIMIT = 24 << 20
VMEM = pl.BlockSpec(memory_space=pltpu.VMEM)


def line_ring(places):
    odd = list(range(1, places, 2))
    even = list(range(0, places, 2))
    return [0] + odd + even[:0:-1]


def pairs(places, steps, flip):
    ring = line_ring(places)
    out = []
    for at, place in enumerate(ring):
        target = ring[(at + steps) % places]
        for corner in range(CORNERS):
            out.append((place * CORNERS + corner, target * CORNERS + (corner ^ flip)))
    return out


def split_pairs(places):
    flips, steps = pairs(places, 0, 2), pairs(places, 1, 0)
    return [pair for pair in flips if pair[0] % CORES == 0] + [
        pair for pair in steps if pair[0] % CORES
    ]


def ring_chip(places, steps, side):
    chip = lax.axis_index("adapter") // CORES
    ring = line_ring(places)
    target = jnp.int32(0)
    for at, name in enumerate(ring):
        target = jnp.where(chip // SIDE == name, jnp.int32(ring[(at + steps) % places]), target)
    return target * SIDE + ((chip % SIDE) ^ side)


def after(x, *others):
    return lax.optimization_barrier((x, *others))[0]


def call(kernel, out_shape, operands):
    return pl.pallas_call(
        kernel,
        out_shape=out_shape,
        in_specs=[VMEM] * len(operands),
        out_specs=jax.tree.map(lambda _: VMEM, out_shape),
        compiler_params=pltpu.CompilerParams(vmem_limit_bytes=VMEM_LIMIT),
        cost_estimate=pl.CostEstimate(flops=1, bytes_accessed=1, transcendentals=0),
    )(*operands)


def norm_kernel(*refs):
    sources, (out_ref, *buffers, sems) = refs[:4], refs[4:]
    copies = [
        pltpu.make_async_copy(source, buffer, sems.at[number])
        for number, (source, buffer) in enumerate(zip(sources, buffers))
    ]
    for copy in copies:
        copy.start()
    for copy in copies:
        copy.wait()
    hidden_ref, gain_ref, index_ref, slot_ref = buffers
    rows, width = hidden_ref.shape
    squares = jnp.zeros((rows, LANES), jnp.float32)
    for start in range(0, width, CHUNK):
        wide = hidden_ref[:, start : start + CHUNK].astype(jnp.float32)
        wide = wide * wide
        for lane in range(0, CHUNK, LANES):
            squares = squares + wide[:, lane : lane + LANES]
    inv_rms = lax.rsqrt(jnp.sum(squares, axis=1, keepdims=True) / width + EPS)
    for start in range(0, width, CHUNK):
        lanes = slice(start, start + CHUNK)
        wide = hidden_ref[:, lanes].astype(jnp.float32)
        out_ref[:, lanes] = (wide * inv_rms * gain_ref[:, lanes]).astype(jnp.bfloat16)
    index = index_ref[...]
    slot = jnp.zeros(index.shape, jnp.float32)
    for name in range(slot_ref.shape[1]):
        slot = jnp.where(index == name, slot_ref[0, name].astype(jnp.float32), slot)
    across = lax.broadcasted_iota(jnp.int32, (rows, rows), 1)
    down = lax.broadcasted_iota(jnp.int32, (rows, rows), 0)
    column = jnp.sum(jnp.where(across == down, slot, 0.0), axis=1, keepdims=True)
    out_ref[:, width:] = jnp.broadcast_to(column, (rows, LANES)).astype(jnp.bfloat16)


def normalize(hidden, norm_weight, adapter_index, adapter_slot):
    rows, width = hidden.shape
    sources = (
        hidden,
        norm_weight.reshape(1, width),
        adapter_index.reshape(1, rows),
        adapter_slot.reshape(1, -1),
    )
    spaces = (pltpu.VMEM, pltpu.VMEM, pltpu.VMEM, pltpu.SMEM)
    return pl.pallas_call(
        norm_kernel,
        out_shape=jax.ShapeDtypeStruct((rows, width + LANES), jnp.bfloat16),
        in_specs=[pl.BlockSpec(memory_space=pltpu.HBM)] * len(sources),
        out_specs=VMEM,
        scratch_shapes=[space(x.shape, x.dtype) for space, x in zip(spaces, sources)]
        + [pltpu.SemaphoreType.DMA((len(sources),))],
    )(*sources)


def shrink_kernel(halves, *refs):
    blocks, (own_ref, other_ref, *before, part_ref, slot_ref, rows_ref) = refs[:SIDE], refs[SIDE:]
    rank, width = own_ref.shape
    rows = slot_ref.shape[0]
    part = jnp.zeros((rows, 2 * rank), jnp.float32)
    for start in range(0, width, CHUNK):
        lanes = slice(start, start + CHUNK)
        wide = [block[:, lanes].astype(jnp.float32) for block in blocks]
        chunk = jnp.concatenate(wide, axis=0).astype(jnp.bfloat16)
        rows_ref[:, lanes] = chunk
        down = jnp.concatenate([own_ref[:, lanes], other_ref[:, lanes]], axis=0)
        part += lax.dot_general(
            chunk, down, (((1,), (1,)), ((), ())), preferred_element_type=jnp.float32
        )
    slot = [block[:, width:].astype(jnp.float32) for block in blocks]
    slot = jnp.concatenate(slot, axis=0)[:, 0:1].astype(jnp.int32)
    slot_ref[...] = jnp.broadcast_to(slot, slot_ref.shape)
    me = lax.axis_index("adapter")
    lanes = lax.broadcasted_iota(jnp.int32, part.shape, 1)
    part = jnp.where(slot == jnp.where(lanes < rank, me, me ^ 1), part, 0.0)
    part = part[:, :rank] + part[:, rank:]
    if halves:
        steps = [ref[...].astype(jnp.float32) for ref in before] + [part]
        middle = len(steps) // 2
        halves = [jnp.concatenate(steps[:middle], axis=0), jnp.concatenate(steps[middle:], axis=0)]
        part = jnp.concatenate(halves, axis=1)
    part_ref[...] = part.astype(jnp.bfloat16)


def shrink_rows(blocks, own, other, before=(), tokens=()):
    rows = blocks[0].shape[0] * SIDE
    rank, width = own.shape
    packed = (rows * (len(before) + 1) // 2, 2 * rank) if before else (rows, rank)
    out_shape = (
        jax.ShapeDtypeStruct(packed, jnp.bfloat16),
        jax.ShapeDtypeStruct((rows, LANES), jnp.int32),
        jax.ShapeDtypeStruct((rows, width), jnp.bfloat16),
    )
    return call(
        lambda *refs: shrink_kernel(bool(before), *refs[len(tokens) :]),
        out_shape,
        (*tokens, *blocks, own, other, *before),
    )


def sum_kernel(places, *refs):
    *moved, out_ref = refs
    half, rank = moved[0].shape[0], moved[0].shape[1] // 2
    rows = half // (places // 2)
    for step in range(places):
        shrink = jnp.zeros((rows, rank), jnp.float32)
        for back in range(places):
            shrink += packed_step(moved[back], (step - back) % places, places)
        side, first = divmod(step, places // 2)
        out_ref[first * rows : (first + 1) * rows, side * rank : (side + 1) * rank] = shrink.astype(
            jnp.bfloat16
        )


def packed_step(ref, step, places):
    rank = ref.shape[1] // 2
    rows = ref.shape[0] // (places // 2)
    side, first = divmod(step, places // 2)
    return ref[first * rows : (first + 1) * rows, side * rank : (side + 1) * rank].astype(jnp.float32)


def base_kernel(*refs):
    *blocks, weight_ref, out_ref, kept_ref, sems = refs
    width = weight_ref.shape[0]
    copies = []
    for number, start in enumerate(range(0, width, CHUNK)):
        here = pl.ds(start, CHUNK)
        copies.append(
            pltpu.make_async_copy(weight_ref.at[here], kept_ref.at[here], sems.at[number])
        )
        copies[-1].start()
    out_ref[...] = jnp.zeros(out_ref.shape, jnp.float32)
    for number, start in enumerate(range(0, width, CHUNK)):
        lanes = slice(start, start + CHUNK)
        rows = jnp.concatenate([block[:, lanes] for block in blocks], axis=0)
        copies[number].wait()
        out_ref[...] += jnp.dot(rows, kept_ref[lanes, :], preferred_element_type=jnp.float32)


def base_and_weight(blocks, weight):
    rows = blocks[0].shape[0] * len(blocks)
    return pl.pallas_call(
        base_kernel,
        out_shape=(
            jax.ShapeDtypeStruct((rows, weight.shape[1]), jnp.float32),
            jax.ShapeDtypeStruct(weight.shape, weight.dtype),
        ),
        in_specs=[VMEM] * len(blocks) + [pl.BlockSpec(memory_space=pltpu.HBM)],
        out_specs=(VMEM, VMEM),
        scratch_shapes=[pltpu.SemaphoreType.DMA((weight.shape[0] // CHUNK,))],
        compiler_params=pltpu.CompilerParams(vmem_limit_bytes=VMEM_LIMIT),
        cost_estimate=pl.CostEstimate(flops=1, bytes_accessed=1, transcendentals=0),
    )(*blocks, weight)


def token_kernel(block_ref, out_ref):
    out_ref[...] = jnp.zeros(out_ref.shape, out_ref.dtype)


def token(block):
    return pl.pallas_call(
        token_kernel,
        out_shape=jax.ShapeDtypeStruct((8, LANES), jnp.float32),
        in_specs=[pl.BlockSpec(memory_space=pl.ANY)],
        out_specs=VMEM,
        compiler_params=pltpu.CompilerParams(vmem_limit_bytes=VMEM_LIMIT),
        cost_estimate=pl.CostEstimate(flops=1000000, bytes_accessed=1, transcendentals=0),
    )(block)


def finish_kernel(places, *refs):
    shrink_ref, across_ref, *refs = refs
    bases, slots = refs[: places + 3], refs[places + 3 : 2 * places + 3]
    own_ref, other_ref, *outs = refs[2 * places + 3 :]
    depth, columns = own_ref.shape
    own_rows = outs[0].shape[0]
    rows = SIDE * own_rows
    core = lax.axis_index("adapter") % CORES
    shrinks = []
    for step in range(places):
        across = packed_step(across_ref, step, places)
        swapped = jnp.concatenate([across[own_rows:], across[:own_rows]], axis=0)
        shrinks.append(packed_step(shrink_ref, step, places) + swapped)
    shrink = jnp.concatenate(shrinks, axis=0)
    slot = jnp.concatenate([ref[:, 0:1] for ref in slots], axis=0)
    wide = jnp.concatenate([shrink] * (depth // shrink.shape[1]), axis=1)
    lanes = lax.broadcasted_iota(jnp.int32, wide.shape, 1)
    spread = jnp.where(lanes // shrink.shape[1] == slot, wide, 0.0).astype(jnp.bfloat16)
    for which, up_ref in enumerate((own_ref, other_ref)):
        update = jnp.dot(spread, up_ref[...], preferred_element_type=jnp.float32)
        at = pl.multiple_of((core ^ which) * columns, columns)
        for step in range(places):
            here = slice(step * rows, (step + 1) * rows)
            if which == 0:
                base = bases[step][...]
            elif step < places - 2:
                base = bases[places][here, :]
            else:
                base = bases[step + 3][...]
            query = (base + ADAPTER_SCALE * update[here]).astype(jnp.bfloat16)
            for side in range(SIDE):
                out_ref = outs[step * SIDE + side]
                out_ref[:, pl.ds(at, columns)] = query[side * own_rows : (side + 1) * own_rows]


def finish(shrink, across, bases, slots, own, other, own_rows):
    places = len(slots)
    return call(
        lambda *refs: finish_kernel(places, *refs),
        [jax.ShapeDtypeStruct((own_rows, CORES * own.shape[1]), jnp.bfloat16)] * (places * SIDE),
        (shrink, across, *bases, *slots, own, other),
    )


def assemble_kernel(places, *refs):
    *blocks, out_ref = refs
    columns = blocks[0].shape[1]
    for step in range(places):
        for side in range(SIDE):
            at = pl.multiple_of(ring_chip(places, step, side) * columns, columns)
            out_ref[:, pl.ds(at, columns)] = blocks[step * SIDE + side][...]


def assemble(places, blocks):
    rows, columns = blocks[0].shape
    out_shape = jax.ShapeDtypeStruct((rows, columns * len(blocks)), jnp.bfloat16)
    return call(lambda *refs: assemble_kernel(places, *refs), out_shape, blocks)


def shards(
    hidden, norm_weight, query_weight, down_weights, up_weights, adapter_index, adapter_slot
):
    devices = lax.axis_size("adapter")
    me = lax.axis_index("adapter")
    places = devices // CORNERS
    own_rows, width = hidden.shape
    columns = query_weight.shape[1]
    rank = down_weights.shape[2]

    def move(x, steps, flip):
        return lax.ppermute(x, "adapter", pairs(places, steps, flip))

    def base_rows(rows, weight):
        return jnp.dot(rows, weight, preferred_element_type=jnp.float32)

    down = down_weights[0].T
    up = up_weights.reshape(devices * rank, columns)
    down_other = move(down, 0, 1)
    up_other = move(up, 0, 1)
    weight_other = move(query_weight, 0, 1)

    block, other = [normalize(hidden, norm_weight, adapter_index, adapter_slot)], []
    parts, slots, rows, bases, tokens = [], [], [], [], []
    last = places - 1

    def meet(blocks, before=()):
        part, slot, here = shrink_rows(blocks, down, down_other, before, tokens if before else ())
        parts.append(part)
        slots.append(slot)
        rows.append(here)

    for step in range(last):
        if step:
            block[step] = after(block[step], *bases[-1:])
            tokens.append(token(block[step]))
        block.append(move(after(block[step], *tokens[-1:]), 1, 0))
        other.append(move(after(block[step], *other[-1:]), 0, 2))
        if step:
            meet(after([block[step - 1], other[step - 1]], block[step]))
            bases.append(base_rows(rows[-1], query_weight))
    base, weight_other = base_and_weight(after(rows, bases[-1]), weight_other)
    block[last] = after(block[last], base)
    tokens.append(token(block[last]))
    source = after(block[last], other[-1], tokens[-1])
    source = jnp.where((me & 1) == 0, source, other[-1])
    crossed = lax.ppermute(source, "adapter", split_pairs(places))
    meet(after([block[last - 1], other[-1]], source))
    bases.append(base_rows(rows[-1], query_weight))
    bases_other = [base, base_rows(rows[-1], weight_other)]
    meet([block[last], after(crossed, bases[-1], bases_other[-1])], parts)

    part = parts[-1]
    moved = [part] + [move(part, steps, 0) for steps in range(1, places)]
    bases.append(base_rows(rows[-1], query_weight))
    moved = after(moved, bases[-1])
    shrink = call(
        lambda *refs: sum_kernel(places, *refs), jax.ShapeDtypeStruct(part.shape, part.dtype), moved
    )
    across = move(shrink, 0, 2)
    bases_other.append(base_rows(after(rows[-1], shrink), weight_other))
    query = list(finish(shrink, across, bases + bases_other, slots, up, up_other, own_rows))
    for step in sorted(range(places), key=lambda step: -min(step, places - step)):
        for side in (1, 0):
            if step or side:
                at = step * SIDE + side
                query[at] = move(query[at], -step, 2 * side)
    return assemble(places, query)


def solution(mesh):
    in_specs = (
        P(("group", "adapter"), None),
        P(),
        P(None, "adapter"),
        P("adapter", None, None),
        P(None, None, "adapter"),
        P(("group", "adapter"), None),
        P(),
    )
    out_specs = P(("group", "adapter"), None)
    return jax.shard_map(shards, mesh=mesh, in_specs=in_specs, out_specs=out_specs, check_vma=False)
```

```python
import jax
import jax.numpy as jnp
from jax import lax
from jax.experimental import pallas as pl
from jax.experimental.pallas import tpu as pltpu
from jax.sharding import PartitionSpec as P

ADAPTER_SCALE = 0.5
EPS = 1e-05

SIDE = 2
CORES = 2
CORNERS = SIDE * CORES
LANES = 128
CHUNK = 1024
VMEM_LIMIT = 24 << 20
VMEM = pl.BlockSpec(memory_space=pltpu.VMEM)


def line_ring(places):
    odd = list(range(1, places, 2))
    even = list(range(0, places, 2))
    return [0] + odd + even[:0:-1]


def pairs(places, steps, flip):
    ring = line_ring(places)
    out = []
    for at, place in enumerate(ring):
        target = ring[(at + steps) % places]
        for corner in range(CORNERS):
            out.append((place * CORNERS + corner, target * CORNERS + (corner ^ flip)))
    return out


def split_pairs(places):
    flips, steps = pairs(places, 0, 2), pairs(places, 1, 0)
    return [pair for pair in flips if pair[0] % CORES == 0] + [
        pair for pair in steps if pair[0] % CORES
    ]


def ring_chip(places, steps, side):
    chip = lax.axis_index("adapter") // CORES
    ring = line_ring(places)
    target = jnp.int32(0)
    for at, name in enumerate(ring):
        target = jnp.where(chip // SIDE == name, jnp.int32(ring[(at + steps) % places]), target)
    return target * SIDE + ((chip % SIDE) ^ side)


def after(x, *others):
    return lax.optimization_barrier((x, *others))[0]


def call(kernel, out_shape, operands):
    return pl.pallas_call(
        kernel,
        out_shape=out_shape,
        in_specs=[VMEM] * len(operands),
        out_specs=jax.tree.map(lambda _: VMEM, out_shape),
        compiler_params=pltpu.CompilerParams(vmem_limit_bytes=VMEM_LIMIT),
        cost_estimate=pl.CostEstimate(flops=1, bytes_accessed=1, transcendentals=0),
    )(*operands)


def norm_kernel(*refs):
    sources, (out_ref, *buffers, sems) = refs[:4], refs[4:]
    copies = [
        pltpu.make_async_copy(source, buffer, sems.at[number])
        for number, (source, buffer) in enumerate(zip(sources, buffers))
    ]
    for copy in copies:
        copy.start()
    for copy in copies:
        copy.wait()
    hidden_ref, gain_ref, index_ref, slot_ref = buffers
    rows, width = hidden_ref.shape
    squares = jnp.zeros((rows, LANES), jnp.float32)
    for start in range(0, width, CHUNK):
        wide = hidden_ref[:, start : start + CHUNK].astype(jnp.float32)
        wide = wide * wide
        for lane in range(0, CHUNK, LANES):
            squares = squares + wide[:, lane : lane + LANES]
    inv_rms = lax.rsqrt(jnp.sum(squares, axis=1, keepdims=True) / width + EPS)
    for start in range(0, width, CHUNK):
        lanes = slice(start, start + CHUNK)
        wide = hidden_ref[:, lanes].astype(jnp.float32)
        out_ref[:, lanes] = (wide * inv_rms * gain_ref[:, lanes]).astype(jnp.bfloat16)
    index = index_ref[...]
    slot = jnp.zeros(index.shape, jnp.float32)
    for name in range(slot_ref.shape[1]):
        slot = jnp.where(index == name, slot_ref[0, name].astype(jnp.float32), slot)
    across = lax.broadcasted_iota(jnp.int32, (rows, rows), 1)
    down = lax.broadcasted_iota(jnp.int32, (rows, rows), 0)
    column = jnp.sum(jnp.where(across == down, slot, 0.0), axis=1, keepdims=True)
    out_ref[:, width:] = jnp.broadcast_to(column, (rows, LANES)).astype(jnp.bfloat16)


def normalize(hidden, norm_weight, adapter_index, adapter_slot):
    rows, width = hidden.shape
    sources = (
        hidden,
        norm_weight.reshape(1, width),
        adapter_index.reshape(1, rows),
        adapter_slot.reshape(1, -1),
    )
    spaces = (pltpu.VMEM, pltpu.VMEM, pltpu.VMEM, pltpu.SMEM)
    return pl.pallas_call(
        norm_kernel,
        out_shape=jax.ShapeDtypeStruct((rows, width + LANES), jnp.bfloat16),
        in_specs=[pl.BlockSpec(memory_space=pltpu.HBM)] * len(sources),
        out_specs=VMEM,
        scratch_shapes=[space(x.shape, x.dtype) for space, x in zip(spaces, sources)]
        + [pltpu.SemaphoreType.DMA((len(sources),))],
    )(*sources)


def shrink_kernel(halves, *refs):
    blocks, (own_ref, other_ref, *before, part_ref, slot_ref, rows_ref) = refs[:SIDE], refs[SIDE:]
    rank, width = own_ref.shape
    rows = slot_ref.shape[0]
    part = jnp.zeros((rows, 2 * rank), jnp.float32)
    for start in range(0, width, CHUNK):
        lanes = slice(start, start + CHUNK)
        wide = [block[:, lanes].astype(jnp.float32) for block in blocks]
        chunk = jnp.concatenate(wide, axis=0).astype(jnp.bfloat16)
        rows_ref[:, lanes] = chunk
        down = jnp.concatenate([own_ref[:, lanes], other_ref[:, lanes]], axis=0)
        part += lax.dot_general(
            chunk, down, (((1,), (1,)), ((), ())), preferred_element_type=jnp.float32
        )
    slot = [block[:, width:].astype(jnp.float32) for block in blocks]
    slot = jnp.concatenate(slot, axis=0)[:, 0:1].astype(jnp.int32)
    slot_ref[...] = jnp.broadcast_to(slot, slot_ref.shape)
    me = lax.axis_index("adapter")
    lanes = lax.broadcasted_iota(jnp.int32, part.shape, 1)
    part = jnp.where(slot == jnp.where(lanes < rank, me, me ^ 1), part, 0.0)
    part = part[:, :rank] + part[:, rank:]
    if halves:
        steps = [ref[...].astype(jnp.float32) for ref in before] + [part]
        middle = len(steps) // 2
        halves = [jnp.concatenate(steps[:middle], axis=0), jnp.concatenate(steps[middle:], axis=0)]
        part = jnp.concatenate(halves, axis=1)
    part_ref[...] = part.astype(jnp.bfloat16)


def shrink_rows(blocks, own, other, before=(), tokens=()):
    rows = blocks[0].shape[0] * SIDE
    rank, width = own.shape
    packed = (rows * (len(before) + 1) // 2, 2 * rank) if before else (rows, rank)
    out_shape = (
        jax.ShapeDtypeStruct(packed, jnp.bfloat16),
        jax.ShapeDtypeStruct((rows, LANES), jnp.int32),
        jax.ShapeDtypeStruct((rows, width), jnp.bfloat16),
    )
    return call(
        lambda *refs: shrink_kernel(bool(before), *refs[len(tokens) :]),
        out_shape,
        (*tokens, *blocks, own, other, *before),
    )


def sum_kernel(places, *refs):
    *moved, out_ref = refs
    half, rank = moved[0].shape[0], moved[0].shape[1] // 2
    rows = half // (places // 2)
    for step in range(places):
        shrink = jnp.zeros((rows, rank), jnp.float32)
        for back in range(places):
            shrink += packed_step(moved[back], (step - back) % places, places)
        side, first = divmod(step, places // 2)
        out_ref[first * rows : (first + 1) * rows, side * rank : (side + 1) * rank] = shrink.astype(
            jnp.bfloat16
        )


def packed_step(ref, step, places):
    rank = ref.shape[1] // 2
    rows = ref.shape[0] // (places // 2)
    side, first = divmod(step, places // 2)
    return ref[first * rows : (first + 1) * rows, side * rank : (side + 1) * rank].astype(jnp.float32)


def base_kernel(*refs):
    *blocks, weight_ref, out_ref, kept_ref, sems = refs
    width = weight_ref.shape[0]
    copies = []
    for number, start in enumerate(range(0, width, CHUNK)):
        here = pl.ds(start, CHUNK)
        copies.append(
            pltpu.make_async_copy(weight_ref.at[here], kept_ref.at[here], sems.at[number])
        )
        copies[-1].start()
    out_ref[...] = jnp.zeros(out_ref.shape, jnp.float32)
    for number, start in enumerate(range(0, width, CHUNK)):
        lanes = slice(start, start + CHUNK)
        rows = jnp.concatenate([block[:, lanes] for block in blocks], axis=0)
        copies[number].wait()
        out_ref[...] += jnp.dot(rows, kept_ref[lanes, :], preferred_element_type=jnp.float32)


def base_and_weight(blocks, weight):
    rows = blocks[0].shape[0] * len(blocks)
    return pl.pallas_call(
        base_kernel,
        out_shape=(
            jax.ShapeDtypeStruct((rows, weight.shape[1]), jnp.float32),
            jax.ShapeDtypeStruct(weight.shape, weight.dtype),
        ),
        in_specs=[VMEM] * len(blocks) + [pl.BlockSpec(memory_space=pltpu.HBM)],
        out_specs=(VMEM, VMEM),
        scratch_shapes=[pltpu.SemaphoreType.DMA((weight.shape[0] // CHUNK,))],
        compiler_params=pltpu.CompilerParams(vmem_limit_bytes=VMEM_LIMIT),
        cost_estimate=pl.CostEstimate(flops=1, bytes_accessed=1, transcendentals=0),
    )(*blocks, weight)


def token_kernel(block_ref, out_ref):
    out_ref[...] = jnp.zeros(out_ref.shape, out_ref.dtype)


def token(block):
    return pl.pallas_call(
        token_kernel,
        out_shape=jax.ShapeDtypeStruct((8, LANES), jnp.float32),
        in_specs=[pl.BlockSpec(memory_space=pl.ANY)],
        out_specs=VMEM,
        compiler_params=pltpu.CompilerParams(vmem_limit_bytes=VMEM_LIMIT),
        cost_estimate=pl.CostEstimate(flops=1000000, bytes_accessed=1, transcendentals=0),
    )(block)


def finish_kernel(places, *refs):
    shrink_ref, across_ref, *refs = refs
    bases, slots = refs[: places + 3], refs[places + 3 : 2 * places + 3]
    own_ref, other_ref, out_ref = refs[2 * places + 3 :]
    depth, columns = own_ref.shape
    own_rows = out_ref.shape[1]
    rows = SIDE * own_rows
    core = lax.axis_index("adapter") % CORES
    shrinks = []
    for step in range(places):
        across = packed_step(across_ref, step, places)
        swapped = jnp.concatenate([across[own_rows:], across[:own_rows]], axis=0)
        shrinks.append(packed_step(shrink_ref, step, places) + swapped)
    shrink = jnp.concatenate(shrinks, axis=0)
    slot = jnp.concatenate([ref[:, 0:1] for ref in slots], axis=0)
    wide = jnp.concatenate([shrink] * (depth // shrink.shape[1]), axis=1)
    lanes = lax.broadcasted_iota(jnp.int32, wide.shape, 1)
    spread = jnp.where(lanes // shrink.shape[1] == slot, wide, 0.0).astype(jnp.bfloat16)
    for which, up_ref in enumerate((own_ref, other_ref)):
        update = jnp.dot(spread, up_ref[...], preferred_element_type=jnp.float32)
        at = pl.multiple_of((core ^ which) * columns, columns)
        for step in range(places):
            here = slice(step * rows, (step + 1) * rows)
            if which == 0:
                base = bases[step][...]
            elif step < places - 2:
                base = bases[places][here, :]
            else:
                base = bases[step + 3][...]
            query = (base + ADAPTER_SCALE * update[here]).astype(jnp.bfloat16)
            for side in range(SIDE):
                chip = ring_chip(places, -step, side)
                out_ref[chip, :, pl.ds(at, columns)] = query[side * own_rows : (side + 1) * own_rows]


def finish(shrink, across, bases, slots, own, other, own_rows):
    places = len(slots)
    return call(
        lambda *refs: finish_kernel(places, *refs),
        jax.ShapeDtypeStruct((places * SIDE, own_rows, CORES * own.shape[1]), jnp.bfloat16),
        (shrink, across, *bases, *slots, own, other),
    )


def shards(
    hidden, norm_weight, query_weight, down_weights, up_weights, adapter_index, adapter_slot
):
    devices = lax.axis_size("adapter")
    me = lax.axis_index("adapter")
    places = devices // CORNERS
    own_rows, width = hidden.shape
    columns = query_weight.shape[1]
    rank = down_weights.shape[2]

    def move(x, steps, flip):
        return lax.ppermute(x, "adapter", pairs(places, steps, flip))

    def base_rows(rows, weight):
        return jnp.dot(rows, weight, preferred_element_type=jnp.float32)

    down = down_weights[0].T
    up = up_weights.reshape(devices * rank, columns)
    down_other = move(down, 0, 1)
    up_other = move(up, 0, 1)
    weight_other = move(query_weight, 0, 1)

    block, other = [normalize(hidden, norm_weight, adapter_index, adapter_slot)], []
    parts, slots, rows, bases, tokens = [], [], [], [], []
    last = places - 1

    def meet(blocks, before=()):
        part, slot, here = shrink_rows(blocks, down, down_other, before, tokens if before else ())
        parts.append(part)
        slots.append(slot)
        rows.append(here)

    for step in range(last):
        if step:
            block[step] = after(block[step], *bases[-1:])
            tokens.append(token(block[step]))
        block.append(move(after(block[step], *tokens[-1:]), 1, 0))
        other.append(move(after(block[step], *other[-1:]), 0, 2))
        if step:
            meet(after([block[step - 1], other[step - 1]], block[step]))
            bases.append(base_rows(rows[-1], query_weight))
    block[last] = after(block[last], bases[-1])
    tokens.append(token(block[last]))
    source = after(block[last], other[-1], tokens[-1])
    source = jnp.where((me & 1) == 0, source, other[-1])
    crossed = lax.ppermute(source, "adapter", split_pairs(places))
    base, weight_other = base_and_weight(after(rows, source), weight_other)
    meet(after([block[last - 1], other[-1]], source))
    bases.append(base_rows(rows[-1], query_weight))
    bases_other = [base, base_rows(rows[-1], weight_other)]
    meet([block[last], after(crossed, bases[-1], bases_other[-1])], parts)

    part = parts[-1]
    moved = [part] + [move(part, steps, 0) for steps in range(1, places)]
    bases.append(base_rows(rows[-1], query_weight))
    moved = after(moved, bases[-1])
    shrink = call(
        lambda *refs: sum_kernel(places, *refs), jax.ShapeDtypeStruct(part.shape, part.dtype), moved
    )
    across = move(shrink, 0, 2)
    bases_other.append(base_rows(after(rows[-1], shrink), weight_other))
    query = finish(shrink, across, bases + bases_other, slots, up, up_other, own_rows)
    groups = [list(range(core, devices, CORES)) for core in range(CORES)]
    query = lax.all_to_all(query, "adapter", 0, 0, axis_index_groups=groups, tiled=True)
    return query.transpose(1, 0, 2).reshape(own_rows, devices * columns)


def solution(mesh):
    in_specs = (
        P(("group", "adapter"), None),
        P(),
        P(None, "adapter"),
        P("adapter", None, None),
        P(None, None, "adapter"),
        P(("group", "adapter"), None),
        P(),
    )
    out_specs = P(("group", "adapter"), None)
    return jax.shard_map(shards, mesh=mesh, in_specs=in_specs, out_specs=out_specs, check_vma=False)
```

```python
import jax
import jax.numpy as jnp
from jax import lax
from jax.experimental import pallas as pl
from jax.experimental.pallas import tpu as pltpu
from jax.sharding import PartitionSpec as P

ADAPTER_SCALE = 0.5
EPS = 1e-05

SIDE = 2
CORES = 2
CORNERS = SIDE * CORES
LANES = 128
CHUNK = 1024
VMEM_LIMIT = 16 << 20
VMEM = pl.BlockSpec(memory_space=pltpu.VMEM)


def line_ring(places):
    odd = list(range(1, places, 2))
    even = list(range(0, places, 2))
    return [0] + odd + even[:0:-1]


def pairs(places, steps, flip):
    ring = line_ring(places)
    out = []
    for at, place in enumerate(ring):
        target = ring[(at + steps) % places]
        for corner in range(CORNERS):
            out.append((place * CORNERS + corner, target * CORNERS + (corner ^ flip)))
    return out


def split_pairs(places):
    flips, steps = pairs(places, 0, 2), pairs(places, 1, 0)
    return [pair for pair in flips if pair[0] % CORES == 0] + [
        pair for pair in steps if pair[0] % CORES
    ]


def ring_chip(places, steps, side):
    chip = lax.axis_index("adapter") // CORES
    ring = line_ring(places)
    target = jnp.int32(0)
    for at, name in enumerate(ring):
        target = jnp.where(chip // SIDE == name, jnp.int32(ring[(at + steps) % places]), target)
    return target * SIDE + ((chip % SIDE) ^ side)


def after(x, *others):
    return lax.optimization_barrier((x, *others))[0]


def call(kernel, out_shape, operands):
    return pl.pallas_call(
        kernel,
        out_shape=out_shape,
        in_specs=[VMEM] * len(operands),
        out_specs=jax.tree.map(lambda _: VMEM, out_shape),
        compiler_params=pltpu.CompilerParams(vmem_limit_bytes=VMEM_LIMIT),
        cost_estimate=pl.CostEstimate(flops=1, bytes_accessed=1, transcendentals=0),
    )(*operands)


def norm_kernel(*refs):
    sources, (out_ref, *buffers, sems) = refs[:4], refs[4:]
    copies = [
        pltpu.make_async_copy(source, buffer, sems.at[number])
        for number, (source, buffer) in enumerate(zip(sources, buffers))
    ]
    for copy in copies:
        copy.start()
    for copy in copies:
        copy.wait()
    hidden_ref, gain_ref, index_ref, slot_ref = buffers
    rows, width = hidden_ref.shape
    squares = jnp.zeros((rows, LANES), jnp.float32)
    for start in range(0, width, CHUNK):
        wide = hidden_ref[:, start : start + CHUNK].astype(jnp.float32)
        wide = wide * wide
        for lane in range(0, CHUNK, LANES):
            squares = squares + wide[:, lane : lane + LANES]
    inv_rms = lax.rsqrt(jnp.sum(squares, axis=1, keepdims=True) / width + EPS)
    for start in range(0, width, CHUNK):
        lanes = slice(start, start + CHUNK)
        wide = hidden_ref[:, lanes].astype(jnp.float32)
        out_ref[:, lanes] = (wide * inv_rms * gain_ref[:, lanes]).astype(jnp.bfloat16)
    index = index_ref[...]
    slot = jnp.zeros(index.shape, jnp.float32)
    for name in range(slot_ref.shape[1]):
        slot = jnp.where(index == name, slot_ref[0, name].astype(jnp.float32), slot)
    across = lax.broadcasted_iota(jnp.int32, (rows, rows), 1)
    down = lax.broadcasted_iota(jnp.int32, (rows, rows), 0)
    column = jnp.sum(jnp.where(across == down, slot, 0.0), axis=1, keepdims=True)
    out_ref[:, width:] = jnp.broadcast_to(column, (rows, LANES)).astype(jnp.bfloat16)


def normalize(hidden, norm_weight, adapter_index, adapter_slot):
    rows, width = hidden.shape
    sources = (
        hidden,
        norm_weight.reshape(1, width),
        adapter_index.reshape(1, rows),
        adapter_slot.reshape(1, -1),
    )
    spaces = (pltpu.VMEM, pltpu.VMEM, pltpu.VMEM, pltpu.SMEM)
    return pl.pallas_call(
        norm_kernel,
        out_shape=jax.ShapeDtypeStruct((rows, width + LANES), jnp.bfloat16),
        in_specs=[pl.BlockSpec(memory_space=pltpu.HBM)] * len(sources),
        out_specs=VMEM,
        scratch_shapes=[space(x.shape, x.dtype) for space, x in zip(spaces, sources)]
        + [pltpu.SemaphoreType.DMA((len(sources),))],
    )(*sources)


def shrink_kernel(halves, *refs):
    blocks, (own_ref, other_ref, *before, part_ref, slot_ref, rows_ref) = refs[:SIDE], refs[SIDE:]
    rank, width = own_ref.shape
    rows = slot_ref.shape[0]
    part = jnp.zeros((rows, 2 * rank), jnp.float32)
    for start in range(0, width, CHUNK):
        lanes = slice(start, start + CHUNK)
        wide = [block[:, lanes].astype(jnp.float32) for block in blocks]
        chunk = jnp.concatenate(wide, axis=0).astype(jnp.bfloat16)
        rows_ref[:, lanes] = chunk
        down = jnp.concatenate([own_ref[:, lanes], other_ref[:, lanes]], axis=0)
        part += lax.dot_general(
            chunk, down, (((1,), (1,)), ((), ())), preferred_element_type=jnp.float32
        )
    slot = [block[:, width:].astype(jnp.float32) for block in blocks]
    slot = jnp.concatenate(slot, axis=0)[:, 0:1].astype(jnp.int32)
    slot_ref[...] = jnp.broadcast_to(slot, slot_ref.shape)
    me = lax.axis_index("adapter")
    lanes = lax.broadcasted_iota(jnp.int32, part.shape, 1)
    part = jnp.where(slot == jnp.where(lanes < rank, me, me ^ 1), part, 0.0)
    part = part[:, :rank] + part[:, rank:]
    if halves:
        steps = [ref[...].astype(jnp.float32) for ref in before] + [part]
        middle = len(steps) // 2
        halves = [jnp.concatenate(steps[:middle], axis=0), jnp.concatenate(steps[middle:], axis=0)]
        part = jnp.concatenate(halves, axis=1)
    part_ref[...] = part.astype(jnp.bfloat16)


def shrink_rows(blocks, own, other, before=(), tokens=()):
    rows = blocks[0].shape[0] * SIDE
    rank, width = own.shape
    packed = (rows * (len(before) + 1) // 2, 2 * rank) if before else (rows, rank)
    out_shape = (
        jax.ShapeDtypeStruct(packed, jnp.bfloat16),
        jax.ShapeDtypeStruct((rows, LANES), jnp.int32),
        jax.ShapeDtypeStruct((rows, width), jnp.bfloat16),
    )
    return call(
        lambda *refs: shrink_kernel(bool(before), *refs[len(tokens) :]),
        out_shape,
        (*tokens, *blocks, own, other, *before),
    )


def sum_kernel(places, *refs):
    *moved, out_ref = refs
    half, rank = moved[0].shape[0], moved[0].shape[1] // 2
    rows = half // (places // 2)
    for step in range(places):
        shrink = jnp.zeros((rows, rank), jnp.float32)
        for back in range(places):
            shrink += packed_step(moved[back], (step - back) % places, places)
        side, first = divmod(step, places // 2)
        out_ref[first * rows : (first + 1) * rows, side * rank : (side + 1) * rank] = shrink.astype(
            jnp.bfloat16
        )


def packed_step(ref, step, places):
    rank = ref.shape[1] // 2
    rows = ref.shape[0] // (places // 2)
    side, first = divmod(step, places // 2)
    return ref[first * rows : (first + 1) * rows, side * rank : (side + 1) * rank].astype(jnp.float32)


def base_kernel(*refs):
    *blocks, weight_ref, out_ref, kept_ref, sems = refs
    width = weight_ref.shape[0]
    copies = []
    for number, start in enumerate(range(0, width, CHUNK)):
        here = pl.ds(start, CHUNK)
        copies.append(
            pltpu.make_async_copy(weight_ref.at[here], kept_ref.at[here], sems.at[number])
        )
        copies[-1].start()
    out_ref[...] = jnp.zeros(out_ref.shape, jnp.float32)
    for number, start in enumerate(range(0, width, CHUNK)):
        lanes = slice(start, start + CHUNK)
        rows = jnp.concatenate([block[:, lanes] for block in blocks], axis=0)
        copies[number].wait()
        out_ref[...] += jnp.dot(rows, kept_ref[lanes, :], preferred_element_type=jnp.float32)


def base_and_weight(blocks, weight):
    rows = blocks[0].shape[0] * len(blocks)
    return pl.pallas_call(
        base_kernel,
        out_shape=(
            jax.ShapeDtypeStruct((rows, weight.shape[1]), jnp.float32),
            jax.ShapeDtypeStruct(weight.shape, weight.dtype),
        ),
        in_specs=[VMEM] * len(blocks) + [pl.BlockSpec(memory_space=pltpu.HBM)],
        out_specs=(VMEM, VMEM),
        scratch_shapes=[pltpu.SemaphoreType.DMA((weight.shape[0] // CHUNK,))],
        compiler_params=pltpu.CompilerParams(vmem_limit_bytes=VMEM_LIMIT),
        cost_estimate=pl.CostEstimate(flops=1, bytes_accessed=1, transcendentals=0),
    )(*blocks, weight)


def token_kernel(block_ref, out_ref):
    out_ref[...] = jnp.zeros(out_ref.shape, out_ref.dtype)


def token(block):
    return pl.pallas_call(
        token_kernel,
        out_shape=jax.ShapeDtypeStruct((8, LANES), jnp.float32),
        in_specs=[pl.BlockSpec(memory_space=pl.ANY)],
        out_specs=VMEM,
        compiler_params=pltpu.CompilerParams(vmem_limit_bytes=VMEM_LIMIT),
        cost_estimate=pl.CostEstimate(flops=1000000, bytes_accessed=1, transcendentals=0),
    )(block)


def finish_kernel(places, *refs):
    shrink_ref, across_ref, *refs = refs
    bases, slots = refs[: places + 3], refs[places + 3 : 2 * places + 3]
    own_ref, other_ref, out_ref = refs[2 * places + 3 :]
    depth, columns = own_ref.shape
    own_rows = out_ref.shape[1]
    rows = SIDE * own_rows
    core = lax.axis_index("adapter") % CORES
    shrinks = []
    for step in range(places):
        across = packed_step(across_ref, step, places)
        swapped = jnp.concatenate([across[own_rows:], across[:own_rows]], axis=0)
        shrinks.append(packed_step(shrink_ref, step, places) + swapped)
    shrink = jnp.concatenate(shrinks, axis=0)
    slot = jnp.concatenate([ref[:, 0:1] for ref in slots], axis=0)
    wide = jnp.concatenate([shrink] * (depth // shrink.shape[1]), axis=1)
    lanes = lax.broadcasted_iota(jnp.int32, wide.shape, 1)
    spread = jnp.where(lanes // shrink.shape[1] == slot, wide, 0.0).astype(jnp.bfloat16)
    for which, up_ref in enumerate((own_ref, other_ref)):
        update = jnp.dot(spread, up_ref[...], preferred_element_type=jnp.float32)
        at = pl.multiple_of((core ^ which) * columns, columns)
        for step in range(places):
            here = slice(step * rows, (step + 1) * rows)
            if which == 0:
                base = bases[step][...]
            elif step < places - 2:
                base = bases[places][here, :]
            else:
                base = bases[step + 3][...]
            query = (base + ADAPTER_SCALE * update[here]).astype(jnp.bfloat16)
            for side in range(SIDE):
                chip = ring_chip(places, -step, side)
                out_ref[chip, :, pl.ds(at, columns)] = query[side * own_rows : (side + 1) * own_rows]


def finish(shrink, across, bases, slots, own, other, own_rows):
    places = len(slots)
    return call(
        lambda *refs: finish_kernel(places, *refs),
        jax.ShapeDtypeStruct((places * SIDE, own_rows, CORES * own.shape[1]), jnp.bfloat16),
        (shrink, across, *bases, *slots, own, other),
    )


def shards(
    hidden, norm_weight, query_weight, down_weights, up_weights, adapter_index, adapter_slot
):
    devices = lax.axis_size("adapter")
    me = lax.axis_index("adapter")
    places = devices // CORNERS
    own_rows, width = hidden.shape
    columns = query_weight.shape[1]
    rank = down_weights.shape[2]

    def move(x, steps, flip):
        return lax.ppermute(x, "adapter", pairs(places, steps, flip))

    def base_rows(rows, weight):
        return jnp.dot(rows, weight, preferred_element_type=jnp.float32)

    down = down_weights[0].T
    up = up_weights.reshape(devices * rank, columns)
    down_other = move(down, 0, 1)
    up_other = move(up, 0, 1)
    weight_other = move(query_weight, 0, 1)

    block, other = [normalize(hidden, norm_weight, adapter_index, adapter_slot)], []
    parts, slots, rows, bases, tokens = [], [], [], [], []
    last = places - 1

    def meet(blocks, before=()):
        part, slot, here = shrink_rows(blocks, down, down_other, before, tokens if before else ())
        parts.append(part)
        slots.append(slot)
        rows.append(here)

    for step in range(last):
        if step:
            block[step] = after(block[step], *bases[-1:])
            tokens.append(token(block[step]))
        block.append(move(after(block[step], *tokens[-1:]), 1, 0))
        other.append(move(after(block[step], *other[-1:]), 0, 2))
        if step:
            meet(after([block[step - 1], other[step - 1]], block[step]))
            bases.append(base_rows(rows[-1], query_weight))
    base, weight_other = base_and_weight(after(rows, bases[-1]), weight_other)
    block[last] = after(block[last], base)
    tokens.append(token(block[last]))
    source = after(block[last], other[-1], tokens[-1])
    source = jnp.where((me & 1) == 0, source, other[-1])
    crossed = lax.ppermute(source, "adapter", split_pairs(places))
    meet(after([block[last - 1], other[-1]], source))
    bases.append(base_rows(rows[-1], query_weight))
    bases_other = [base, base_rows(rows[-1], weight_other)]
    meet([block[last], after(crossed, bases[-1], bases_other[-1])], parts)

    part = parts[-1]
    moved = [part] + [move(part, steps, 0) for steps in range(1, places)]
    bases.append(base_rows(rows[-1], query_weight))
    moved = after(moved, bases[-1])
    shrink = call(
        lambda *refs: sum_kernel(places, *refs), jax.ShapeDtypeStruct(part.shape, part.dtype), moved
    )
    across = move(shrink, 0, 2)
    bases_other.append(base_rows(after(rows[-1], shrink), weight_other))
    query = finish(shrink, across, bases + bases_other, slots, up, up_other, own_rows)
    groups = [list(range(core, devices, CORES)) for core in range(CORES)]
    query = lax.all_to_all(query, "adapter", 0, 0, axis_index_groups=groups, tiled=True)
    return query.transpose(1, 0, 2).reshape(own_rows, devices * columns)


def solution(mesh):
    in_specs = (
        P(("group", "adapter"), None),
        P(),
        P(None, "adapter"),
        P("adapter", None, None),
        P(None, None, "adapter"),
        P(("group", "adapter"), None),
        P(),
    )
    out_specs = P(("group", "adapter"), None)
    return jax.shard_map(shards, mesh=mesh, in_specs=in_specs, out_specs=out_specs, check_vma=False)
```
